256 devices in a mesh: gx: 4 (over x_lo, core), gy: 8 (over z), gz: 8 (over y, x_hi).
Axes of the slice: x: 4 (x_hi: 2, x_lo: 2; x = x_hi * 2 + x_lo), y: 4, z: 8, core: 2. Of those that a mesh axis runs over, the one named last changes fastest.
Arguments:
- charges: float32 [4, 8, 8, 1024], P('gx', 'gy', 'gz'), may hold values from -6 to 6
- cells: int32 [4, 8, 8, 3, 1024], P('gx', 'gy', 'gz'), may hold values from 0 to 391, as said below
- counts: int32 [4, 8, 8], P('gx', 'gy', 'gz'), may hold values from 128 to 1024, as said below
Outputs:
- potential: float32 [128, 256, 3072], P('gx', 'gy', 'gz')
- forces: float32 [4, 8, 8, 3, 1024], P('gx', 'gy', 'gz')
The draws below stay inside these ranges and needn't reach their ends.
Inputs may be any that keep to these rules, and one draw needn't show every extreme that they name: `cells`: component 0 lies below 40, component 1 below 40, component 2 below 392. Slots at or past a brick's count are unused. `counts`: some brick holds 1024 atoms.
All inputs are finite; a program needn't handle non-finite values.
Results may differ from the reference program's by a relative error of at most 0.0075.
Values sent between devices are 32-bit elements; how exact they have to be, the bound alone decides.
No kernel may reach another device: no remote copies, remote signals or barrier semaphores. Data moves between devices by JAX's collectives and lax.ppermute only.
A program may use at most 128 MiB of HBM per device.

```python
import jax
import jax.numpy as jnp
from jax import lax

BX = 32
BY = 32
BZ = 384
A_DEV = 1024
PAD = 4
REACH = 4
NX = 128
NY = 256
NZ = 3072
N_GX = 4
N_GY = 8
N_GZ = 8


def draw_cells(key, part):
    key = jax.random.fold_in(key, 11)
    first, second, third = jax.random.split(key, 3)
    limits = jnp.array([BX + 2 * PAD, BY + 2 * PAD, BZ + 2 * PAD], jnp.int32).reshape(1, 1, 1, 3, 1)
    cells = jax.random.randint(first, (N_GX, N_GY, N_GZ, 3, A_DEV), 0, limits, dtype=jnp.int32)
    bricks = N_GX * N_GY * N_GZ
    brick_ids = jnp.arange(bricks, dtype=jnp.int32).reshape(N_GX, N_GY, N_GZ, 1, 1)
    slot_ids = jnp.arange(A_DEV, dtype=jnp.int32).reshape(1, 1, 1, 1, A_DEV)
    upper = jax.random.randint(second, (), 0, bricks, dtype=jnp.int32)
    lower = jax.random.randint(third, (), 0, bricks, dtype=jnp.int32)
    cells = jnp.where((brick_ids == upper) & (slot_ids == 0), limits - 1, cells)
    cells = jnp.where((brick_ids == lower) & (slot_ids == 1), 0, cells)
    return cells.astype(jnp.int32)


def draw_counts(key, part):
    key = jax.random.fold_in(key, 23)
    first, second = jax.random.split(key)
    counts = jax.random.randint(first, (N_GX, N_GY, N_GZ), A_DEV // 8, A_DEV // 2 + 1, dtype=jnp.int32)
    bricks = N_GX * N_GY * N_GZ
    brick_ids = jnp.arange(bricks, dtype=jnp.int32).reshape(N_GX, N_GY, N_GZ)
    fullest = jax.random.randint(second, (), 0, bricks, dtype=jnp.int32)
    return jnp.where(brick_ids == fullest, A_DEV, counts).astype(jnp.int32)


def levels(stream_key, shape, cuts, smallest, top_value):
    gain = 1.0
    for axis_at, blocks in cuts:
        draws = jax.random.uniform(jax.random.fold_in(jax.random.fold_in(stream_key, 6), axis_at), (blocks,), jnp.float32, smallest / len(cuts), top_value / len(cuts))
        gain = gain * jnp.repeat(jnp.exp(draws), shape[axis_at] // blocks).reshape((-1,) + (1,) * (len(shape) - 1 - axis_at))
    return gain


def centred(own_key, dims, deviation, reach, cuts=(), kind=jnp.bfloat16):
    gain = levels(own_key, dims, cuts, -0.22, 0.18) if cuts else 1.0
    result = jax.random.normal(own_key, dims, jnp.float32) * deviation * gain
    return jnp.minimum(jnp.maximum(result, -reach), reach).astype(kind)


def setup_inputs(seed: int = 0) -> dict:
    keys = jax.random.split(jax.random.key(seed), 4)
    charges = centred(keys[0], (N_GX, N_GY, N_GZ, A_DEV), 1.0, 6.0, ((0, 4), (1, 8), (2, 8)), jnp.float32)
    cells = draw_cells(jax.random.fold_in(keys[3], 71), 0)
    counts = draw_counts(jax.random.fold_in(keys[3], 71), 0)
    return {"charges": charges, "cells": cells, "counts": counts}


kernel_width = 2.0


def kernel_taps():
    offsets = jnp.arange(-REACH, REACH + 1).astype(jnp.float32)
    return jnp.exp(-offsets * offsets / (2.0 * kernel_width * kernel_width))


def smooth_along(field, axis, weights):
    total = jnp.zeros_like(field)
    for offset in range(-REACH, REACH + 1):
        total = total + weights[offset + REACH] * jnp.roll(field, -offset, axis)
    return total


def reference(charges, cells, counts):
    slots = jnp.arange(A_DEV).astype(jnp.int32)
    live = slots[None, None, None, :] < counts[..., None]
    rounded = lax.optimization_barrier(charges.astype(jnp.bfloat16)).astype(jnp.float32)
    masses = jnp.where(live, rounded, jnp.float32(0.0))
    anchor_x = (jnp.arange(N_GX).astype(jnp.int32) * BX)[:, None, None, None]
    anchor_y = (jnp.arange(N_GY).astype(jnp.int32) * BY)[None, :, None, None]
    anchor_z = (jnp.arange(N_GZ).astype(jnp.int32) * BZ)[None, None, :, None]
    cell_x = (anchor_x + cells[:, :, :, 0, :] - PAD) % NX
    cell_y = (anchor_y + cells[:, :, :, 1, :] - PAD) % NY
    cell_z = (anchor_z + cells[:, :, :, 2, :] - PAD) % NZ
    flat = ((cell_x * NY + cell_y) * NZ + cell_z).astype(jnp.int32)
    density = jnp.zeros((NX * NY * NZ,), jnp.float32).at[flat.ravel()].add(masses.ravel())
    density = density.reshape(NX, NY, NZ)
    weights = kernel_taps()
    potential = smooth_along(density, 0, weights)
    potential = smooth_along(potential, 1, weights)
    potential = smooth_along(potential, 2, weights)
    parts = []
    for axis in range(3):
        field = -0.5 * (jnp.roll(potential, -1, axis) - jnp.roll(potential, 1, axis))
        parts.append(field.ravel()[flat])
    forces = jnp.stack(parts, axis=3) * charges[:, :, :, None, :]
    forces = jnp.where(live[:, :, :, None, :], forces, jnp.float32(0.0))
    return potential, forces
```

```python
import functools
import math

import jax
import jax.numpy as jnp
from jax import lax
from jax.experimental import pallas as pl
from jax.experimental.pallas import tpu as pltpu
from jax.sharding import PartitionSpec as P

BX = 32
BY = 32
BZ = 384
A_DEV = 1024
PAD = 4
REACH = 4
WIDTH = A_DEV + 128
BLOCK = 256

X0 = 5
Y0 = 8
PX = 42
PY = 48
PZ = 512
CHUNK = 7
FX = 40
FY = 40
FCHUNK = 4

kernel_width = 2.0
EXPONENT = -math.log2(math.e) / (2.0 * kernel_width * kernel_width)
SCALE = 1.3903614627339054
FAR = 1.0e4


def weight(distance, scale=1.0):
    square = distance * distance
    value = jnp.exp2(square * EXPONENT + math.log2(scale))
    return jnp.where(square < (REACH + 0.5) ** 2, value, 0.0)


def iota(shape, dim):
    return lax.broadcasted_iota(jnp.int32, shape, dim).astype(jnp.float32)


def brick_count(ref, brick):
    return jnp.max(ref[brick, 0:1, A_DEV:WIDTH]).astype(jnp.int32)


def contribute(ref, brick, dx, dy, dz, grid, rows_x):
    y0, ny = {0: (0, PY), -1: (0, 16), 1: (32, 16)}[dy]
    x0, nx = {0: (0, PX), -1: (0, 14), 1: (28, 14)}[dx]
    nz = PZ if dz == 0 else 256
    count = brick_count(ref, brick)

    def block(k, _):
        cols = pl.ds(pl.multiple_of(k * BLOCK, BLOCK), BLOCK)
        charge = ref[brick, 0:1, cols].astype(jnp.bfloat16).astype(jnp.float32)
        xa = ref[brick, 1:2, cols] + float(X0 - PAD + BX * dx)
        ya = ref[brick, 2:3, cols] + float(Y0 - PAD + BY * dy)
        za = ref[brick, 3:4, cols] + float(BZ * dz - PAD)
        gy = weight(iota((ny, BLOCK), 0) + float(y0) - ya) * (charge * (1.0 / SCALE))
        zi = iota((nz, BLOCK), 0)
        if dz == 0:
            zi = jnp.where(zi < 448.0, zi, zi - float(PZ))
        elif dz < 0:
            zi = jnp.where(zi < 64.0, FAR, zi - 128.0)
        else:
            zi = jnp.where(zi < 192.0, zi + 256.0, FAR)
        right = weight(zi - za, SCALE).astype(jnp.bfloat16)
        rows_x[...] = weight(iota((48, BLOCK), 0) - xa)

        def planes(c):
            left = jnp.stack(
                [rows_x[pl.ds(x0 + c * CHUNK + i, 1), :] * gy for i in range(CHUNK)], axis=0
            )
            left = left.reshape(CHUNK * ny, BLOCK).astype(jnp.bfloat16)
            part = lax.dot_general(
                left, right, (((1,), (1,)), ((), ())), preferred_element_type=jnp.float32
            )
            part = part.reshape(CHUNK, ny, nz)
            xs = pl.ds(x0 + c * CHUNK, CHUNK)
            ys = pl.ds(y0, ny)
            if dz == 0:
                grid[xs, ys, :] += part
            elif dz < 0:
                grid[xs, ys, 384:512] += part[:, :, 0:128]
                grid[xs, ys, 0:128] += part[:, :, 128:256]
            else:
                grid[xs, ys, 256:512] += part

        if dx == 0:
            def step(c, _):
                planes(c)
                return 0
            lax.fori_loop(0, PX // CHUNK, step, 0)
        else:
            for c in range(nx // CHUNK):
                planes(c)
        return 0

    lax.fori_loop(0, (count + BLOCK - 1) // BLOCK, block, 0)


def kernel(centre, low, high, charges, potential, forces, grid, rows_x, fields, out_sem):
    grid[...] = jnp.zeros_like(grid)
    for dx, ref in ((0, centre), (-1, low), (1, high)):
        for dy in (-1, 0, 1):
            for dz in (-1, 0, 1):
                contribute(ref, (dy + 1) * 3 + dz + 1, dx, dy, dz, grid, rows_x)
    copy = pltpu.make_async_copy(
        grid.at[X0 : X0 + BX, Y0 : Y0 + BY, 0:BZ], potential, out_sem
    )
    copy.start()

    def build(c, _):
        gx, gy, gz = [], [], []
        for i in range(FCHUNK):
            x = c * FCHUNK + i
            gx.append(grid[x + 2, 4:44, :] - grid[x, 4:44, :])
            gy.append(grid[x + 1, 5:45, :] - grid[x + 1, 3:43, :])
            mid = grid[x + 1, 4:44, :]
            gz.append(pltpu.roll(mid, PZ - 1, 1) - pltpu.roll(mid, 1, 1))
        rows = FCHUNK * FY
        for d, parts in enumerate((gx, gy, gz)):
            both = jnp.stack(parts, axis=0).reshape(rows, PZ).astype(jnp.bfloat16)
            fields[d, pl.ds(pl.multiple_of(c * rows, rows), rows), :] = both
        return 0

    lax.fori_loop(0, FX // FCHUNK, build, 0)
    forces[...] = jnp.zeros_like(forces)
    count = brick_count(centre, 4)

    def sample(k, _):
        cols = pl.ds(pl.multiple_of(k * BLOCK, BLOCK), BLOCK)
        xa = centre[4, 1:2, cols]
        ya = centre[4, 2:3, cols]
        za = centre[4, 3:4, cols] - float(PAD)
        zi = iota((PZ, BLOCK), 0)
        zi = jnp.where(zi < 448.0, zi, zi - float(PZ))
        depth = jnp.where(zi == za, 1.0, 0.0).astype(jnp.bfloat16)
        hot_y = iota((FY, BLOCK), 0) == ya

        def step(c, sums):
            rows = FCHUNK * FY
            sums = list(sums)
            for d in range(3):
                part = jnp.dot(
                    fields[d, pl.ds(pl.multiple_of(c * rows, rows), rows), :],
                    depth,
                    preferred_element_type=jnp.float32,
                ).reshape(FCHUNK, FY, BLOCK)
                for i in range(FCHUNK):
                    hot_x = xa == (c * FCHUNK + i).astype(jnp.float32)
                    sums[d] = sums[d] + jnp.where(hot_x, part[i], 0.0)
            return tuple(sums)

        zero = jnp.zeros((FY, BLOCK), jnp.float32)
        sums = lax.fori_loop(0, FX // FCHUNK, step, (zero, zero, zero))
        slots = lax.broadcasted_iota(jnp.int32, (1, BLOCK), 1) + k * BLOCK
        factor = jnp.where(slots < count, -0.5 * charges[0:1, cols], 0.0)
        for d in range(3):
            value = jnp.sum(jnp.where(hot_y, sums[d], 0.0), axis=0, keepdims=True)
            forces[d : d + 1, cols] = value * factor
        return 0

    lax.fori_loop(0, (count + BLOCK - 1) // BLOCK, sample, 0)
    copy.wait()


def neighbours(block, axis):
    size = lax.axis_size(axis)
    up = [(i, (i + 1) % size) for i in range(size)]
    down = [(target, source) for source, target in up]
    return lax.ppermute(block, axis, up), lax.ppermute(block, axis, down)


def local(charges, cells, counts):
    count = counts.reshape(())
    charge = charges.reshape(1, A_DEV)
    live = lax.broadcasted_iota(jnp.int32, (1, A_DEV), 1) < count
    atoms = jnp.concatenate([charge, cells.reshape(3, A_DEV).astype(jnp.float32)], axis=0)
    atoms = jnp.where(live, atoms, 0.0)
    tail = jnp.full((4, WIDTH - A_DEV), count.astype(jnp.float32))
    atoms = jnp.concatenate([atoms, tail], axis=1)[None]
    for axis in ("gz", "gy"):
        low, high = neighbours(atoms, axis)
        atoms = jnp.concatenate([low, atoms, high], axis=0)
    low, high = neighbours(atoms, "gx")
    potential, forces = pl.pallas_call(
        kernel,
        out_shape=(
            jax.ShapeDtypeStruct((BX, BY, BZ), jnp.float32),
            jax.ShapeDtypeStruct((3, A_DEV), jnp.float32),
        ),
        in_specs=[pl.BlockSpec(memory_space=pltpu.VMEM)] * 4,
        out_specs=(pl.BlockSpec(memory_space=pl.ANY), pl.BlockSpec(memory_space=pltpu.VMEM)),
        scratch_shapes=[
            pltpu.VMEM((PX, PY, PZ), jnp.float32),
            pltpu.VMEM((48, BLOCK), jnp.float32),
            pltpu.VMEM((3, FX * FY, PZ), jnp.bfloat16),
            pltpu.SemaphoreType.DMA,
        ],
        compiler_params=pltpu.CompilerParams(vmem_limit_bytes=40 * 1024 * 1024),
    )(atoms, low, high, charge)
    return potential, forces.reshape(1, 1, 1, 3, A_DEV)


def solution(mesh):
    in_specs = (P("gx", "gy", "gz", None), P("gx", "gy", "gz", None, None), P("gx", "gy", "gz"))
    out_specs = (P("gx", "gy", "gz"), P("gx", "gy", "gz", None, None))
    return jax.shard_map(local, mesh=mesh, in_specs=in_specs, out_specs=out_specs, check_vma=False)
```

```python
import functools
import math

import jax
import jax.numpy as jnp
from jax import lax
from jax.experimental import pallas as pl
from jax.experimental.pallas import tpu as pltpu
from jax.sharding import PartitionSpec as P

BX = 32
BY = 32
BZ = 384
A_DEV = 1024
PAD = 4
REACH = 4
WIDTH = A_DEV + 128
BLOCK = 256

X0 = 5
Y0 = 8
PX = 42
PY = 48
PZ = 512
CHUNK = 7
FX = 40
FY = 40
FCHUNK = 4

kernel_width = 2.0
EXPONENT = -math.log2(math.e) / (2.0 * kernel_width * kernel_width)
SCALE = 1.3903614627339054
UNIT = math.sqrt(-EXPONENT)
LOW_END = 2 * PAD + 5
HIGH_START = BZ + PAD - 9
SPAN = A_DEV + 384
MERGED = 9 * A_DEV + SPAN


def weight(first, second, scale=1.0):
    away = first - second
    square = away * away
    value = jnp.exp2(math.log2(scale) - square)
    return jnp.where(square < (REACH + 0.5) ** 2 * UNIT * UNIT, value, 0.0)


def iota(shape, dim):
    return lax.broadcasted_iota(jnp.int32, shape, dim).astype(jnp.float32)


def compact(numbers, charges, cells, own, below, above):
    count = numbers[0]
    slots = lax.broadcasted_iota(jnp.int32, (1, A_DEV), 1)
    live = slots < count
    charge = jnp.where(live, charges[...], 0.0).astype(jnp.bfloat16).astype(jnp.float32)
    places = jnp.where(live, cells[...], 0)
    own[0:1, 0:A_DEV] = charge
    own[1:4, 0:A_DEV] = places.astype(jnp.float32)
    own[:, A_DEV:WIDTH] = jnp.full((4, WIDTH - A_DEV), count.astype(jnp.float32))
    depth = places[2:3]
    near = jnp.concatenate(
        [
            jnp.where(live & (depth < LOW_END), 1.0, 0.0),
            jnp.where(live & (depth >= HIGH_START), 1.0, 0.0),
        ],
        axis=0,
    )
    near = jnp.concatenate([near, jnp.zeros((6, A_DEV), jnp.float32)], axis=0)
    before = near
    lanes = lax.broadcasted_iota(jnp.int32, (8, A_DEV), 1)
    shift = 1
    while shift < A_DEV:
        before = before + jnp.where(lanes >= shift, pltpu.roll(before, shift, 1), 0.0)
        shift *= 2
    totals = before[:, A_DEV - 1 : A_DEV]
    spot = jnp.where(near > 0.5, before - 1.0, -1.0)
    steps = (jnp.max(totals).astype(jnp.int32) + BLOCK - 1) // BLOCK
    for side, (out, base) in enumerate(((below, 0), (above, BZ // 2))):
        out[:, 0:A_DEV] = jnp.zeros((4, A_DEV), jnp.float32)
        out[:, A_DEV:WIDTH] = jnp.broadcast_to(totals[side : side + 1], (4, WIDTH - A_DEV))

    def window(k, _):
        for side, (out, base) in enumerate(((below, 0), (above, BZ // 2))):
            rows = jnp.concatenate(
                [
                    charge,
                    places[0:2].astype(jnp.float32),
                    (places[2:3] - base).astype(jnp.float32),
                    jnp.zeros((4, A_DEV), jnp.float32),
                ],
                axis=0,
            ).astype(jnp.bfloat16)
            want = iota((BLOCK, A_DEV), 0) + (k * BLOCK).astype(jnp.float32)
            pick = jnp.where(want == spot[side : side + 1], 1.0, 0.0).astype(jnp.bfloat16)
            moved = lax.dot_general(
                rows, pick, (((1,), (1,)), ((), ())), preferred_element_type=jnp.float32
            )
            cols = pl.ds(pl.multiple_of(k * BLOCK, BLOCK), BLOCK)
            out[0:3, cols] = moved[0:3]
            out[3:4, cols] = moved[3:4] + float(base)
        return 0

    lax.fori_loop(0, steps, window, 0)


def append(ref, brick, number, offset, dx, dy, dz, merged):
    lanes = lax.broadcasted_iota(jnp.int32, (1, A_DEV), 1)
    live = lanes < number
    moved = (float(X0 - PAD + BX * dx), float(Y0 - PAD + BY * dy), float(BZ * dz - PAD))
    rows = [ref[brick, 0:1, 0:A_DEV]]
    for i in range(3):
        rows.append(jnp.where(live, (ref[brick, 1 + i : 2 + i, 0:A_DEV] + moved[i]) * UNIT, 0.0))
    atoms = jnp.concatenate(rows + [jnp.zeros((4, A_DEV), jnp.float32)], axis=0)
    atoms = jnp.concatenate([atoms, jnp.zeros((8, SPAN - A_DEV), jnp.float32)], axis=1)
    atoms = pltpu.roll(atoms, offset % 128, 1)
    start = pl.multiple_of(offset // 128 * 128, 128)
    merged[:, pl.ds(start, 128)] += atoms[:, 0:128]
    merged[:, pl.ds(start + 128, SPAN - 128)] = atoms[:, 128:SPAN]
    return offset + number


def spread(merged, k, x0, nx, y0, ny, grid, rows_x, first):
    cols = pl.ds(pl.multiple_of(k * BLOCK, BLOCK), BLOCK)
    charge = merged[0:1, cols]
    xa = merged[1:2, cols]
    ya = merged[2:3, cols]
    za = merged[3:4, cols]
    gy = weight((iota((ny, BLOCK), 0) + float(y0)) * UNIT, ya) * (charge * (1.0 / SCALE))
    zi = iota((PZ, BLOCK), 0)
    zi = jnp.where(zi < 448.0, zi, zi - float(PZ)) * UNIT
    right = weight(zi, za, SCALE).astype(jnp.bfloat16)
    rows_x[...] = weight(iota((48, BLOCK), 0) * UNIT, xa)
    for c in range(nx // CHUNK):
        left = jnp.stack(
            [rows_x[x0 + c * CHUNK + i : x0 + c * CHUNK + i + 1, :] * gy for i in range(CHUNK)],
            axis=0,
        )
        left = left.reshape(CHUNK * ny, BLOCK).astype(jnp.bfloat16)
        part = lax.dot_general(
            left, right, (((1,), (1,)), ((), ())), preferred_element_type=jnp.float32
        )
        part = part.reshape(CHUNK, ny, PZ)
        start = x0 + c * CHUNK
        if first:
            grid[start : start + CHUNK, y0 : y0 + ny, :] = part
        else:
            grid[start : start + CHUNK, y0 : y0 + ny, :] += part


def kernel(centre, low, high, charges, potential, forces, grid, rows_x, fields, merged, numbers, sems):
    refs = (low, centre, high)
    copies = [
        pltpu.make_async_copy(ref.at[:, 0:1, A_DEV:WIDTH], numbers.at[i], sems.at[i])
        for i, ref in enumerate(refs)
    ]
    for copy in copies:
        copy.start()
    for copy in copies:
        copy.wait()

    def number(dx, brick):
        return numbers[dx + 1, brick, 0, 0].astype(jnp.int32)

    def gather(pairs):
        merged[:, 0:128] = jnp.zeros((8, 128), jnp.float32)
        offset = jnp.int32(0)
        for dx, dy in pairs:
            for dz in (0, -1, 1):
                brick = (dy + 1) * 3 + dz + 1
                offset = append(
                    refs[dx + 1], brick, number(dx, brick), offset, dx, dy, dz, merged
                )
        return offset

    groups = (
        (((0, 0),), 0, PX, 0, PY),
        (((-1, 0),), 0, 14, 0, PY),
        (((1, 0),), 28, 14, 0, PY),
        (((-1, -1), (0, -1), (1, -1)), 0, PX, 0, 16),
        (((-1, 1), (0, 1), (1, 1)), 0, PX, 32, 16),
    )
    for index, (pairs, x0, nx, y0, ny) in enumerate(groups):
        total = gather(pairs)
        begin = 0
        if index == 0:
            spread(merged, jnp.int32(0), x0, nx, y0, ny, grid, rows_x, True)
            begin = 1

        def block(k, _):
            spread(merged, k, x0, nx, y0, ny, grid, rows_x, False)
            return 0

        lax.fori_loop(begin, (total + BLOCK - 1) // BLOCK, block, 0)
    copy = pltpu.make_async_copy(
        grid.at[X0 : X0 + BX, Y0 : Y0 + BY, 0:BZ], potential, sems.at[0]
    )
    copy.start()

    rows = FCHUNK * FY

    def build(c, _):
        gx, gy, gz = [], [], []
        for i in range(FCHUNK):
            x = c * FCHUNK + i
            gx.append(grid[x + 2, 4:44, :] - grid[x, 4:44, :])
            gy.append(grid[x + 1, 5:45, :] - grid[x + 1, 3:43, :])
            mid = grid[x + 1, 4:44, :]
            gz.append(pltpu.roll(mid, PZ - 1, 1) - pltpu.roll(mid, 1, 1))
        for d, parts in enumerate((gx, gy, gz)):
            both = jnp.stack(parts, axis=0).reshape(rows, PZ).astype(jnp.bfloat16)
            fields[d, pl.ds(pl.multiple_of(c * rows, rows), rows), :] = both
        return 0

    lax.fori_loop(0, FX // FCHUNK, build, 0)
    forces[...] = jnp.zeros_like(forces)
    count = number(0, 4)

    def sample(k, _):
        cols = pl.ds(pl.multiple_of(k * BLOCK, BLOCK), BLOCK)
        xa = centre[4, 1:2, cols]
        ya = centre[4, 2:3, cols]
        za = centre[4, 3:4, cols] - float(PAD)
        zi = iota((PZ, BLOCK), 0)
        zi = jnp.where(zi < 448.0, zi, zi - float(PZ))
        depth = jnp.where(zi == za, 1.0, 0.0).astype(jnp.bfloat16)
        hot_y = iota((FY, BLOCK), 0) == ya
        slots = lax.broadcasted_iota(jnp.int32, (1, BLOCK), 1) + k * BLOCK
        factor = jnp.where(slots < count, -0.5 * charges[0:1, cols], 0.0)
        for d in range(3):
            total = jnp.zeros((FY, BLOCK), jnp.float32)
            for c in range(FX // FCHUNK):
                part = jnp.dot(
                    fields[d, c * rows : (c + 1) * rows, :],
                    depth,
                    preferred_element_type=jnp.float32,
                ).reshape(FCHUNK, FY, BLOCK)
                for i in range(FCHUNK):
                    total = total + jnp.where(xa == float(c * FCHUNK + i), part[i], 0.0)
            value = jnp.sum(jnp.where(hot_y, total, 0.0), axis=0, keepdims=True)
            forces[d : d + 1, cols] = value * factor
        return 0

    lax.fori_loop(0, (count + BLOCK - 1) // BLOCK, sample, 0)
    copy.wait()


def rings(axis):
    size = lax.axis_size(axis)
    up = [(i, (i + 1) % size) for i in range(size)]
    return up, [(target, source) for source, target in up]


def compute(atoms, low, high, charge):
    return pl.pallas_call(
        kernel,
        out_shape=(
            jax.ShapeDtypeStruct((BX, BY, BZ), jnp.float32),
            jax.ShapeDtypeStruct((3, A_DEV), jnp.float32),
        ),
        in_specs=[pl.BlockSpec(memory_space=pltpu.VMEM)] * 4,
        out_specs=(pl.BlockSpec(memory_space=pl.ANY), pl.BlockSpec(memory_space=pltpu.VMEM)),
        scratch_shapes=[
            pltpu.VMEM((PX, PY, PZ), jnp.float32),
            pltpu.VMEM((48, BLOCK), jnp.float32),
            pltpu.VMEM((3, FX * FY, PZ), jnp.bfloat16),
            pltpu.VMEM((8, MERGED), jnp.float32),
            pltpu.SMEM((3, 9, 1, WIDTH - A_DEV), jnp.float32),
            pltpu.SemaphoreType.DMA((3,)),
        ],
        compiler_params=pltpu.CompilerParams(vmem_limit_bytes=40 * 1024 * 1024),
    )(atoms, low, high, charge)


def local(charges, cells, counts):
    charge = charges.reshape(1, A_DEV)
    shape = jax.ShapeDtypeStruct((4, WIDTH), jnp.float32)
    own, below, above = pl.pallas_call(
        compact,
        out_shape=(shape, shape, shape),
        in_specs=[pl.BlockSpec(memory_space=pltpu.SMEM)]
        + [pl.BlockSpec(memory_space=pltpu.VMEM)] * 2,
        out_specs=(pl.BlockSpec(memory_space=pltpu.VMEM),) * 3,
    )(counts.reshape(1), charge, cells.reshape(3, A_DEV))
    up, down = rings("gz")
    low = lax.ppermute(above[None], "gz", up)
    high = lax.ppermute(below[None], "gz", down)
    atoms = jnp.concatenate([low, own[None], high], axis=0)
    up, down = rings("gy")
    low, high = lax.ppermute(atoms, "gy", up), lax.ppermute(atoms, "gy", down)
    atoms = jnp.concatenate([low, atoms, high], axis=0)
    up, down = rings("gx")
    low, high = lax.ppermute(atoms, "gx", up), lax.ppermute(atoms, "gx", down)
    potential, forces = compute(atoms, low, high, charge)
    return potential, forces.reshape(1, 1, 1, 3, A_DEV)


def solution(mesh):
    in_specs = (P("gx", "gy", "gz", None), P("gx", "gy", "gz", None, None), P("gx", "gy", "gz"))
    out_specs = (P("gx", "gy", "gz"), P("gx", "gy", "gz", None, None))
    return jax.shard_map(local, mesh=mesh, in_specs=in_specs, out_specs=out_specs, check_vma=False)
```

```python
import functools
import math

import jax
import jax.numpy as jnp
from jax import lax
from jax.experimental import pallas as pl
from jax.experimental.pallas import tpu as pltpu
from jax.sharding import PartitionSpec as P

BX = 32
BY = 32
BZ = 384
A_DEV = 1024
PAD = 4
REACH = 4
WIDTH = A_DEV + 128
BLOCK = 256
WIDE = 2 * BLOCK

X0 = 5
Y0 = 8
PX = 42
PY = 48
PZ = 512
CHUNK = 7
FX = 40
FY = 40
FCHUNK = 4

kernel_width = 2.0
EXPONENT = -math.log2(math.e) / (2.0 * kernel_width * kernel_width)
SCALE = 1.3903614627339054
UNIT = math.sqrt(-EXPONENT)
LOW_END = 2 * PAD + 5
HIGH_START = BZ + PAD - 9
SPAN = A_DEV + 128 + WIDE
MERGED = 9 * A_DEV + SPAN
ROWS = FCHUNK * FY


def weight(first, second, scale=1.0):
    away = first - second
    square = away * away
    value = jnp.exp2(math.log2(scale) - square)
    return jnp.where(square < (REACH + 0.5) ** 2 * UNIT * UNIT, value, 0.0)


def iota(shape, dim):
    return lax.broadcasted_iota(jnp.int32, shape, dim).astype(jnp.float32)


def toward(axis):
    return 1 - 2 * (lax.axis_index(axis) % 2)


def compact(numbers, charges, cells, own, first, second, lists):
    count = numbers[0]
    slots = lax.broadcasted_iota(jnp.int32, (1, A_DEV), 1)
    live = slots < count
    charge = jnp.where(live, charges[...], 0.0).astype(jnp.bfloat16).astype(jnp.float32)
    places = jnp.concatenate([jnp.where(live, cells[i], 0) for i in range(3)], axis=0)
    own[0:1, 0:A_DEV] = charge
    own[1:4, 0:A_DEV] = places.astype(jnp.float32)
    own[:, A_DEV:WIDTH] = jnp.full((4, WIDTH - A_DEV), count.astype(jnp.float32))
    depth = places[2:3]
    before = jnp.concatenate(
        [
            jnp.where(live & (depth < LOW_END), 1.0, 0.0),
            jnp.where(live & (depth >= HIGH_START), 1.0, 0.0),
            jnp.zeros((6, A_DEV), jnp.float32),
        ],
        axis=0,
    )
    near = before
    lanes = lax.broadcasted_iota(jnp.int32, (8, A_DEV), 1)
    shift = 1
    while shift < A_DEV:
        before = before + jnp.where(lanes >= shift, pltpu.roll(before, shift, 1), 0.0)
        shift *= 2
    totals = before[:, A_DEV - 1 : A_DEV]
    spot = jnp.where(near > 0.5, before - 1.0, -1.0)
    steps = (jnp.max(totals).astype(jnp.int32) + BLOCK - 1) // BLOCK
    for side in range(2):
        lists[side, :, 0:A_DEV] = jnp.zeros((4, A_DEV), jnp.float32)
        lists[side, :, A_DEV:WIDTH] = jnp.broadcast_to(
            totals[side : side + 1], (4, WIDTH - A_DEV)
        )

    def window(k, _):
        for side, base in enumerate((0, BZ // 2)):
            rows = jnp.concatenate(
                [
                    charge,
                    places[0:2].astype(jnp.float32),
                    (places[2:3] - base).astype(jnp.float32),
                    jnp.zeros((4, A_DEV), jnp.float32),
                ],
                axis=0,
            ).astype(jnp.bfloat16)
            want = iota((BLOCK, A_DEV), 0) + (k * BLOCK).astype(jnp.float32)
            pick = jnp.where(want == spot[side : side + 1], 1.0, 0.0).astype(jnp.bfloat16)
            moved = lax.dot_general(
                rows, pick, (((1,), (1,)), ((), ())), preferred_element_type=jnp.float32
            )
            cols = pl.ds(pl.multiple_of(k * BLOCK, BLOCK), BLOCK)
            lists[side, 0:3, cols] = moved[0:3]
            lists[side, 3:4, cols] = moved[3:4] + float(base)
        return 0

    lax.fori_loop(0, steps, window, 0)
    odd = lax.axis_index("gz") % 2
    first[...] = lists[1 - odd]
    second[...] = lists[odd]


def append(ref, brick, number, offset, dx, dy, dz, merged):
    lanes = lax.broadcasted_iota(jnp.int32, (1, A_DEV), 1)
    live = lanes < number
    moved = (X0 - PAD + BX * dx, Y0 - PAD + BY * dy, BZ * dz - PAD)
    rows = [ref[brick, 0:1, 0:A_DEV]]
    for i in range(3):
        place = ref[brick, 1 + i : 2 + i, 0:A_DEV] + jnp.float32(moved[i])
        rows.append(jnp.where(live, place * UNIT, 0.0))
    atoms = jnp.concatenate(rows + [jnp.zeros((4, A_DEV), jnp.float32)], axis=0)
    atoms = jnp.concatenate([atoms, jnp.zeros((8, SPAN - A_DEV), jnp.float32)], axis=1)
    atoms = pltpu.roll(atoms, offset % 128, 1)
    start = pl.multiple_of(offset // 128 * 128, 128)
    merged[:, pl.ds(start, 128)] += atoms[:, 0:128]
    merged[:, pl.ds(start + 128, SPAN - 128)] = atoms[:, 128:SPAN]
    return offset + number


def spread(merged, start, size, x0, nx, y0, ny, grid, rows_x, first):
    cols = pl.ds(pl.multiple_of(start, BLOCK), size)
    charge = merged[0:1, cols]
    xa = merged[1:2, cols]
    ya = merged[2:3, cols]
    za = merged[3:4, cols]
    gy = weight((iota((ny, size), 0) + jnp.float32(y0)) * UNIT, ya) * (charge * (1.0 / SCALE))
    zi = iota((PZ, size), 0)
    zi = jnp.where(zi < 448.0, zi, zi - float(PZ)) * UNIT
    right = weight(zi, za, SCALE).astype(jnp.bfloat16)
    rows_x[:, 0:size] = weight(iota((48, size), 0) * UNIT, xa)
    for c in range(nx // CHUNK):
        at = x0 + c * CHUNK
        left = jnp.stack(
            [rows_x[pl.ds(at + i, 1), 0:size] * gy for i in range(CHUNK)], axis=0
        )
        left = left.reshape(CHUNK * ny, size).astype(jnp.bfloat16)
        part = lax.dot_general(
            left, right, (((1,), (1,)), ((), ())), preferred_element_type=jnp.float32
        )
        part = part.reshape(CHUNK, ny, PZ)
        if first:
            grid[pl.ds(at, CHUNK), pl.ds(y0, ny), :] = part
        else:
            grid[pl.ds(at, CHUNK), pl.ds(y0, ny), :] += part


def spread_all(merged, total, x0, nx, y0, ny, grid, rows_x, clear):
    rest = total % WIDE
    wide = total // WIDE + (rest > BLOCK).astype(jnp.int32)
    if clear:
        wide = jnp.maximum(wide, 1)
        spread(merged, 0, WIDE, x0, nx, y0, ny, grid, rows_x, True)

    def block(k, _):
        spread(merged, k * WIDE, WIDE, x0, nx, y0, ny, grid, rows_x, False)
        return 0

    lax.fori_loop(1 if clear else 0, wide, block, 0)

    @pl.when(total > wide * WIDE)
    def _():
        spread(merged, wide * WIDE, BLOCK, x0, nx, y0, ny, grid, rows_x, False)


def gather(ref, bricks, numbers, merged):
    merged[:, 0:128] = jnp.zeros((8, 128), jnp.float32)
    offset = jnp.int32(0)
    for brick, (dx, dy, dz) in bricks:
        number = numbers[brick, 0, 0].astype(jnp.int32)
        offset = append(ref, brick, number, offset, dx, dy, dz, merged)
    return offset


def slots_of(axis):
    step = toward(axis)
    return (step, 0, -step)


def column(lists, grid, rows_x, merged, numbers, sem):
    copy = pltpu.make_async_copy(lists.at[:, 0:1, A_DEV:WIDTH], numbers, sem)
    copy.start()
    copy.wait()
    xs, zs = slots_of("gx"), slots_of("gz")
    for i in (1, 0, 2):
        total = gather(
            lists,
            [(3 * i + j, (xs[i], 0, zs[j])) for j in (1, 0, 2)],
            numbers,
            merged,
        )
        if i == 1:
            spread_all(merged, total, 0, PX, 0, PY, grid, rows_x, True)
        else:
            x0 = jnp.where(xs[i] > 0, 28, 0)
            spread_all(merged, total, x0, 14, 0, PY, grid, rows_x, False)


def finish(
    near, far, own, charges, before, potential, forces, grid,
    rows_x, fields, merged, numbers, charge, sems,
):
    copies = [
        pltpu.make_async_copy(near.at[:, 0:1, A_DEV:WIDTH], numbers.at[0], sems.at[0]),
        pltpu.make_async_copy(far.at[:, 0:1, A_DEV:WIDTH], numbers.at[1], sems.at[1]),
        pltpu.make_async_copy(own.at[:, 0:1, A_DEV:WIDTH], numbers.at[2, 0:1], sems.at[2]),
        pltpu.make_async_copy(charges, charge, sems.at[3]),
    ]
    for copy in copies:
        copy.start()
    for copy in copies:
        copy.wait()
    xs, zs = slots_of("gx"), slots_of("gz")
    dy = toward("gy")
    for i, ref in enumerate((near, far)):
        step = dy * (1 - 2 * i)
        total = gather(
            ref,
            [(3 * m + j, (xs[m], step, zs[j])) for m in range(3) for j in range(3)],
            numbers.at[i],
            merged,
        )
        y0 = pl.multiple_of(jnp.where(step > 0, 32, 0), 8)
        spread_all(merged, total, 0, PX, y0, 16, grid, rows_x, False)
    copy = pltpu.make_async_copy(
        grid.at[X0 : X0 + BX, Y0 : Y0 + BY, 0:BZ], potential, sems.at[0]
    )
    copy.start()

    def build(c, _):
        gx, gy, gz = [], [], []
        for i in range(FCHUNK):
            x = c * FCHUNK + i
            gx.append(grid[x + 2, 4:44, :] - grid[x, 4:44, :])
            gy.append(grid[x + 1, 5:45, :] - grid[x + 1, 3:43, :])
            mid = grid[x + 1, 4:44, :]
            gz.append(pltpu.roll(mid, PZ - 2, 1) - mid)
        for d, parts in enumerate((gx, gy, gz)):
            both = jnp.stack(parts, axis=0).reshape(ROWS, PZ).astype(jnp.bfloat16)
            fields[d, pl.ds(pl.multiple_of(c * ROWS, ROWS), ROWS), :] = both
        return 0

    lax.fori_loop(0, FX // FCHUNK, build, 0)
    forces[...] = jnp.zeros_like(forces)
    count = numbers[2, 0, 0, 0].astype(jnp.int32)

    def sample(k, _):
        cols = pl.ds(pl.multiple_of(k * BLOCK, BLOCK), BLOCK)
        xa = own[0, 1:2, cols]
        ya = own[0, 2:3, cols]
        za = own[0, 3:4, cols] - float(PAD)
        zi = iota((PZ, BLOCK), 0)
        zi = jnp.where(zi < 448.0, zi, zi - float(PZ))
        depth = jnp.where(zi == za, 1.0, 0.0).astype(jnp.bfloat16)
        below = jnp.where(zi == za - 1.0, 1.0, 0.0).astype(jnp.bfloat16)
        hot_y = iota((FY, BLOCK), 0) == ya
        slots = lax.broadcasted_iota(jnp.int32, (1, BLOCK), 1) + k * BLOCK
        factor = jnp.where(slots < count, -0.5 * charge[0:1, cols], 0.0)
        for d in range(3):
            total = jnp.zeros((FY, BLOCK), jnp.float32)
            for c in range(FX // FCHUNK):
                part = jnp.dot(
                    fields[d, c * ROWS : (c + 1) * ROWS, :],
                    below if d == 2 else depth,
                    preferred_element_type=jnp.float32,
                ).reshape(FCHUNK, FY, BLOCK)
                for i in range(FCHUNK):
                    total = total + jnp.where(xa == float(c * FCHUNK + i), part[i], 0.0)
            value = jnp.sum(jnp.where(hot_y, total, 0.0), axis=0, keepdims=True)
            forces[d, :, cols] = value * factor
        return 0

    lax.fori_loop(0, (count + BLOCK - 1) // BLOCK, sample, 0)
    copy.wait()


def swaps(block, other, axis):
    size = lax.axis_size(axis)
    first = [(i, i ^ 1) for i in range(size)]
    second = [(i, (i + 1 if i % 2 else i - 1) % size) for i in range(size)]
    return lax.ppermute(block, axis, first), lax.ppermute(other, axis, second)


def local(charges, cells, counts):
    charge = charges.reshape(1, A_DEV)
    vmem = pl.BlockSpec(memory_space=pltpu.VMEM)
    hbm = pl.BlockSpec(memory_space=pl.ANY)
    shape = pltpu.VMEM((4, WIDTH), jnp.float32)
    own, first, second = pl.pallas_call(
        compact,
        out_shape=(shape, shape, shape),
        in_specs=[pl.BlockSpec(memory_space=pltpu.SMEM), vmem, vmem],
        out_specs=(vmem,) * 3,
        scratch_shapes=[pltpu.VMEM((2, 4, WIDTH), jnp.float32)],
    )(counts.reshape(1), charge, cells.reshape(3, 1, A_DEV))
    own = own[None]
    first, second = swaps(first[None], second[None], "gz")
    atoms = jnp.concatenate([first, own, second], axis=0)
    first, second = swaps(atoms, atoms, "gx")
    atoms = jnp.concatenate([first, atoms, second], axis=0)
    first, second = swaps(atoms, atoms, "gy")
    limit = 40 * 1024 * 1024
    grid = pl.pallas_call(
        column,
        out_shape=pltpu.VMEM((PX, PY, PZ), jnp.float32),
        in_specs=[vmem],
        out_specs=vmem,
        scratch_shapes=[
            pltpu.VMEM((48, WIDE), jnp.float32),
            pltpu.VMEM((8, MERGED), jnp.float32),
            pltpu.SMEM((9, 1, WIDTH - A_DEV), jnp.float32),
            pltpu.SemaphoreType.DMA,
        ],
        compiler_params=pltpu.CompilerParams(vmem_limit_bytes=limit),
        cost_estimate=pl.CostEstimate(flops=6 * 10**9, bytes_accessed=10**6, transcendentals=0),
    )(atoms)
    potential, forces, _ = pl.pallas_call(
        finish,
        out_shape=(
            jax.ShapeDtypeStruct((BX, BY, BZ), jnp.float32),
            jax.ShapeDtypeStruct((3, 1, A_DEV), jnp.float32),
            pltpu.VMEM((PX, PY, PZ), jnp.float32),
        ),
        in_specs=[vmem, vmem, vmem, hbm, vmem],
        out_specs=(hbm, vmem, vmem),
        input_output_aliases={4: 2},
        scratch_shapes=[
            pltpu.VMEM((48, WIDE), jnp.float32),
            pltpu.VMEM((3, FX * FY, PZ), jnp.bfloat16),
            pltpu.VMEM((8, MERGED), jnp.float32),
            pltpu.SMEM((3, 9, 1, WIDTH - A_DEV), jnp.float32),
            pltpu.VMEM((1, A_DEV), jnp.float32),
            pltpu.SemaphoreType.DMA((4,)),
        ],
        compiler_params=pltpu.CompilerParams(vmem_limit_bytes=limit),
    )(first, second, own, charge, grid)
    return potential, forces.reshape(1, 1, 1, 3, A_DEV)


def solution(mesh):
    in_specs = (P("gx", "gy", "gz", None), P("gx", "gy", "gz", None, None), P("gx", "gy", "gz"))
    out_specs = (P("gx", "gy", "gz"), P("gx", "gy", "gz", None, None))
    return jax.shard_map(local, mesh=mesh, in_specs=in_specs, out_specs=out_specs, check_vma=False)
```

```python
import functools
import math

import jax
import jax.numpy as jnp
from jax import lax
from jax.experimental import pallas as pl
from jax.experimental.pallas import tpu as pltpu
from jax.sharding import PartitionSpec as P

BX = 32
BY = 32
BZ = 384
A_DEV = 1024
PAD = 4
REACH = 4
WIDTH = A_DEV + 128
BLOCK = 256
WIDE = 2 * BLOCK

X0 = 5
Y0 = 8
PX = 42
PY = 48
PZ = 512
CHUNK = 14
FX = 40
FY = 40
FCHUNK = 20

kernel_width = 2.0
EXPONENT = -math.log2(math.e) / (2.0 * kernel_width * kernel_width)
SCALE = 1.3903614627339054
UNIT = math.sqrt(-EXPONENT)
LOW_END = 2 * PAD + 5
HIGH_START = BZ + PAD - 9
SPAN = A_DEV + 128 + WIDE
MERGED = 9 * A_DEV + SPAN
ROWS = FCHUNK * FY


def weight(first, second, scale=1.0):
    away = first - second
    square = away * away
    value = jnp.exp2(math.log2(scale) - square)
    return jnp.where(square < (REACH + 0.5) ** 2 * UNIT * UNIT, value, 0.0)


def iota(shape, dim):
    return lax.broadcasted_iota(jnp.int32, shape, dim).astype(jnp.float32)


def toward(axis):
    return 1 - 2 * (lax.axis_index(axis) % 2)


def compact(numbers, charges, cells, own, first, second, lists):
    count = numbers[0]
    slots = lax.broadcasted_iota(jnp.int32, (1, A_DEV), 1)
    live = slots < count
    charge = jnp.where(live, charges[...], 0.0).astype(jnp.bfloat16).astype(jnp.float32)
    places = jnp.concatenate([jnp.where(live, cells[i], 0) for i in range(3)], axis=0)
    own[0:1, 0:A_DEV] = charge
    own[1:4, 0:A_DEV] = places.astype(jnp.float32)
    own[:, A_DEV:WIDTH] = jnp.full((4, WIDTH - A_DEV), count.astype(jnp.float32))
    depth = places[2:3]
    before = jnp.concatenate(
        [
            jnp.where(live & (depth < LOW_END), 1.0, 0.0),
            jnp.where(live & (depth >= HIGH_START), 1.0, 0.0),
            jnp.zeros((6, A_DEV), jnp.float32),
        ],
        axis=0,
    )
    near = before
    lanes = lax.broadcasted_iota(jnp.int32, (8, A_DEV), 1)
    shift = 1
    while shift < A_DEV:
        before = before + jnp.where(lanes >= shift, pltpu.roll(before, shift, 1), 0.0)
        shift *= 2
    totals = before[:, A_DEV - 1 : A_DEV]
    spot = jnp.where(near > 0.5, before - 1.0, -1.0)
    steps = (jnp.max(totals).astype(jnp.int32) + BLOCK - 1) // BLOCK
    for side in range(2):
        lists[side, :, 0:A_DEV] = jnp.zeros((4, A_DEV), jnp.float32)
        lists[side, :, A_DEV:WIDTH] = jnp.broadcast_to(
            totals[side : side + 1], (4, WIDTH - A_DEV)
        )

    def window(k, _):
        for side, base in enumerate((0, BZ // 2)):
            rows = jnp.concatenate(
                [
                    charge,
                    places[0:2].astype(jnp.float32),
                    (places[2:3] - base).astype(jnp.float32),
                    jnp.zeros((4, A_DEV), jnp.float32),
                ],
                axis=0,
            ).astype(jnp.bfloat16)
            want = iota((BLOCK, A_DEV), 0) + (k * BLOCK).astype(jnp.float32)
            pick = jnp.where(want == spot[side : side + 1], 1.0, 0.0).astype(jnp.bfloat16)
            moved = lax.dot_general(
                rows, pick, (((1,), (1,)), ((), ())), preferred_element_type=jnp.float32
            )
            cols = pl.ds(pl.multiple_of(k * BLOCK, BLOCK), BLOCK)
            lists[side, 0:3, cols] = moved[0:3]
            lists[side, 3:4, cols] = moved[3:4] + float(base)
        return 0

    lax.fori_loop(0, steps, window, 0)
    odd = lax.axis_index("gz") % 2
    first[...] = lists[1 - odd]
    second[...] = lists[odd]


def append(ref, brick, number, offset, dx, dy, dz, merged):
    lanes = lax.broadcasted_iota(jnp.int32, (1, A_DEV), 1)
    live = lanes < number
    moved = (X0 - PAD + BX * dx, Y0 - PAD + BY * dy, BZ * dz - PAD)
    rows = [ref[brick, 0:1, 0:A_DEV]]
    for i in range(3):
        place = ref[brick, 1 + i : 2 + i, 0:A_DEV] + jnp.float32(moved[i])
        rows.append(jnp.where(live, place * UNIT, 0.0))
    atoms = jnp.concatenate(rows + [jnp.zeros((4, A_DEV), jnp.float32)], axis=0)
    atoms = jnp.concatenate([atoms, jnp.zeros((8, SPAN - A_DEV), jnp.float32)], axis=1)
    atoms = pltpu.roll(atoms, offset % 128, 1)
    start = pl.multiple_of(offset // 128 * 128, 128)
    merged[:, pl.ds(start, 128)] += atoms[:, 0:128]
    merged[:, pl.ds(start + 128, SPAN - 128)] = atoms[:, 128:SPAN]
    return offset + number


def spread(merged, start, size, x0, nx, y0, ny, grid, rows_x, first):
    cols = pl.ds(pl.multiple_of(start, BLOCK), size)
    charge = merged[0:1, cols]
    xa = merged[1:2, cols]
    ya = merged[2:3, cols]
    za = merged[3:4, cols]
    gy = weight((iota((ny, size), 0) + jnp.float32(y0)) * UNIT, ya) * (charge * (1.0 / SCALE))
    zi = iota((PZ, size), 0)
    zi = jnp.where(zi < 448.0, zi, zi - float(PZ)) * UNIT
    right = weight(zi, za, SCALE).astype(jnp.bfloat16)
    rows_x[:, 0:size] = weight(iota((48, size), 0) * UNIT, xa)
    chunk = min(nx, CHUNK * PY // ny)
    for c in range(0, nx, chunk):
        at = x0 + c
        left = jnp.stack(
            [rows_x[pl.ds(at + i, 1), 0:size] * gy for i in range(chunk)], axis=0
        )
        left = left.reshape(chunk * ny, size).astype(jnp.bfloat16)
        part = lax.dot_general(
            left, right, (((1,), (1,)), ((), ())), preferred_element_type=jnp.float32
        )
        part = part.reshape(chunk, ny, PZ)
        if first:
            grid[pl.ds(at, chunk), pl.ds(y0, ny), :] = part
        else:
            grid[pl.ds(at, chunk), pl.ds(y0, ny), :] += part


def spread_all(merged, total, x0, nx, y0, ny, grid, rows_x, clear):
    rest = total % WIDE
    wide = total // WIDE + (rest > BLOCK).astype(jnp.int32)
    if clear:
        wide = jnp.maximum(wide, 1)
        spread(merged, 0, WIDE, x0, nx, y0, ny, grid, rows_x, True)

    def block(k, _):
        spread(merged, k * WIDE, WIDE, x0, nx, y0, ny, grid, rows_x, False)
        return 0

    lax.fori_loop(1 if clear else 0, wide, block, 0)

    @pl.when(total > wide * WIDE)
    def _():
        spread(merged, wide * WIDE, BLOCK, x0, nx, y0, ny, grid, rows_x, False)


def gather(ref, bricks, numbers, merged):
    merged[:, 0:128] = jnp.zeros((8, 128), jnp.float32)
    offset = jnp.int32(0)
    for brick, (dx, dy, dz) in bricks:
        number = numbers[brick, 0, 0].astype(jnp.int32)
        offset = append(ref, brick, number, offset, dx, dy, dz, merged)
    return offset


def slots_of(axis):
    step = toward(axis)
    return (step, 0, -step)


def column(lists, grid, rows_x, merged, numbers, sem):
    copy = pltpu.make_async_copy(lists.at[:, 0:1, A_DEV:WIDTH], numbers, sem)
    copy.start()
    copy.wait()
    xs, zs = slots_of("gx"), slots_of("gz")
    for i in (1, 0, 2):
        total = gather(
            lists,
            [(3 * i + j, (xs[i], 0, zs[j])) for j in (1, 0, 2)],
            numbers,
            merged,
        )
        if i == 1:
            spread_all(merged, total, 0, PX, 0, PY, grid, rows_x, True)
        else:
            x0 = jnp.where(xs[i] > 0, 28, 0)
            spread_all(merged, total, x0, 14, 0, PY, grid, rows_x, False)


def finish(
    near, far, own, charges, before, potential, forces, grid,
    rows_x, fields, merged, numbers, charge, sems,
):
    copies = [
        pltpu.make_async_copy(near.at[:, 0:1, A_DEV:WIDTH], numbers.at[0], sems.at[0]),
        pltpu.make_async_copy(far.at[:, 0:1, A_DEV:WIDTH], numbers.at[1], sems.at[1]),
        pltpu.make_async_copy(own.at[:, 0:1, A_DEV:WIDTH], numbers.at[2, 0:1], sems.at[2]),
        pltpu.make_async_copy(charges, charge, sems.at[3]),
    ]
    for copy in copies:
        copy.start()
    for copy in copies:
        copy.wait()
    xs, zs = slots_of("gx"), slots_of("gz")
    dy = toward("gy")
    for i, ref in enumerate((near, far)):
        step = dy * (1 - 2 * i)
        total = gather(
            ref,
            [(3 * m + j, (xs[m], step, zs[j])) for m in range(3) for j in range(3)],
            numbers.at[i],
            merged,
        )
        y0 = pl.multiple_of(jnp.where(step > 0, 32, 0), 8)
        spread_all(merged, total, 0, PX, y0, 16, grid, rows_x, False)
    copy = pltpu.make_async_copy(
        grid.at[X0 : X0 + BX, Y0 : Y0 + BY, 0:BZ], potential, sems.at[0]
    )
    copy.start()

    forces[...] = jnp.zeros_like(forces)
    count = numbers[2, 0, 0, 0].astype(jnp.int32)

    def build(c):
        gx, gy, gz = [], [], []
        for x in range(c * FCHUNK, (c + 1) * FCHUNK):
            gx.append(grid[x + 2, 4:44, :] - grid[x, 4:44, :])
            gy.append(grid[x + 1, 5:45, :] - grid[x + 1, 3:43, :])
            mid = grid[x + 1, 4:44, :]
            gz.append(pltpu.roll(mid, PZ - 2, 1) - mid)
        for d, parts in enumerate((gx, gy, gz)):
            both = jnp.stack(parts, axis=0).reshape(ROWS, PZ).astype(jnp.bfloat16)
            fields[d, c * ROWS : (c + 1) * ROWS, :] = both

    def sample(start, size, fresh):
        cols = pl.ds(pl.multiple_of(start, BLOCK), size)
        xa = own[0, 1:2, cols]
        za = own[0, 3:4, cols] - float(PAD)
        zi = iota((PZ, size), 0)
        zi = jnp.where(zi < 448.0, zi, zi - float(PZ))
        depth = jnp.where(zi == za, 1.0, 0.0).astype(jnp.bfloat16)
        below = jnp.where(zi == za - 1.0, 1.0, 0.0).astype(jnp.bfloat16)
        sums = [jnp.zeros((FY, size), jnp.float32)] * 3
        for c in range(FX // FCHUNK):
            if fresh:
                build(c)
            for d in range(3):
                part = jnp.dot(
                    fields[d, c * ROWS : (c + 1) * ROWS, :],
                    below if d == 2 else depth,
                    preferred_element_type=jnp.float32,
                ).reshape(FCHUNK, FY, size)
                for i in range(FCHUNK):
                    hot_x = xa == float(c * FCHUNK + i)
                    sums[d] = sums[d] + jnp.where(hot_x, part[i], 0.0)
        hot_y = iota((FY, size), 0) == own[0, 2:3, cols]
        slots = lax.broadcasted_iota(jnp.int32, (1, size), 1) + start
        factor = jnp.where(slots < count, -0.5 * charge[0:1, cols], 0.0)
        for d in range(3):
            value = jnp.sum(jnp.where(hot_y, sums[d], 0.0), axis=0, keepdims=True)
            forces[d, :, cols] = value * factor

    sample(0, WIDE, True)

    def more(k, _):
        sample(k * WIDE, WIDE, False)
        return 0

    lax.fori_loop(1, (count + WIDE - 1) // WIDE, more, 0)
    copy.wait()


def swaps(block, other, axis):
    size = lax.axis_size(axis)
    first = [(i, i ^ 1) for i in range(size)]
    second = [(i, (i + 1 if i % 2 else i - 1) % size) for i in range(size)]
    return lax.ppermute(block, axis, first), lax.ppermute(other, axis, second)


VMEM = pl.BlockSpec(memory_space=pltpu.VMEM)
HBM = pl.BlockSpec(memory_space=pl.ANY)
LIMIT = 40 * 1024 * 1024


def call_compact(counts, charge, cells):
    shape = pltpu.VMEM((4, WIDTH), jnp.float32)
    return pl.pallas_call(
        compact,
        out_shape=(shape, shape, shape),
        in_specs=[pl.BlockSpec(memory_space=pltpu.SMEM), VMEM, VMEM],
        out_specs=(VMEM,) * 3,
        scratch_shapes=[pltpu.VMEM((2, 4, WIDTH), jnp.float32)],
    )(counts, charge, cells)


def call_column(atoms):
    return pl.pallas_call(
        column,
        out_shape=pltpu.VMEM((PX, PY, PZ), jnp.float32),
        in_specs=[VMEM],
        out_specs=VMEM,
        scratch_shapes=[
            pltpu.VMEM((48, WIDE), jnp.float32),
            pltpu.VMEM((8, MERGED), jnp.float32),
            pltpu.SMEM((9, 1, WIDTH - A_DEV), jnp.float32),
            pltpu.SemaphoreType.DMA,
        ],
        compiler_params=pltpu.CompilerParams(vmem_limit_bytes=LIMIT),
        cost_estimate=pl.CostEstimate(flops=6 * 10**9, bytes_accessed=10**6, transcendentals=0),
    )(atoms)


def call_finish(near, far, own, charge, grid):
    potential, forces, _ = pl.pallas_call(
        finish,
        out_shape=(
            jax.ShapeDtypeStruct((BX, BY, BZ), jnp.float32),
            jax.ShapeDtypeStruct((3, 1, A_DEV), jnp.float32),
            pltpu.VMEM((PX, PY, PZ), jnp.float32),
        ),
        in_specs=[VMEM, VMEM, VMEM, HBM, VMEM],
        out_specs=(HBM, VMEM, VMEM),
        input_output_aliases={4: 2},
        scratch_shapes=[
            pltpu.VMEM((48, WIDE), jnp.float32),
            pltpu.VMEM((3, FX * FY, PZ), jnp.bfloat16),
            pltpu.VMEM((8, MERGED), jnp.float32),
            pltpu.SMEM((3, 9, 1, WIDTH - A_DEV), jnp.float32),
            pltpu.VMEM((1, A_DEV), jnp.float32),
            pltpu.SemaphoreType.DMA((4,)),
        ],
        compiler_params=pltpu.CompilerParams(vmem_limit_bytes=LIMIT),
    )(near, far, own, charge, grid)
    return potential, forces


def local(charges, cells, counts):
    charge = charges.reshape(1, A_DEV)
    own, first, second = call_compact(counts.reshape(1), charge, cells.reshape(3, 1, A_DEV))
    own = own[None]
    first, second = swaps(first[None], second[None], "gz")
    atoms = jnp.concatenate([first, own, second], axis=0)
    first, second = swaps(atoms, atoms, "gx")
    atoms = jnp.concatenate([first, atoms, second], axis=0)
    first, second = swaps(atoms, atoms, "gy")
    grid = call_column(atoms)
    potential, forces = call_finish(first, second, own, charge, grid)
    return potential, forces.reshape(1, 1, 1, 3, A_DEV)


def solution(mesh):
    in_specs = (P("gx", "gy", "gz", None), P("gx", "gy", "gz", None, None), P("gx", "gy", "gz"))
    out_specs = (P("gx", "gy", "gz"), P("gx", "gy", "gz", None, None))
    return jax.shard_map(local, mesh=mesh, in_specs=in_specs, out_specs=out_specs, check_vma=False)
```

```python
import functools
import math

import jax
import jax.numpy as jnp
from jax import lax
from jax.experimental import pallas as pl
from jax.experimental.pallas import tpu as pltpu
from jax.sharding import PartitionSpec as P

BX = 32
BY = 32
BZ = 384
A_DEV = 1024
PAD = 4
REACH = 4
WIDTH = A_DEV + 128
BLOCK = 256
SMALL = 128
WIDE = 2 * BLOCK

X0 = 5
Y0 = 8
PX = 42
PY = 48
PZ = 512
CHUNK = 14
FX = 40
FY = 40
FCHUNK = 20

kernel_width = 2.0
EXPONENT = -math.log2(math.e) / (2.0 * kernel_width * kernel_width)
SCALE = 1.3903614627339054
UNIT = math.sqrt(-EXPONENT)
LOW_END = 2 * PAD + 5
HIGH_START = BZ + PAD - 9
HIGH_START_Y = BY + PAD - 9
MIDDLE = BZ // 2
SPAN = A_DEV + 256 + WIDE
FRONT = 128
MERGED = 9 * A_DEV + SPAN + FRONT
ROWS = FCHUNK * FY


def weight(first, second, scale=1.0):
    away = first - second
    square = away * away
    value = jnp.exp2(math.log2(scale) - square)
    return jnp.where(square < (REACH + 0.5) ** 2 * UNIT * UNIT, value, 0.0)


def iota(shape, dim):
    return lax.broadcasted_iota(jnp.int32, shape, dim).astype(jnp.float32)


def toward(axis):
    return 1 - 2 * (lax.axis_index(axis) % 2)


def live_atoms(numbers, charges, cells):
    live = lax.broadcasted_iota(jnp.int32, (1, A_DEV), 1) < numbers[0]
    charge = jnp.where(live, charges[...], 0.0).astype(jnp.bfloat16).astype(jnp.float32)
    places = [jnp.where(live, cells[i], 0) for i in range(3)]
    rows = [charge] + [place.astype(jnp.float32) for place in places[:2]]
    rows.append((places[2] - MIDDLE).astype(jnp.float32))
    rows.append(jnp.zeros((4, A_DEV), jnp.float32))
    return live, places, jnp.concatenate(rows, axis=0).astype(jnp.bfloat16)


def running_sums(masks):
    rows = [jnp.where(mask, 1.0, 0.0) for mask in masks]
    rows.append(jnp.zeros((8 - len(masks), A_DEV), jnp.float32))
    near = jnp.concatenate(rows, axis=0)
    sums = near
    lanes = lax.broadcasted_iota(jnp.int32, (8, A_DEV), 1)
    shift = 1
    while shift < A_DEV:
        sums = sums + jnp.where(lanes >= shift, pltpu.roll(sums, shift, 1), 0.0)
        shift *= 2
    return sums, near


def pick(rows, spot, start, size):
    want = iota((size, A_DEV), 0) + start.astype(jnp.float32)
    hot = jnp.where(want == spot, 1.0, 0.0).astype(jnp.bfloat16)
    return lax.dot_general(
        rows, hot, (((1,), (1,)), ((), ())), preferred_element_type=jnp.float32
    )


def compact(numbers, charges, cells, first, second, lists):
    live, places, rows = live_atoms(numbers, charges, cells)
    depth = places[2]
    sums, near = running_sums([live & (depth < LOW_END), live & (depth >= HIGH_START)])
    totals = sums[:, A_DEV - 1 : A_DEV]
    spot = jnp.where(near > 0.5, sums - 1.0, -1.0)
    steps = (jnp.max(totals).astype(jnp.int32) + SMALL - 1) // SMALL
    for side in range(2):
        lists[side, :, 0:A_DEV] = jnp.zeros((4, A_DEV), jnp.float32)
        lists[side, :, A_DEV:WIDTH] = jnp.broadcast_to(
            totals[side : side + 1], (4, WIDTH - A_DEV)
        )

    def window(k, _):
        cols = pl.ds(pl.multiple_of(k * SMALL, SMALL), SMALL)
        for side in range(2):
            moved = pick(rows, spot[side : side + 1], k * SMALL, SMALL)
            lists[side, 0:3, cols] = moved[0:3]
            lists[side, 3:4, cols] = moved[3:4] + float(MIDDLE)
        return 0

    lax.fori_loop(0, steps, window, 0)
    odd = lax.axis_index("gz") % 2
    first[...] = lists[1 - odd]
    second[...] = lists[odd]


def arrange(numbers, charges, cells, own):
    live, places, rows = live_atoms(numbers, charges, cells)
    high = live & (places[1] >= HIGH_START_Y)
    low = live & (places[1] < LOW_END)
    sums, near = running_sums([high, low, live])
    totals = sums[:, A_DEV - 1 : A_DEV]
    middle_at = totals[0:1] - 1.0
    low_at = totals[2:3] - totals[1:2] - 1.0
    spot = jnp.where(low, low_at + sums[1:2], middle_at + sums[2:3] - sums[0:1] - sums[1:2])
    spot = jnp.where(high, sums[0:1] - 1.0, spot)
    spot = jnp.where(live, spot, -1.0)
    own[:, 0:A_DEV] = jnp.zeros((4, A_DEV), jnp.float32)
    for row, total in enumerate((2, 0, 1, 2)):
        own[row : row + 1, A_DEV:WIDTH] = jnp.broadcast_to(
            totals[total : total + 1], (1, WIDTH - A_DEV)
        )

    def window(k, _):
        cols = pl.ds(pl.multiple_of(k * BLOCK, BLOCK), BLOCK)
        moved = pick(rows, spot, k * BLOCK, BLOCK)
        own[0:3, cols] = moved[0:3]
        own[3:4, cols] = moved[3:4] + float(MIDDLE)
        return 0

    lax.fori_loop(0, (numbers[0] + BLOCK - 1) // BLOCK, window, 0)


def append(ref, brick, start, number, offset, dx, dy, dz, merged, padded):
    moved = (X0 - PAD + BX * dx, Y0 - PAD + BY * dy, BZ * dz - PAD)
    padded[0:1, 0:A_DEV] = ref[brick, 0:1, 0:A_DEV]
    for i in range(3):
        place = ref[brick, 1 + i : 2 + i, 0:A_DEV] + jnp.float32(moved[i])
        padded[1 + i : 2 + i, 0:A_DEV] = place * UNIT
    skip = start % 128
    atoms = padded[:, pl.ds(pl.multiple_of(start - skip, 128), SPAN)]
    lanes = lax.broadcasted_iota(jnp.int32, (8, SPAN), 1)
    atoms = jnp.where((lanes >= skip) & (lanes < skip + number), atoms, 0.0)
    room = offset % 128
    back = jnp.where(room >= skip, 0, 128)
    atoms = pltpu.roll(atoms, room - skip + back, 1)
    base = pl.multiple_of(FRONT + offset - room - back, 128)
    merged[:, pl.ds(base, 256)] += atoms[:, 0:256]
    merged[:, pl.ds(base + 256, SPAN - 256)] = atoms[:, 256:SPAN]
    return offset + number


def spread(merged, start, size, x0, nx, y0, ny, grid, rows_x, first):
    cols = pl.ds(pl.multiple_of(start + FRONT, 128), size)
    charge = merged[0:1, cols]
    xa = merged[1:2, cols]
    ya = merged[2:3, cols]
    za = merged[3:4, cols]
    gy = weight((iota((ny, size), 0) + jnp.float32(y0)) * UNIT, ya) * (charge * (1.0 / SCALE))
    zi = iota((PZ, size), 0)
    zi = jnp.where(zi < 448.0, zi, zi - float(PZ)) * UNIT
    right = weight(zi, za, SCALE).astype(jnp.bfloat16)
    rows_x[:, 0:size] = weight(iota((48, size), 0) * UNIT, xa)
    chunk = min(nx, CHUNK * PY // ny)
    for c in range(0, nx, chunk):
        at = x0 + c
        left = jnp.stack(
            [rows_x[pl.ds(at + i, 1), 0:size] * gy for i in range(chunk)], axis=0
        )
        left = left.reshape(chunk * ny, size).astype(jnp.bfloat16)
        part = lax.dot_general(
            left, right, (((1,), (1,)), ((), ())), preferred_element_type=jnp.float32
        )
        part = part.reshape(chunk, ny, PZ)
        if first:
            grid[pl.ds(at, chunk), pl.ds(y0, ny), :] = part
        else:
            grid[pl.ds(at, chunk), pl.ds(y0, ny), :] += part


def spread_all(merged, total, x0, nx, y0, ny, grid, rows_x, clear):
    rest = total % WIDE
    wide = total // WIDE + (rest > BLOCK).astype(jnp.int32)
    if clear:
        wide = jnp.maximum(wide, 1)
        spread(merged, 0, WIDE, x0, nx, y0, ny, grid, rows_x, True)

    def block(k, _):
        spread(merged, k * WIDE, WIDE, x0, nx, y0, ny, grid, rows_x, False)
        return 0

    lax.fori_loop(1 if clear else 0, wide, block, 0)

    @pl.when(total > wide * WIDE)
    def _():
        spread(merged, wide * WIDE, BLOCK, x0, nx, y0, ny, grid, rows_x, False)


def gather(ref, bricks, numbers, side, merged, padded):
    merged[:, 0 : FRONT + 256] = jnp.zeros((8, FRONT + 256), jnp.float32)
    offset = jnp.int32(0)
    for brick, (dx, dy, dz) in bricks:
        number = numbers[brick, 0, 0].astype(jnp.int32)
        start = jnp.int32(0)
        if side is not None:
            low = numbers[brick, 2, 0].astype(jnp.int32)
            start = jnp.where(side > 0, number - low, 0)
            number = jnp.where(side > 0, low, numbers[brick, 1, 0].astype(jnp.int32))
        offset = append(ref, brick, start, number, offset, dx, dy, dz, merged, padded)
    return offset


def slots_of(axis):
    step = toward(axis)
    return (step, 0, -step)


def column(lists, grid, rows_x, merged, padded, numbers, sem):
    copy = pltpu.make_async_copy(lists.at[:, :, A_DEV:WIDTH], numbers, sem)
    copy.start()
    padded[...] = jnp.zeros_like(padded)
    copy.wait()
    xs, zs = slots_of("gx"), slots_of("gz")
    for i in (1, 0, 2):
        total = gather(
            lists,
            [(3 * i + j, (xs[i], 0, zs[j])) for j in (1, 0, 2)],
            numbers,
            None,
            merged,
            padded,
        )
        if i == 1:
            spread_all(merged, total, 0, PX, 0, PY, grid, rows_x, True)
        else:
            x0 = jnp.where(xs[i] > 0, 28, 0)
            spread_all(merged, total, x0, 14, 0, PY, grid, rows_x, False)


def finish(
    near, far, own, charges, cells, before, potential, forces, grid,
    rows_x, fields, merged, padded, numbers, charge, place, sems,
):
    copies = [
        pltpu.make_async_copy(near.at[:, :, A_DEV:WIDTH], numbers.at[0], sems.at[0]),
        pltpu.make_async_copy(far.at[:, :, A_DEV:WIDTH], numbers.at[1], sems.at[1]),
        pltpu.make_async_copy(own.at[:, :, A_DEV:WIDTH], numbers.at[2, 0:1], sems.at[2]),
        pltpu.make_async_copy(charges, charge, sems.at[3]),
        pltpu.make_async_copy(cells, place, sems.at[4]),
    ]
    for copy in copies:
        copy.start()
    padded[...] = jnp.zeros_like(padded)
    for copy in copies[:3]:
        copy.wait()
    xs, zs = slots_of("gx"), slots_of("gz")
    dy = toward("gy")
    for i, ref in enumerate((near, far)):
        step = dy * (1 - 2 * i)
        total = gather(
            ref,
            [(3 * m + j, (xs[m], step, zs[j])) for m in range(3) for j in range(3)],
            numbers.at[i],
            step,
            merged,
            padded,
        )
        y0 = pl.multiple_of(jnp.where(step > 0, 32, 0), 8)
        spread_all(merged, total, 0, PX, y0, 16, grid, rows_x, False)
    copy = pltpu.make_async_copy(
        grid.at[X0 : X0 + BX, Y0 : Y0 + BY, 0:BZ], potential, sems.at[0]
    )
    copy.start()

    for late in copies[3:]:
        late.wait()
    forces[...] = jnp.zeros_like(forces)
    count = numbers[2, 0, 0, 0].astype(jnp.int32)

    def build(c):
        gx, gy, gz = [], [], []
        for x in range(c * FCHUNK, (c + 1) * FCHUNK):
            gx.append(grid[x + 2, 4:44, :] - grid[x, 4:44, :])
            gy.append(grid[x + 1, 5:45, :] - grid[x + 1, 3:43, :])
            mid = grid[x + 1, 4:44, :]
            gz.append(pltpu.roll(mid, PZ - 2, 1) - mid)
        for d, parts in enumerate((gx, gy, gz)):
            both = jnp.stack(parts, axis=0).reshape(ROWS, PZ).astype(jnp.bfloat16)
            fields[d, c * ROWS : (c + 1) * ROWS, :] = both

    def sample(start, size, fresh):
        cols = pl.ds(pl.multiple_of(start, BLOCK), size)
        xa = place[0, :, cols].astype(jnp.float32)
        za = (place[2, :, cols] - PAD).astype(jnp.float32)
        zi = iota((PZ, size), 0)
        zi = jnp.where(zi < 448.0, zi, zi - float(PZ))
        depth = jnp.where(zi == za, 1.0, 0.0).astype(jnp.bfloat16)
        below = jnp.where(zi == za - 1.0, 1.0, 0.0).astype(jnp.bfloat16)
        sums = [jnp.zeros((FY, size), jnp.float32)] * 3
        for c in range(FX // FCHUNK):
            if fresh:
                build(c)
            for d in range(3):
                part = jnp.dot(
                    fields[d, c * ROWS : (c + 1) * ROWS, :],
                    below if d == 2 else depth,
                    preferred_element_type=jnp.float32,
                ).reshape(FCHUNK, FY, size)
                for i in range(FCHUNK):
                    hot_x = xa == float(c * FCHUNK + i)
                    sums[d] = sums[d] + jnp.where(hot_x, part[i], 0.0)
        hot_y = iota((FY, size), 0) == place[1, :, cols].astype(jnp.float32)
        slots = lax.broadcasted_iota(jnp.int32, (1, size), 1) + start
        factor = jnp.where(slots < count, -0.5 * charge[0:1, cols], 0.0)
        for d in range(3):
            value = jnp.sum(jnp.where(hot_y, sums[d], 0.0), axis=0, keepdims=True)
            forces[d, :, cols] = value * factor

    sample(0, WIDE, True)

    def more(k, _):
        sample(k * WIDE, WIDE, False)
        return 0

    lax.fori_loop(1, (count + WIDE - 1) // WIDE, more, 0)
    copy.wait()


def swaps(block, other, axis):
    size = lax.axis_size(axis)
    first = [(i, i ^ 1) for i in range(size)]
    second = [(i, (i + 1 if i % 2 else i - 1) % size) for i in range(size)]
    return lax.ppermute(block, axis, first), lax.ppermute(other, axis, second)


VMEM = pl.BlockSpec(memory_space=pltpu.VMEM)
HBM = pl.BlockSpec(memory_space=pl.ANY)
LIMIT = 40 * 1024 * 1024


def call_compact(counts, charge, cells):
    shape = pltpu.VMEM((4, WIDTH), jnp.float32)
    return pl.pallas_call(
        compact,
        out_shape=(shape, shape),
        in_specs=[pl.BlockSpec(memory_space=pltpu.SMEM), VMEM, VMEM],
        out_specs=(VMEM,) * 2,
        scratch_shapes=[pltpu.VMEM((2, 4, WIDTH), jnp.float32)],
    )(counts, charge, cells)


def call_arrange(counts, charge, cells):
    return pl.pallas_call(
        arrange,
        out_shape=pltpu.VMEM((4, WIDTH), jnp.float32),
        in_specs=[pl.BlockSpec(memory_space=pltpu.SMEM), VMEM, VMEM],
        out_specs=VMEM,
        cost_estimate=pl.CostEstimate(flops=2 * 10**9, bytes_accessed=10**5, transcendentals=0),
    )(counts, charge, cells)


def call_column(atoms):
    return pl.pallas_call(
        column,
        out_shape=pltpu.VMEM((PX, PY, PZ), jnp.float32),
        in_specs=[VMEM],
        out_specs=VMEM,
        scratch_shapes=[
            pltpu.VMEM((48, WIDE), jnp.float32),
            pltpu.VMEM((8, MERGED), jnp.float32),
            pltpu.VMEM((8, A_DEV + SPAN), jnp.float32),
            pltpu.SMEM((9, 4, WIDTH - A_DEV), jnp.float32),
            pltpu.SemaphoreType.DMA,
        ],
        compiler_params=pltpu.CompilerParams(vmem_limit_bytes=LIMIT),
        cost_estimate=pl.CostEstimate(flops=6 * 10**9, bytes_accessed=10**6, transcendentals=0),
    )(atoms)


def call_finish(near, far, own, charge, cells, grid):
    potential, forces, _ = pl.pallas_call(
        finish,
        out_shape=(
            jax.ShapeDtypeStruct((BX, BY, BZ), jnp.float32),
            jax.ShapeDtypeStruct((3, 1, A_DEV), jnp.float32),
            pltpu.VMEM((PX, PY, PZ), jnp.float32),
        ),
        in_specs=[VMEM, VMEM, VMEM, HBM, HBM, VMEM],
        out_specs=(HBM, VMEM, VMEM),
        input_output_aliases={5: 2},
        scratch_shapes=[
            pltpu.VMEM((48, WIDE), jnp.float32),
            pltpu.VMEM((3, FX * FY, PZ), jnp.bfloat16),
            pltpu.VMEM((8, MERGED), jnp.float32),
            pltpu.VMEM((8, A_DEV + SPAN), jnp.float32),
            pltpu.SMEM((3, 9, 4, WIDTH - A_DEV), jnp.float32),
            pltpu.VMEM((1, A_DEV), jnp.float32),
            pltpu.VMEM((3, 1, A_DEV), jnp.int32),
            pltpu.SemaphoreType.DMA((5,)),
        ],
        compiler_params=pltpu.CompilerParams(vmem_limit_bytes=LIMIT),
    )(near, far, own, charge, cells, grid)
    return potential, forces


def local(charges, cells, counts):
    charge = charges.reshape(1, A_DEV)
    cells = cells.reshape(3, 1, A_DEV)
    counts = counts.reshape(1)
    first, second = call_compact(counts, charge, cells)
    own = call_arrange(counts, charge, cells)[None]
    first, second = swaps(first[None], second[None], "gz")
    atoms = jnp.concatenate([first, own, second], axis=0)
    first, second = swaps(atoms, atoms, "gx")
    atoms = jnp.concatenate([first, atoms, second], axis=0)
    first, second = swaps(atoms, atoms, "gy")
    grid = call_column(atoms)
    potential, forces = call_finish(first, second, own, charge, cells, grid)
    return potential, forces.reshape(1, 1, 1, 3, A_DEV)


def solution(mesh):
    in_specs = (P("gx", "gy", "gz", None), P("gx", "gy", "gz", None, None), P("gx", "gy", "gz"))
    out_specs = (P("gx", "gy", "gz"), P("gx", "gy", "gz", None, None))
    return jax.shard_map(local, mesh=mesh, in_specs=in_specs, out_specs=out_specs, check_vma=False)
```

```python
import functools
import math

import jax
import jax.numpy as jnp
from jax import lax
from jax.experimental import pallas as pl
from jax.experimental.pallas import tpu as pltpu
from jax.sharding import PartitionSpec as P

BX = 32
BY = 32
BZ = 384
A_DEV = 1024
PAD = 4
REACH = 4
WIDTH = A_DEV + 128
BLOCK = 256
SMALL = 128
WIDE = 2 * BLOCK

X0 = 5
Y0 = 8
PX = 42
PY = 48
PZ = 512
CHUNK = 14
FX = 40
FY = 40
FCHUNK = 20

kernel_width = 2.0
EXPONENT = -math.log2(math.e) / (2.0 * kernel_width * kernel_width)
SCALE = 1.3903614627339054
UNIT = math.sqrt(-EXPONENT)
LOW_END = 2 * PAD + 5
HIGH_START = BZ + PAD - 9
HIGH_START_Y = BY + PAD - 9
MIDDLE = BZ // 2
SPAN = A_DEV + 256 + WIDE
FRONT = 128
MERGED = 9 * A_DEV + SPAN + FRONT
ROWS = FCHUNK * FY


def weight(first, second, scale=1.0):
    away = first - second
    square = away * away
    value = jnp.exp2(math.log2(scale) - square)
    return jnp.where(square < (REACH + 0.5) ** 2 * UNIT * UNIT, value, 0.0)


def iota(shape, dim):
    return lax.broadcasted_iota(jnp.int32, shape, dim).astype(jnp.float32)


def toward(axis):
    return 1 - 2 * (lax.axis_index(axis) % 2)


def live_atoms(numbers, charges, cells):
    live = lax.broadcasted_iota(jnp.int32, (1, A_DEV), 1) < numbers[0]
    charge = jnp.where(live, charges[...], 0.0).astype(jnp.bfloat16).astype(jnp.float32)
    places = [jnp.where(live, cells[i], 0) for i in range(3)]
    rows = [charge] + [place.astype(jnp.float32) for place in places[:2]]
    rows.append((places[2] - MIDDLE).astype(jnp.float32))
    rows.append(jnp.zeros((4, A_DEV), jnp.float32))
    return live, places, jnp.concatenate(rows, axis=0).astype(jnp.bfloat16)


def running_sums(masks):
    rows = [jnp.where(mask, 1.0, 0.0) for mask in masks]
    rows.append(jnp.zeros((8 - len(masks), A_DEV), jnp.float32))
    near = jnp.concatenate(rows, axis=0)
    sums = near
    lanes = lax.broadcasted_iota(jnp.int32, (8, A_DEV), 1)
    shift = 1
    while shift < A_DEV:
        sums = sums + jnp.where(lanes >= shift, pltpu.roll(sums, shift, 1), 0.0)
        shift *= 2
    return sums, near


def pick(rows, spot, start, size):
    want = iota((size, A_DEV), 0) + start.astype(jnp.float32)
    hot = jnp.where(want == spot, 1.0, 0.0).astype(jnp.bfloat16)
    return lax.dot_general(
        rows, hot, (((1,), (1,)), ((), ())), preferred_element_type=jnp.float32
    )


def compact(numbers, charges, cells, first, second, lists):
    live, places, rows = live_atoms(numbers, charges, cells)
    depth = places[2]
    sums, near = running_sums([live & (depth < LOW_END), live & (depth >= HIGH_START)])
    totals = sums[:, A_DEV - 1 : A_DEV]
    spot = jnp.where(near > 0.5, sums - 1.0, -1.0)
    steps = (jnp.max(totals).astype(jnp.int32) + SMALL - 1) // SMALL
    for side in range(2):
        lists[side, :, 0:A_DEV] = jnp.zeros((4, A_DEV), jnp.float32)
        lists[side, :, A_DEV:WIDTH] = jnp.broadcast_to(
            totals[side : side + 1], (4, WIDTH - A_DEV)
        )

    def window(k, _):
        cols = pl.ds(pl.multiple_of(k * SMALL, SMALL), SMALL)
        for side in range(2):
            moved = pick(rows, spot[side : side + 1], k * SMALL, SMALL)
            lists[side, 0:3, cols] = moved[0:3]
            lists[side, 3:4, cols] = moved[3:4] + float(MIDDLE)
        return 0

    lax.fori_loop(0, steps, window, 0)
    odd = lax.axis_index("gz") % 2
    first[...] = lists[1 - odd]
    second[...] = lists[odd]


def arrange(numbers, charges, cells, own):
    live, places, rows = live_atoms(numbers, charges, cells)
    high = live & (places[1] >= HIGH_START_Y)
    low = live & (places[1] < LOW_END)
    sums, near = running_sums([high, low, live])
    totals = sums[:, A_DEV - 1 : A_DEV]
    middle_at = totals[0:1] - 1.0
    low_at = totals[2:3] - totals[1:2] - 1.0
    spot = jnp.where(low, low_at + sums[1:2], middle_at + sums[2:3] - sums[0:1] - sums[1:2])
    spot = jnp.where(high, sums[0:1] - 1.0, spot)
    spot = jnp.where(live, spot, -1.0)
    own[:, 0:A_DEV] = jnp.zeros((4, A_DEV), jnp.float32)
    for row, total in enumerate((2, 0, 1, 2)):
        own[row : row + 1, A_DEV:WIDTH] = jnp.broadcast_to(
            totals[total : total + 1], (1, WIDTH - A_DEV)
        )

    def window(k, _):
        cols = pl.ds(pl.multiple_of(k * BLOCK, BLOCK), BLOCK)
        moved = pick(rows, spot, k * BLOCK, BLOCK)
        own[0:3, cols] = moved[0:3]
        own[3:4, cols] = moved[3:4] + float(MIDDLE)
        return 0

    lax.fori_loop(0, (numbers[0] + BLOCK - 1) // BLOCK, window, 0)


def append(ref, brick, start, number, offset, dx, dy, dz, merged, padded):
    moved = (X0 - PAD + BX * dx, Y0 - PAD + BY * dy, BZ * dz - PAD)
    padded[0:1, 0:A_DEV] = ref[brick, 0:1, 0:A_DEV]
    for i in range(3):
        place = ref[brick, 1 + i : 2 + i, 0:A_DEV] + jnp.float32(moved[i])
        padded[1 + i : 2 + i, 0:A_DEV] = place * UNIT
    skip = start % 128
    atoms = padded[:, pl.ds(pl.multiple_of(start - skip, 128), SPAN)]
    lanes = lax.broadcasted_iota(jnp.int32, (8, SPAN), 1)
    atoms = jnp.where((lanes >= skip) & (lanes < skip + number), atoms, 0.0)
    room = offset % 128
    back = jnp.where(room >= skip, 0, 128)
    atoms = pltpu.roll(atoms, room - skip + back, 1)
    base = pl.multiple_of(FRONT + offset - room - back, 128)
    merged[:, pl.ds(base, 256)] += atoms[:, 0:256]
    merged[:, pl.ds(base + 256, SPAN - 256)] = atoms[:, 256:SPAN]
    return offset + number


def spread(merged, start, size, x0, nx, y0, ny, grid, rows_x, first):
    cols = pl.ds(pl.multiple_of(start + FRONT, 128), size)
    charge = merged[0:1, cols]
    xa = merged[1:2, cols]
    ya = merged[2:3, cols]
    za = merged[3:4, cols]
    gy = weight((iota((ny, size), 0) + jnp.float32(y0)) * UNIT, ya) * (charge * (1.0 / SCALE))
    zi = iota((PZ, size), 0)
    zi = jnp.where(zi < 448.0, zi, zi - float(PZ)) * UNIT
    right = weight(zi, za, SCALE).astype(jnp.bfloat16)
    rows_x[:, 0:size] = weight(iota((48, size), 0) * UNIT, xa)
    chunk = min(nx, CHUNK * PY // ny)
    for c in range(0, nx, chunk):
        at = x0 + c
        left = jnp.stack(
            [rows_x[pl.ds(at + i, 1), 0:size] * gy for i in range(chunk)], axis=0
        )
        left = left.reshape(chunk * ny, size).astype(jnp.bfloat16)
        part = lax.dot_general(
            left, right, (((1,), (1,)), ((), ())), preferred_element_type=jnp.float32
        )
        part = part.reshape(chunk, ny, PZ)
        if first:
            grid[pl.ds(at, chunk), pl.ds(y0, ny), :] = part
        else:
            grid[pl.ds(at, chunk), pl.ds(y0, ny), :] += part


def spread_all(merged, total, x0, nx, y0, ny, grid, rows_x, clear):
    rest = total % WIDE
    wide = total // WIDE + (rest > BLOCK).astype(jnp.int32)
    if clear:
        wide = jnp.maximum(wide, 1)
        spread(merged, 0, WIDE, x0, nx, y0, ny, grid, rows_x, True)

    def block(k, _):
        spread(merged, k * WIDE, WIDE, x0, nx, y0, ny, grid, rows_x, False)
        return 0

    lax.fori_loop(1 if clear else 0, wide, block, 0)

    @pl.when(total > wide * WIDE)
    def _():
        spread(merged, wide * WIDE, BLOCK, x0, nx, y0, ny, grid, rows_x, False)


def number_of(ref, brick, row):
    return ref[brick, row : row + 1, A_DEV:WIDTH][0, 0].astype(jnp.int32)


def gather(ref, bricks, side, merged, padded):
    merged[:, 0 : FRONT + 256] = jnp.zeros((8, FRONT + 256), jnp.float32)
    offset = jnp.int32(0)
    for brick, (dx, dy, dz) in bricks:
        number = number_of(ref, brick, 0)
        start = jnp.int32(0)
        if side is not None:
            low = number_of(ref, brick, 2)
            start = jnp.where(side > 0, number - low, 0)
            number = jnp.where(side > 0, low, number_of(ref, brick, 1))
        offset = append(ref, brick, start, number, offset, dx, dy, dz, merged, padded)
    return offset


def slots_of(axis):
    step = toward(axis)
    return (step, 0, -step)


def column(lists, grid, rows_x, merged, padded):
    padded[...] = jnp.zeros_like(padded)
    xs, zs = slots_of("gx"), slots_of("gz")
    for i in (1, 0, 2):
        total = gather(
            lists,
            [(3 * i + j, (xs[i], 0, zs[j])) for j in (1, 0, 2)],
            None,
            merged,
            padded,
        )
        if i == 1:
            spread_all(merged, total, 0, PX, 0, PY, grid, rows_x, True)
        else:
            x0 = jnp.where(xs[i] > 0, 28, 0)
            spread_all(merged, total, x0, 14, 0, PY, grid, rows_x, False)


def slab(turn, lists, grid, rows_x, merged, padded):
    padded[...] = jnp.zeros_like(padded)
    xs, zs = slots_of("gx"), slots_of("gz")
    dy = toward("gy") * turn
    total = gather(
        lists,
        [(3 * m + j, (xs[m], dy, zs[j])) for m in range(3) for j in range(3)],
        dy,
        merged,
        padded,
    )
    y0 = pl.multiple_of(jnp.where(dy > 0, 32, 0), 8)
    spread_all(merged, total, 0, PX, y0, 16, grid, rows_x, False)


def add_slab(turn, lists, before, grid, rows_x, merged, padded):
    slab(turn, lists, grid, rows_x, merged, padded)


def finish(
    lists, own, charges, cells, before, potential, forces, grid,
    rows_x, fields, merged, padded, charge, place, sems,
):
    late = [
        pltpu.make_async_copy(charges, charge, sems.at[1]),
        pltpu.make_async_copy(cells, place, sems.at[2]),
    ]
    for copy in late:
        copy.start()
    slab(1, lists, grid, rows_x, merged, padded)
    copy = pltpu.make_async_copy(
        grid.at[X0 : X0 + BX, Y0 : Y0 + BY, 0:BZ], potential, sems.at[0]
    )
    copy.start()

    for one in late:
        one.wait()
    forces[...] = jnp.zeros_like(forces)
    count = number_of(own, 0, 0)

    def build(c):
        gx, gy, gz = [], [], []
        for x in range(c * FCHUNK, (c + 1) * FCHUNK):
            gx.append(grid[x + 2, 4:44, :] - grid[x, 4:44, :])
            gy.append(grid[x + 1, 5:45, :] - grid[x + 1, 3:43, :])
            mid = grid[x + 1, 4:44, :]
            gz.append(pltpu.roll(mid, PZ - 2, 1) - mid)
        for d, parts in enumerate((gx, gy, gz)):
            both = jnp.stack(parts, axis=0).reshape(ROWS, PZ).astype(jnp.bfloat16)
            fields[d, c * ROWS : (c + 1) * ROWS, :] = both

    def sample(start, size, fresh):
        cols = pl.ds(pl.multiple_of(start, BLOCK), size)
        xa = place[0, :, cols].astype(jnp.float32)
        za = (place[2, :, cols] - PAD).astype(jnp.float32)
        zi = iota((PZ, size), 0)
        zi = jnp.where(zi < 448.0, zi, zi - float(PZ))
        depth = jnp.where(zi == za, 1.0, 0.0).astype(jnp.bfloat16)
        below = jnp.where(zi == za - 1.0, 1.0, 0.0).astype(jnp.bfloat16)
        sums = [jnp.zeros((FY, size), jnp.float32)] * 3
        for c in range(FX // FCHUNK):
            if fresh:
                build(c)
            for d in range(3):
                part = jnp.dot(
                    fields[d, c * ROWS : (c + 1) * ROWS, :],
                    below if d == 2 else depth,
                    preferred_element_type=jnp.float32,
                ).reshape(FCHUNK, FY, size)
                for i in range(FCHUNK):
                    hot_x = xa == float(c * FCHUNK + i)
                    sums[d] = sums[d] + jnp.where(hot_x, part[i], 0.0)
        hot_y = iota((FY, size), 0) == place[1, :, cols].astype(jnp.float32)
        slots = lax.broadcasted_iota(jnp.int32, (1, size), 1) + start
        factor = jnp.where(slots < count, -0.5 * charge[0:1, cols], 0.0)
        for d in range(3):
            value = jnp.sum(jnp.where(hot_y, sums[d], 0.0), axis=0, keepdims=True)
            forces[d, :, cols] = value * factor

    sample(0, WIDE, True)

    def more(k, _):
        sample(k * WIDE, WIDE, False)
        return 0

    lax.fori_loop(1, (count + WIDE - 1) // WIDE, more, 0)
    copy.wait()


def swaps(block, other, axis):
    size = lax.axis_size(axis)
    first = [(i, i ^ 1) for i in range(size)]
    second = [(i, (i + 1 if i % 2 else i - 1) % size) for i in range(size)]
    return lax.ppermute(block, axis, first), lax.ppermute(other, axis, second)


VMEM = pl.BlockSpec(memory_space=pltpu.VMEM)
HBM = pl.BlockSpec(memory_space=pl.ANY)
LIMIT = 40 * 1024 * 1024


def call_compact(counts, charge, cells):
    shape = pltpu.VMEM((4, WIDTH), jnp.float32)
    return pl.pallas_call(
        compact,
        out_shape=(shape, shape),
        in_specs=[pl.BlockSpec(memory_space=pltpu.SMEM), VMEM, VMEM],
        out_specs=(VMEM,) * 2,
        scratch_shapes=[pltpu.VMEM((2, 4, WIDTH), jnp.float32)],
    )(counts, charge, cells)


def call_arrange(counts, charge, cells):
    return pl.pallas_call(
        arrange,
        out_shape=pltpu.VMEM((4, WIDTH), jnp.float32),
        in_specs=[pl.BlockSpec(memory_space=pltpu.SMEM), VMEM, VMEM],
        out_specs=VMEM,
        cost_estimate=pl.CostEstimate(flops=2 * 10**9, bytes_accessed=10**5, transcendentals=0),
    )(counts, charge, cells)


def call_column(atoms):
    return pl.pallas_call(
        column,
        out_shape=pltpu.VMEM((PX, PY, PZ), jnp.float32),
        in_specs=[VMEM],
        out_specs=VMEM,
        scratch_shapes=[
            pltpu.VMEM((48, WIDE), jnp.float32),
            pltpu.VMEM((8, MERGED), jnp.float32),
            pltpu.VMEM((8, A_DEV + SPAN), jnp.float32),
        ],
        compiler_params=pltpu.CompilerParams(vmem_limit_bytes=LIMIT),
        cost_estimate=pl.CostEstimate(flops=6 * 10**9, bytes_accessed=10**6, transcendentals=0),
    )(atoms)


def call_slab(turn, lists, grid):
    return pl.pallas_call(
        functools.partial(add_slab, turn),
        out_shape=pltpu.VMEM((PX, PY, PZ), jnp.float32),
        in_specs=[VMEM, VMEM],
        out_specs=VMEM,
        input_output_aliases={1: 0},
        scratch_shapes=[
            pltpu.VMEM((48, WIDE), jnp.float32),
            pltpu.VMEM((8, MERGED), jnp.float32),
            pltpu.VMEM((8, A_DEV + SPAN), jnp.float32),
        ],
        compiler_params=pltpu.CompilerParams(vmem_limit_bytes=LIMIT),
        cost_estimate=pl.CostEstimate(flops=10**9, bytes_accessed=10**6, transcendentals=0),
    )(lists, grid)


def call_finish(lists, own, charge, cells, grid):
    potential, forces, _ = pl.pallas_call(
        finish,
        out_shape=(
            jax.ShapeDtypeStruct((BX, BY, BZ), jnp.float32),
            jax.ShapeDtypeStruct((3, 1, A_DEV), jnp.float32),
            pltpu.VMEM((PX, PY, PZ), jnp.float32),
        ),
        in_specs=[VMEM, VMEM, HBM, HBM, VMEM],
        out_specs=(HBM, VMEM, VMEM),
        input_output_aliases={4: 2},
        scratch_shapes=[
            pltpu.VMEM((48, WIDE), jnp.float32),
            pltpu.VMEM((3, FX * FY, PZ), jnp.bfloat16),
            pltpu.VMEM((8, MERGED), jnp.float32),
            pltpu.VMEM((8, A_DEV + SPAN), jnp.float32),
            pltpu.VMEM((1, A_DEV), jnp.float32),
            pltpu.VMEM((3, 1, A_DEV), jnp.int32),
            pltpu.SemaphoreType.DMA((3,)),
        ],
        compiler_params=pltpu.CompilerParams(vmem_limit_bytes=LIMIT),
    )(lists, own, charge, cells, grid)
    return potential, forces


def local(charges, cells, counts):
    charge = charges.reshape(1, A_DEV)
    cells = cells.reshape(3, 1, A_DEV)
    counts = counts.reshape(1)
    first, second = call_compact(counts, charge, cells)
    own = call_arrange(counts, charge, cells)[None]
    first, second = swaps(first[None], second[None], "gz")
    atoms = jnp.concatenate([first, own, second], axis=0)
    first, second = swaps(atoms, atoms, "gx")
    atoms = jnp.concatenate([first, atoms, second], axis=0)
    first, second = swaps(atoms, atoms, "gy")
    grid = call_column(atoms)
    grid = call_slab(-1, second, grid)
    potential, forces = call_finish(first, own, charge, cells, grid)
    return potential, forces.reshape(1, 1, 1, 3, A_DEV)


def solution(mesh):
    in_specs = (P("gx", "gy", "gz", None), P("gx", "gy", "gz", None, None), P("gx", "gy", "gz"))
    out_specs = (P("gx", "gy", "gz"), P("gx", "gy", "gz", None, None))
    return jax.shard_map(local, mesh=mesh, in_specs=in_specs, out_specs=out_specs, check_vma=False)
```

```python
import functools
import math

import jax
import jax.numpy as jnp
from jax import lax
from jax.experimental import pallas as pl
from jax.experimental.pallas import tpu as pltpu
from jax.sharding import PartitionSpec as P

BX = 32
BY = 32
BZ = 384
A_DEV = 1024
PAD = 4
REACH = 4
WIDTH = A_DEV + 128
BLOCK = 256
SMALL = 128
WIDE = 2 * BLOCK

X0 = 5
Y0 = 8
PX = 42
PY = 48
PZ = 512
CHUNK = 14
FX = 40
FY = 40
FCHUNK = 20

kernel_width = 2.0
EXPONENT = -math.log2(math.e) / (2.0 * kernel_width * kernel_width)
SCALE = 1.3903614627339054
UNIT = math.sqrt(-EXPONENT)
LOW_END = 2 * PAD + 5
HIGH_START = BZ + PAD - 9
HIGH_START_Y = BY + PAD - 9
MIDDLE = BZ // 2
SPAN = A_DEV + 256 + WIDE
FRONT = 128
MERGED = 9 * A_DEV + SPAN + FRONT
ROWS = FCHUNK * FY


def weight(first, second, scale=1.0):
    away = first - second
    square = away * away
    value = jnp.exp2(math.log2(scale) - square)
    return jnp.where(square < (REACH + 0.5) ** 2 * UNIT * UNIT, value, 0.0)


def iota(shape, dim):
    return lax.broadcasted_iota(jnp.int32, shape, dim).astype(jnp.float32)


def toward(axis):
    return 1 - 2 * (lax.axis_index(axis) % 2)


def live_atoms(numbers, charges, cells):
    live = lax.broadcasted_iota(jnp.int32, (1, A_DEV), 1) < numbers[0]
    charge = jnp.where(live, charges[...], 0.0).astype(jnp.bfloat16).astype(jnp.float32)
    places = [jnp.where(live, cells[i], 0) for i in range(3)]
    rows = [charge] + [place.astype(jnp.float32) for place in places[:2]]
    rows.append((places[2] - MIDDLE).astype(jnp.float32))
    rows.append(jnp.zeros((4, A_DEV), jnp.float32))
    return live, places, jnp.concatenate(rows, axis=0).astype(jnp.bfloat16)


def running_sums(masks):
    rows = [jnp.where(mask, 1.0, 0.0) for mask in masks]
    rows.append(jnp.zeros((8 - len(masks), A_DEV), jnp.float32))
    near = jnp.concatenate(rows, axis=0)
    parts = A_DEV // 128
    chunks = jnp.concatenate([near[:, 128 * c : 128 * c + 128] for c in range(parts)], axis=0)
    upto = jnp.where(iota((128, 128), 0) <= iota((128, 128), 1), 1.0, 0.0)
    ahead = jnp.where(iota((A_DEV, 128), 0) < iota((A_DEV, 128), 1) * 128.0, 1.0, 0.0)
    within = jnp.dot(
        chunks.astype(jnp.bfloat16),
        upto.astype(jnp.bfloat16),
        preferred_element_type=jnp.float32,
    )
    before = jnp.dot(
        near.astype(jnp.bfloat16),
        ahead.astype(jnp.bfloat16),
        preferred_element_type=jnp.float32,
    )
    sums = [within[8 * c : 8 * c + 8] + before[:, c : c + 1] for c in range(parts)]
    return jnp.concatenate(sums, axis=1), near


def pick(rows, spot, start, size):
    want = iota((size, A_DEV), 0) + start.astype(jnp.float32)
    hot = jnp.where(want == spot, 1.0, 0.0).astype(jnp.bfloat16)
    return lax.dot_general(
        rows, hot, (((1,), (1,)), ((), ())), preferred_element_type=jnp.float32
    )


def compact(numbers, charges, cells, first, second, lists):
    live, places, rows = live_atoms(numbers, charges, cells)
    depth = places[2]
    sums, near = running_sums([live & (depth < LOW_END), live & (depth >= HIGH_START)])
    totals = sums[:, A_DEV - 1 : A_DEV]
    spot = jnp.where(near > 0.5, sums - 1.0, -1.0)
    steps = (jnp.max(totals).astype(jnp.int32) + SMALL - 1) // SMALL
    for side in range(2):
        lists[side, :, 0:A_DEV] = jnp.zeros((4, A_DEV), jnp.float32)
        lists[side, :, A_DEV:WIDTH] = jnp.broadcast_to(
            totals[side : side + 1], (4, WIDTH - A_DEV)
        )

    def window(k, _):
        cols = pl.ds(pl.multiple_of(k * SMALL, SMALL), SMALL)
        for side in range(2):
            moved = pick(rows, spot[side : side + 1], k * SMALL, SMALL)
            lists[side, 0:3, cols] = moved[0:3]
            lists[side, 3:4, cols] = moved[3:4] + float(MIDDLE)
        return 0

    window(jnp.int32(0), 0)
    lax.fori_loop(1, steps, window, 0)
    odd = lax.axis_index("gz") % 2
    first[...] = lists[1 - odd]
    second[...] = lists[odd]


def arrange(numbers, charges, cells, own):
    live, places, rows = live_atoms(numbers, charges, cells)
    high = live & (places[1] >= HIGH_START_Y)
    low = live & (places[1] < LOW_END)
    sums, near = running_sums([high, low, live])
    totals = sums[:, A_DEV - 1 : A_DEV]
    middle_at = totals[0:1] - 1.0
    low_at = totals[2:3] - totals[1:2] - 1.0
    spot = jnp.where(low, low_at + sums[1:2], middle_at + sums[2:3] - sums[0:1] - sums[1:2])
    spot = jnp.where(high, sums[0:1] - 1.0, spot)
    spot = jnp.where(live, spot, -1.0)
    own[:, 0:A_DEV] = jnp.zeros((4, A_DEV), jnp.float32)
    for row, total in enumerate((2, 0, 1, 2)):
        own[row : row + 1, A_DEV:WIDTH] = jnp.broadcast_to(
            totals[total : total + 1], (1, WIDTH - A_DEV)
        )

    def window(k, _):
        cols = pl.ds(pl.multiple_of(k * BLOCK, BLOCK), BLOCK)
        moved = pick(rows, spot, k * BLOCK, BLOCK)
        own[0:3, cols] = moved[0:3]
        own[3:4, cols] = moved[3:4] + float(MIDDLE)
        return 0

    lax.fori_loop(0, (numbers[0] + BLOCK - 1) // BLOCK, window, 0)


def append(ref, brick, start, number, offset, dx, dy, dz, merged, padded):
    moved = (X0 - PAD + BX * dx, Y0 - PAD + BY * dy, BZ * dz - PAD)
    padded[0:1, 0:A_DEV] = ref[brick, 0:1, 0:A_DEV]
    for i in range(3):
        place = ref[brick, 1 + i : 2 + i, 0:A_DEV] + jnp.float32(moved[i])
        padded[1 + i : 2 + i, 0:A_DEV] = place * UNIT
    skip = start % 128
    atoms = padded[:, pl.ds(pl.multiple_of(start - skip, 128), SPAN)]
    lanes = lax.broadcasted_iota(jnp.int32, (8, SPAN), 1)
    atoms = jnp.where((lanes >= skip) & (lanes < skip + number), atoms, 0.0)
    room = offset % 128
    back = jnp.where(room >= skip, 0, 128)
    atoms = pltpu.roll(atoms, room - skip + back, 1)
    base = pl.multiple_of(FRONT + offset - room - back, 128)
    merged[:, pl.ds(base, 256)] += atoms[:, 0:256]
    merged[:, pl.ds(base + 256, SPAN - 256)] = atoms[:, 256:SPAN]
    return offset + number


def spread(merged, start, size, x0, nx, y0, ny, grid, rows_x, first, row0):
    cols = pl.ds(pl.multiple_of(start + FRONT, 128), size)
    charge = merged[0:1, cols]
    xa = merged[1:2, cols]
    ya = merged[2:3, cols]
    za = merged[3:4, cols]
    gy = weight((iota((ny, size), 0) + jnp.float32(y0)) * UNIT, ya) * (charge * (1.0 / SCALE))
    zi = iota((PZ, size), 0)
    zi = jnp.where(zi < 448.0, zi, zi - float(PZ)) * UNIT
    right = weight(zi, za, SCALE).astype(jnp.bfloat16)
    rows_x[:, 0:size] = weight(iota((48, size), 0) * UNIT, xa)
    chunk = min(nx, CHUNK * PY // ny)
    for c in range(0, nx, chunk):
        at = x0 + c
        left = jnp.stack(
            [rows_x[pl.ds(at + i, 1), 0:size] * gy for i in range(chunk)], axis=0
        )
        left = left.reshape(chunk * ny, size).astype(jnp.bfloat16)
        part = lax.dot_general(
            left, right, (((1,), (1,)), ((), ())), preferred_element_type=jnp.float32
        )
        part = part.reshape(chunk, ny, PZ)
        if first:
            grid[pl.ds(at, chunk), pl.ds(row0, ny), :] = part
        else:
            grid[pl.ds(at, chunk), pl.ds(row0, ny), :] += part


def spread_all(merged, total, x0, nx, y0, ny, grid, rows_x, clear, row0):
    rest = total % WIDE
    wide = total // WIDE + (rest > BLOCK).astype(jnp.int32)
    if clear:
        wide = jnp.maximum(wide, 1)
        spread(merged, 0, WIDE, x0, nx, y0, ny, grid, rows_x, True, row0)

    def block(k, _):
        spread(merged, k * WIDE, WIDE, x0, nx, y0, ny, grid, rows_x, False, row0)
        return 0

    lax.fori_loop(1 if clear else 0, wide, block, 0)

    @pl.when(total > wide * WIDE)
    def _():
        spread(merged, wide * WIDE, BLOCK, x0, nx, y0, ny, grid, rows_x, False, row0)


def number_of(ref, brick, row):
    return ref[brick, row : row + 1, A_DEV:WIDTH][0, 0].astype(jnp.int32)


def gather(ref, bricks, side, merged, padded):
    merged[:, 0 : FRONT + 256] = jnp.zeros((8, FRONT + 256), jnp.float32)
    offset = jnp.int32(0)
    for brick, (dx, dy, dz) in bricks:
        number = number_of(ref, brick, 0)
        start = jnp.int32(0)
        if side is not None:
            low = number_of(ref, brick, 2)
            start = jnp.where(side > 0, number - low, 0)
            number = jnp.where(side > 0, low, number_of(ref, brick, 1))
        offset = append(ref, brick, start, number, offset, dx, dy, dz, merged, padded)
    return offset


def slots_of(axis):
    step = toward(axis)
    return (step, 0, -step)


def inner(lists, grid, rows_x, merged, padded):
    padded[...] = jnp.zeros_like(padded)
    zs = slots_of("gz")
    total = gather(lists, [(j, (0, 0, zs[j])) for j in (1, 0, 2)], None, merged, padded)
    spread_all(merged, total, 0, PX, 0, PY, grid, rows_x, True, 0)


def column(
    lists, cells, before, grid, potential, found, rows_x, fields, merged, padded, place, sems
):
    fetch = pltpu.make_async_copy(cells, place, sems.at[0])
    fetch.start()
    padded[...] = jnp.zeros_like(padded)
    xs, zs = slots_of("gx"), slots_of("gz")
    for i in (0, 2):
        total = gather(
            lists, [(3 * i + j, (xs[i], 0, zs[j])) for j in range(3)], None, merged, padded
        )
        x0 = jnp.where(xs[i] > 0, 28, 0)
        spread_all(merged, total, x0, 14, 0, PY, grid, rows_x, False, 0)
    copy = pltpu.make_async_copy(
        grid.at[X0 : X0 + BX, 16:32, 0:BZ], potential.at[:, 8:24, :], sems.at[1]
    )
    copy.start()
    found[...] = jnp.zeros_like(found)
    count = number_of(lists, 4, 0)
    fetch.wait()

    def build(c):
        gx, gy, gz = [], [], []
        for x in range(c * FCHUNK, (c + 1) * FCHUNK):
            gx.append(grid[x + 2, 4:44, :] - grid[x, 4:44, :])
            gy.append(grid[x + 1, 5:45, :] - grid[x + 1, 3:43, :])
            mid = grid[x + 1, 4:44, :]
            gz.append(pltpu.roll(mid, PZ - 2, 1) - mid)
        for d, parts in enumerate((gx, gy, gz)):
            both = jnp.stack(parts, axis=0).reshape(ROWS, PZ).astype(jnp.bfloat16)
            fields[d, c * ROWS : (c + 1) * ROWS, :] = both

    def sample(start, fresh):
        cols = pl.ds(pl.multiple_of(start, WIDE), WIDE)
        xa, ya, za = atom_cells(place, cols)
        zi = depths(WIDE)
        depth = jnp.where(zi == za, 1.0, 0.0).astype(jnp.bfloat16)
        below = jnp.where(zi == za - 1.0, 1.0, 0.0).astype(jnp.bfloat16)
        sums = [jnp.zeros((FY, WIDE), jnp.float32)] * 3
        for c in range(FX // FCHUNK):
            if fresh:
                build(c)
            for d in range(3):
                part = jnp.dot(
                    fields[d, c * ROWS : (c + 1) * ROWS, :],
                    below if d == 2 else depth,
                    preferred_element_type=jnp.float32,
                ).reshape(FCHUNK, FY, WIDE)
                for i in range(FCHUNK):
                    hot_x = xa == float(c * FCHUNK + i)
                    sums[d] = sums[d] + jnp.where(hot_x, part[i], 0.0)
        hot_y = iota((FY, WIDE), 0) == ya
        for d in range(3):
            value = jnp.sum(jnp.where(hot_y, sums[d], 0.0), axis=0, keepdims=True)
            found[d : d + 1, cols] = value

    sample(0, True)

    def more(k, _):
        sample(k * WIDE, False)
        return 0

    lax.fori_loop(1, (count + WIDE - 1) // WIDE, more, 0)
    copy.wait()


def atom_cells(place, cols):
    xa = place[0, :, cols].astype(jnp.float32)
    ya = place[1, :, cols].astype(jnp.float32)
    return xa, ya, (place[2, :, cols] - PAD).astype(jnp.float32)


def depths(size):
    zi = iota((PZ, size), 0)
    return jnp.where(zi < 448.0, zi, zi - float(PZ))


def slab(turn, lists, own, grid, found, potential, place, part, stage, rows_x, merged, padded, fetch, sem):
    padded[...] = jnp.zeros_like(padded)
    xs, zs = slots_of("gx"), slots_of("gz")
    dy = toward("gy") * turn
    total = gather(
        lists,
        [(3 * m + j, (xs[m], dy, zs[j])) for m in range(3) for j in range(3)],
        dy,
        merged,
        padded,
    )
    y0 = pl.multiple_of(jnp.where(dy > 0, 32, 0), 8)
    spread_all(merged, total, 0, PX, y0, 16, part, rows_x, True, 0)
    at = pl.multiple_of(jnp.where(dy > 0, 0, 8), 8)
    stage[...] = (
        part[X0 : X0 + BX, pl.ds(at, 8), 0:BZ] + grid[X0 : X0 + BX, pl.ds(y0 + at, 8), 0:BZ]
    )
    row = pl.multiple_of(jnp.where(dy > 0, 24, 0), 8)
    copy = pltpu.make_async_copy(stage, potential.at[:, pl.ds(row, 8), :], sem)
    copy.start()
    fetch.wait()
    count = number_of(own, 0, 0)

    def block(k, _):
        cols = pl.ds(pl.multiple_of(k * WIDE, WIDE), WIDE)
        xa, ya, za = atom_cells(place, cols)
        zi = depths(WIDE)
        here = jnp.where(zi == za, 1.0, 0.0).astype(jnp.bfloat16)
        slope = jnp.where(zi == za + 1.0, 1.0, 0.0) - jnp.where(zi == za - 1.0, 1.0, 0.0)
        rows = part[...].reshape(PX * 16, PZ).astype(jnp.bfloat16)
        value = jnp.dot(rows, here, preferred_element_type=jnp.float32)
        value = value.reshape(PX, 16, WIDE)
        change = jnp.dot(rows, slope.astype(jnp.bfloat16), preferred_element_type=jnp.float32)
        change = change.reshape(PX, 16, WIDE)
        level = jnp.zeros((16, WIDE), jnp.float32)
        along_x = level
        along_z = level
        for x in range(PX):
            at_x = xa == float(x - 1)
            level = level + jnp.where(at_x, value[x], 0.0)
            along_z = along_z + jnp.where(at_x, change[x], 0.0)
            side = jnp.where(xa == float(x - 2), 1.0, 0.0) - jnp.where(xa == float(x), 1.0, 0.0)
            along_x = along_x + side * value[x]
        away = iota((16, WIDE), 0) + (y0.astype(jnp.float32) - float(Y0 - PAD)) - ya
        at_y = away == 0.0
        fx = jnp.where(at_y, along_x, 0.0)
        fy = jnp.where(away == 1.0, level, 0.0) - jnp.where(away == -1.0, level, 0.0)
        fz = jnp.where(at_y, along_z, 0.0)
        for d, value in enumerate((fx, fy, fz)):
            found[d : d + 1, cols] += jnp.sum(value, axis=0, keepdims=True)
        return 0

    lax.fori_loop(0, (count + WIDE - 1) // WIDE, block, 0)
    copy.wait()
    return count


def add_slab(
    turn, lists, own, cells, grid, found_in, potential_in, found, potential,
    part, stage, rows_x, merged, padded, place, sems,
):
    fetch = pltpu.make_async_copy(cells, place, sems.at[0])
    fetch.start()
    slab(
        turn, lists, own, grid, found, potential, place, part, stage,
        rows_x, merged, padded, fetch, sems.at[1],
    )


def finish(
    turn, lists, own, cells, grid, found_in, potential_in, charges, found, potential, forces,
    part, stage, rows_x, merged, padded, place, sems, charge,
):
    fetch = pltpu.make_async_copy(cells, place, sems.at[0])
    fetch.start()
    fetch_charge = pltpu.make_async_copy(charges, charge, sems.at[2])
    fetch_charge.start()
    count = slab(
        turn, lists, own, grid, found, potential, place, part, stage,
        rows_x, merged, padded, fetch, sems.at[1],
    )
    fetch_charge.wait()
    slots = lax.broadcasted_iota(jnp.int32, (1, A_DEV), 1)
    for d in range(3):
        forces[d] = jnp.where(slots < count, found[d : d + 1] * (-0.5 * charge[...]), 0.0)


def swaps(block, other, axis):
    size = lax.axis_size(axis)
    first = [(i, i ^ 1) for i in range(size)]
    second = [(i, (i + 1 if i % 2 else i - 1) % size) for i in range(size)]
    return lax.ppermute(block, axis, first), lax.ppermute(other, axis, second)


VMEM = pl.BlockSpec(memory_space=pltpu.VMEM)
HBM = pl.BlockSpec(memory_space=pl.ANY)
LIMIT = 40 * 1024 * 1024


def call_compact(counts, charge, cells):
    shape = pltpu.VMEM((4, WIDTH), jnp.float32)
    return pl.pallas_call(
        compact,
        out_shape=(shape, shape),
        in_specs=[pl.BlockSpec(memory_space=pltpu.SMEM), VMEM, VMEM],
        out_specs=(VMEM,) * 2,
        scratch_shapes=[pltpu.VMEM((2, 4, WIDTH), jnp.float32)],
    )(counts, charge, cells)


def call_arrange(counts, charge, cells):
    return pl.pallas_call(
        arrange,
        out_shape=pltpu.VMEM((4, WIDTH), jnp.float32),
        in_specs=[pl.BlockSpec(memory_space=pltpu.SMEM), VMEM, VMEM],
        out_specs=VMEM,
        cost_estimate=pl.CostEstimate(flops=2 * 10**9, bytes_accessed=10**5, transcendentals=0),
    )(counts, charge, cells)


GRID = pltpu.VMEM((PX, PY, PZ), jnp.float32)
FOUND = pltpu.VMEM((8, A_DEV), jnp.float32)
ROWS_X = pltpu.VMEM((48, WIDE), jnp.float32)
LISTS = [
    pltpu.VMEM((8, MERGED), jnp.float32),
    pltpu.VMEM((8, A_DEV + SPAN), jnp.float32),
]
PLACE = pltpu.VMEM((3, 1, A_DEV), jnp.int32)
PARAMS = pltpu.CompilerParams(vmem_limit_bytes=LIMIT)


def cost(flops):
    return pl.CostEstimate(flops=flops, bytes_accessed=10**6, transcendentals=0)


def call_inner(lists):
    return pl.pallas_call(
        inner,
        out_shape=GRID,
        in_specs=[VMEM],
        out_specs=VMEM,
        scratch_shapes=[ROWS_X] + LISTS,
        compiler_params=PARAMS,
        cost_estimate=cost(2 * 10**9),
    )(lists)


def call_column(lists, cells, grid):
    return pl.pallas_call(
        column,
        out_shape=(GRID, jax.ShapeDtypeStruct((BX, BY, BZ), jnp.float32), FOUND),
        in_specs=[VMEM, HBM, VMEM],
        out_specs=(VMEM, HBM, VMEM),
        input_output_aliases={2: 0},
        scratch_shapes=[ROWS_X, pltpu.VMEM((3, FX * FY, PZ), jnp.bfloat16)]
        + LISTS
        + [PLACE, pltpu.SemaphoreType.DMA((2,))],
        compiler_params=PARAMS,
        cost_estimate=cost(6 * 10**9),
    )(lists, cells, grid)


def slab_scratch():
    return (
        [
            pltpu.VMEM((PX, 16, PZ), jnp.float32),
            pltpu.VMEM((BX, 8, BZ), jnp.float32),
            ROWS_X,
        ]
        + LISTS
        + [PLACE, pltpu.SemaphoreType.DMA((3,))]
    )


def call_slab(turn, lists, own, cells, grid, found, potential):
    return pl.pallas_call(
        functools.partial(add_slab, turn),
        out_shape=(FOUND, jax.ShapeDtypeStruct((BX, BY, BZ), jnp.float32)),
        in_specs=[VMEM, VMEM, HBM, VMEM, VMEM, HBM],
        out_specs=(VMEM, HBM),
        input_output_aliases={4: 0, 5: 1},
        scratch_shapes=slab_scratch(),
        compiler_params=PARAMS,
        cost_estimate=cost(10**9),
    )(lists, own, cells, grid, found, potential)


def call_finish(turn, lists, own, cells, grid, found, potential, charge):
    _, potential, forces = pl.pallas_call(
        functools.partial(finish, turn),
        out_shape=(
            FOUND,
            jax.ShapeDtypeStruct((BX, BY, BZ), jnp.float32),
            jax.ShapeDtypeStruct((3, 1, A_DEV), jnp.float32),
        ),
        in_specs=[VMEM, VMEM, HBM, VMEM, VMEM, HBM, HBM],
        out_specs=(VMEM, HBM, VMEM),
        input_output_aliases={4: 0, 5: 1},
        scratch_shapes=slab_scratch() + [pltpu.VMEM((1, A_DEV), jnp.float32)],
        compiler_params=PARAMS,
        cost_estimate=cost(10**9),
    )(lists, own, cells, grid, found, potential, charge)
    return potential, forces


def local(charges, cells, counts):
    charge = charges.reshape(1, A_DEV)
    cells = cells.reshape(3, 1, A_DEV)
    counts = counts.reshape(1)
    first, second = call_compact(counts, charge, cells)
    own = call_arrange(counts, charge, cells)[None]
    first, second = swaps(first[None], second[None], "gz")
    atoms = jnp.concatenate([first, own, second], axis=0)
    first, second = swaps(atoms, atoms, "gx")
    grid = call_inner(atoms)
    atoms = jnp.concatenate([first, atoms, second], axis=0)
    first, second = swaps(atoms, atoms, "gy")
    grid, potential, found = call_column(atoms, cells, grid)
    found, potential = call_slab(-1, second, own, cells, grid, found, potential)
    potential, forces = call_finish(1, first, own, cells, grid, found, potential, charge)
    return potential, forces.reshape(1, 1, 1, 3, A_DEV)


def solution(mesh):
    in_specs = (P("gx", "gy", "gz", None), P("gx", "gy", "gz", None, None), P("gx", "gy", "gz"))
    out_specs = (P("gx", "gy", "gz"), P("gx", "gy", "gz", None, None))
    return jax.shard_map(local, mesh=mesh, in_specs=in_specs, out_specs=out_specs, check_vma=False)
```

```python
import math

import jax
import jax.numpy as jnp
from jax import lax
from jax.experimental import pallas as pl
from jax.experimental.pallas import tpu as pltpu
from jax.sharding import PartitionSpec as P

BX = 32
BY = 32
BZ = 384
A_DEV = 1024
PAD = 4
REACH = 4
WIDTH = A_DEV + 128
BLOCK = 256
SMALL = 128
WIDE = 2 * BLOCK

X0 = 5
Y0 = 8
PX = 42
PY = 48
PZ = 512
CHUNK = 14
FX = 40
FY = 40
FCHUNK = 20

kernel_width = 2.0
EXPONENT = -math.log2(math.e) / (2.0 * kernel_width * kernel_width)
SCALE = 1.3903614627339054
UNIT = math.sqrt(-EXPONENT)
LOW_END = 2 * PAD + 5
HIGH_START = BZ + PAD - 9
HIGH_START_Y = BY + PAD - 9
MIDDLE = BZ // 2
SPAN = A_DEV + 256 + WIDE
FRONT = 128
MERGED = 9 * A_DEV + SPAN + FRONT
ROWS = FCHUNK * FY


def weight(first, second, scale=1.0):
    away = first - second
    square = away * away
    value = jnp.exp2(math.log2(scale) - square)
    return jnp.where(square < (REACH + 0.5) ** 2 * UNIT * UNIT, value, 0.0)


def iota(shape, dim):
    return lax.broadcasted_iota(jnp.int32, shape, dim).astype(jnp.float32)


def toward(axis):
    return 1 - 2 * (lax.axis_index(axis) % 2)


def live_atoms(numbers, charges, cells):
    live = lax.broadcasted_iota(jnp.int32, (1, A_DEV), 1) < numbers[0]
    charge = jnp.where(live, charges[...], 0.0).astype(jnp.bfloat16).astype(jnp.float32)
    places = [jnp.where(live, cells[i], 0) for i in range(3)]
    rows = [charge] + [place.astype(jnp.float32) for place in places[:2]]
    rows.append((places[2] - MIDDLE).astype(jnp.float32))
    rows.append(jnp.zeros((4, A_DEV), jnp.float32))
    return live, places, jnp.concatenate(rows, axis=0).astype(jnp.bfloat16)


def running_sums(masks):
    rows = [jnp.where(mask, 1.0, 0.0) for mask in masks]
    rows.append(jnp.zeros((8 - len(masks), A_DEV), jnp.float32))
    near = jnp.concatenate(rows, axis=0)
    parts = A_DEV // 128
    chunks = jnp.concatenate([near[:, 128 * c : 128 * c + 128] for c in range(parts)], axis=0)
    upto = jnp.where(iota((128, 128), 0) <= iota((128, 128), 1), 1.0, 0.0)
    ahead = jnp.where(iota((A_DEV, 128), 0) < iota((A_DEV, 128), 1) * 128.0, 1.0, 0.0)
    within = jnp.dot(
        chunks.astype(jnp.bfloat16),
        upto.astype(jnp.bfloat16),
        preferred_element_type=jnp.float32,
    )
    before = jnp.dot(
        near.astype(jnp.bfloat16),
        ahead.astype(jnp.bfloat16),
        preferred_element_type=jnp.float32,
    )
    sums = [within[8 * c : 8 * c + 8] + before[:, c : c + 1] for c in range(parts)]
    return jnp.concatenate(sums, axis=1), near


def pick(rows, spot, start, size):
    want = iota((size, A_DEV), 0) + start.astype(jnp.float32)
    hot = jnp.where(want == spot, 1.0, 0.0).astype(jnp.bfloat16)
    return lax.dot_general(
        rows, hot, (((1,), (1,)), ((), ())), preferred_element_type=jnp.float32
    )


def compact(numbers, charges, cells, first, second, lists):
    live, places, rows = live_atoms(numbers, charges, cells)
    depth = places[2]
    sums, near = running_sums([live & (depth < LOW_END), live & (depth >= HIGH_START)])
    totals = sums[:, A_DEV - 1 : A_DEV]
    spot = jnp.where(near > 0.5, sums - 1.0, -1.0)
    steps = (jnp.max(totals).astype(jnp.int32) + SMALL - 1) // SMALL
    for side in range(2):
        lists[side, :, 0:A_DEV] = jnp.zeros((4, A_DEV), jnp.float32)
        lists[side, :, A_DEV:WIDTH] = jnp.broadcast_to(
            totals[side : side + 1], (4, WIDTH - A_DEV)
        )

    def window(k, _):
        cols = pl.ds(pl.multiple_of(k * SMALL, SMALL), SMALL)
        for side in range(2):
            moved = pick(rows, spot[side : side + 1], k * SMALL, SMALL)
            lists[side, 0:3, cols] = moved[0:3]
            lists[side, 3:4, cols] = moved[3:4] + float(MIDDLE)
        return 0

    window(jnp.int32(0), 0)
    lax.fori_loop(1, steps, window, 0)
    odd = lax.axis_index("gz") % 2
    first[...] = lists[1 - odd]
    second[...] = lists[odd]


def arrange(numbers, charges, cells, own):
    live, places, rows = live_atoms(numbers, charges, cells)
    high = live & (places[1] >= HIGH_START_Y)
    low = live & (places[1] < LOW_END)
    sums, near = running_sums([high, low, live])
    totals = sums[:, A_DEV - 1 : A_DEV]
    middle_at = totals[0:1] - 1.0
    low_at = totals[2:3] - totals[1:2] - 1.0
    spot = jnp.where(low, low_at + sums[1:2], middle_at + sums[2:3] - sums[0:1] - sums[1:2])
    spot = jnp.where(high, sums[0:1] - 1.0, spot)
    spot = jnp.where(live, spot, -1.0)
    own[:, 0:A_DEV] = jnp.zeros((4, A_DEV), jnp.float32)
    for row, total in enumerate((2, 0, 1, 2)):
        own[row : row + 1, A_DEV:WIDTH] = jnp.broadcast_to(
            totals[total : total + 1], (1, WIDTH - A_DEV)
        )

    def window(k, _):
        cols = pl.ds(pl.multiple_of(k * BLOCK, BLOCK), BLOCK)
        moved = pick(rows, spot, k * BLOCK, BLOCK)
        own[0:3, cols] = moved[0:3]
        own[3:4, cols] = moved[3:4] + float(MIDDLE)
        return 0

    lax.fori_loop(0, (numbers[0] + BLOCK - 1) // BLOCK, window, 0)


def append(ref, brick, start, number, offset, dx, dy, dz, merged, padded):
    row = lax.broadcasted_iota(jnp.int32, (4, 128), 0)
    moved = jnp.where(row == 1, jnp.float32(X0 - PAD + BX * dx), 0.0)
    moved = jnp.where(row == 2, jnp.float32(Y0 - PAD + BY * dy), moved)
    moved = jnp.where(row == 3, jnp.float32(BZ * dz - PAD), moved)
    unit = jnp.where(row == 0, 1.0, UNIT)
    for c in range(0, A_DEV, 128):
        padded[0:4, c : c + 128] = (ref[brick, :, c : c + 128] + moved) * unit
    skip = start % 128
    atoms = padded[:, pl.ds(pl.multiple_of(start - skip, 128), SPAN)]
    lanes = lax.broadcasted_iota(jnp.int32, (8, SPAN), 1)
    atoms = jnp.where((lanes >= skip) & (lanes < skip + number), atoms, 0.0)
    room = offset % 128
    back = jnp.where(room >= skip, 0, 128)
    atoms = pltpu.roll(atoms, room - skip + back, 1)
    base = pl.multiple_of(FRONT + offset - room - back, 128)
    merged[:, pl.ds(base, 256)] += atoms[:, 0:256]
    merged[:, pl.ds(base + 256, SPAN - 256)] = atoms[:, 256:SPAN]
    return offset + number


def spread(merged, start, size, x0, nx, y0, ny, grid, rows_x, first, row0):
    cols = pl.ds(pl.multiple_of(start + FRONT, 128), size)
    charge = merged[0:1, cols]
    xa = merged[1:2, cols]
    ya = merged[2:3, cols]
    za = merged[3:4, cols]
    gy = weight((iota((ny, size), 0) + jnp.float32(y0)) * UNIT, ya) * (charge * (1.0 / SCALE))
    zi = iota((PZ, size), 0)
    zi = jnp.where(zi < 448.0, zi, zi - float(PZ)) * UNIT
    right = weight(zi, za, SCALE).astype(jnp.bfloat16)
    rows_x[:, 0:size] = weight(iota((48, size), 0) * UNIT, xa)
    chunk = min(nx, CHUNK * PY // ny)
    for c in range(0, nx, chunk):
        at = x0 + c
        left = jnp.stack(
            [rows_x[pl.ds(at + i, 1), 0:size] * gy for i in range(chunk)], axis=0
        )
        left = left.reshape(chunk * ny, size).astype(jnp.bfloat16)
        part = lax.dot_general(
            left, right, (((1,), (1,)), ((), ())), preferred_element_type=jnp.float32
        )
        part = part.reshape(chunk, ny, PZ)
        if first:
            grid[pl.ds(at, chunk), pl.ds(row0, ny), :] = part
        else:
            grid[pl.ds(at, chunk), pl.ds(row0, ny), :] += part


def spread_all(merged, total, x0, nx, y0, ny, grid, rows_x, clear, row0):
    rest = total % WIDE
    wide = total // WIDE + (rest > BLOCK).astype(jnp.int32)
    if clear:
        wide = jnp.maximum(wide, 1)
        spread(merged, 0, WIDE, x0, nx, y0, ny, grid, rows_x, True, row0)

    def block(k, _):
        spread(merged, k * WIDE, WIDE, x0, nx, y0, ny, grid, rows_x, False, row0)
        return 0

    lax.fori_loop(1 if clear else 0, wide, block, 0)

    @pl.when(total > wide * WIDE)
    def _():
        spread(merged, wide * WIDE, BLOCK, x0, nx, y0, ny, grid, rows_x, False, row0)


def number_of(ref, brick, row):
    return ref[brick, row : row + 1, A_DEV:WIDTH][0, 0].astype(jnp.int32)


def gather(ref, bricks, side, merged, padded):
    merged[:, 0 : FRONT + 256] = jnp.zeros((8, FRONT + 256), jnp.float32)
    offset = jnp.int32(0)
    for brick, (dx, dy, dz) in bricks:
        number = number_of(ref, brick, 0)
        start = jnp.int32(0)
        if side is not None:
            low = number_of(ref, brick, 2)
            start = jnp.where(side > 0, number - low, 0)
            number = jnp.where(side > 0, low, number_of(ref, brick, 1))
        offset = append(ref, brick, start, number, offset, dx, dy, dz, merged, padded)
    return offset


def slots_of(axis):
    step = toward(axis)
    return (step, 0, -step)


def inner(lists, grid, rows_x, merged, padded):
    padded[...] = jnp.zeros_like(padded)
    zs = slots_of("gz")
    total = gather(lists, [(j, (0, 0, zs[j])) for j in (1, 0, 2)], None, merged, padded)
    spread_all(merged, total, 0, PX, 0, PY, grid, rows_x, True, 0)


def column(
    lists, place, before, grid, potential, found, rows_x, fields, merged, padded, sem
):
    padded[...] = jnp.zeros_like(padded)
    xs, zs = slots_of("gx"), slots_of("gz")
    for i in (0, 2):
        total = gather(
            lists, [(3 * i + j, (xs[i], 0, zs[j])) for j in range(3)], None, merged, padded
        )
        x0 = jnp.where(xs[i] > 0, 28, 0)
        spread_all(merged, total, x0, 14, 0, PY, grid, rows_x, False, 0)
    copy = pltpu.make_async_copy(
        grid.at[X0 : X0 + BX, 16:32, 0:BZ], potential.at[:, 8:24, :], sem
    )
    copy.start()
    found[...] = jnp.zeros_like(found)
    count = number_of(lists, 4, 0)

    def build(c):
        gx, gy, gz = [], [], []
        for x in range(c * FCHUNK, (c + 1) * FCHUNK):
            gx.append(grid[x + 2, 4:44, :] - grid[x, 4:44, :])
            gy.append(grid[x + 1, 5:45, :] - grid[x + 1, 3:43, :])
            mid = grid[x + 1, 4:44, :]
            gz.append(pltpu.roll(mid, PZ - 2, 1) - mid)
        for d, parts in enumerate((gx, gy, gz)):
            both = jnp.stack(parts, axis=0).reshape(ROWS, PZ).astype(jnp.bfloat16)
            fields[d, c * ROWS : (c + 1) * ROWS, :] = both

    def sample(start, fresh):
        cols = pl.ds(pl.multiple_of(start, WIDE), WIDE)
        xa, ya, za = atom_cells(place, cols)
        zi = depths(WIDE)
        depth = jnp.where(zi == za, 1.0, 0.0).astype(jnp.bfloat16)
        below = jnp.where(zi == za - 1.0, 1.0, 0.0).astype(jnp.bfloat16)
        sums = [jnp.zeros((FY, WIDE), jnp.float32)] * 3
        for c in range(FX // FCHUNK):
            if fresh:
                build(c)
            for d in range(3):
                part = jnp.dot(
                    fields[d, c * ROWS : (c + 1) * ROWS, :],
                    below if d == 2 else depth,
                    preferred_element_type=jnp.float32,
                ).reshape(FCHUNK, FY, WIDE)
                for i in range(FCHUNK):
                    hot_x = xa == float(c * FCHUNK + i)
                    sums[d] = sums[d] + jnp.where(hot_x, part[i], 0.0)
        hot_y = iota((FY, WIDE), 0) == ya
        for d in range(3):
            value = jnp.sum(jnp.where(hot_y, sums[d], 0.0), axis=0, keepdims=True)
            found[d : d + 1, cols] = value

    sample(0, True)

    def more(k, _):
        sample(k * WIDE, False)
        return 0

    lax.fori_loop(1, (count + WIDE - 1) // WIDE, more, 0)
    copy.wait()


def atom_cells(place, cols):
    xa = place[0, :, cols].astype(jnp.float32)
    ya = place[1, :, cols].astype(jnp.float32)
    return xa, ya, (place[2, :, cols] - PAD).astype(jnp.float32)


def depths(size):
    zi = iota((PZ, size), 0)
    return jnp.where(zi < 448.0, zi, zi - float(PZ))


def slab(turn, lists, grid, potential, part, stage, rows_x, merged, padded, sem):
    xs, zs = slots_of("gx"), slots_of("gz")
    dy = toward("gy") * turn
    total = gather(
        lists,
        [(3 * m + j, (xs[m], dy, zs[j])) for m in range(3) for j in range(3)],
        dy,
        merged,
        padded,
    )
    y0 = pl.multiple_of(jnp.where(dy > 0, 32, 0), 8)
    spread_all(merged, total, 0, PX, y0, 16, part, rows_x, True, 0)
    at = pl.multiple_of(jnp.where(dy > 0, 0, 8), 8)
    stage[...] = (
        part[X0 : X0 + BX, pl.ds(at, 8), 0:BZ] + grid[X0 : X0 + BX, pl.ds(y0 + at, 8), 0:BZ]
    )
    row = pl.multiple_of(jnp.where(dy > 0, 24, 0), 8)
    copy = pltpu.make_async_copy(stage, potential.at[:, pl.ds(row, 8), :], sem)
    copy.start()
    return y0, copy


def finish(
    near, far, own, place, charge, grid, found, potential_in, potential, forces,
    parts, stages, rows_x, merged, padded, sems,
):
    padded[...] = jnp.zeros_like(padded)
    slabs = [
        slab(
            1 - 2 * i, lists, grid, potential, parts.at[i], stages.at[i],
            rows_x, merged, padded, sems.at[i],
        )
        for i, lists in enumerate((near, far))
    ]
    count = number_of(own, 0, 0)
    forces[...] = jnp.zeros_like(forces)

    def block(k, _):
        cols = pl.ds(pl.multiple_of(k * WIDE, WIDE), WIDE)
        xa, ya, za = atom_cells(place, cols)
        zi = depths(WIDE)
        here = jnp.where(zi == za, 1.0, 0.0).astype(jnp.bfloat16)
        slope = jnp.where(zi == za + 1.0, 1.0, 0.0) - jnp.where(zi == za - 1.0, 1.0, 0.0)
        slope = slope.astype(jnp.bfloat16)
        sums = [found[d : d + 1, cols] for d in range(3)]
        for i, (y0, _) in enumerate(slabs):
            rows = parts[i].reshape(PX * 16, PZ).astype(jnp.bfloat16)
            value = jnp.dot(rows, here, preferred_element_type=jnp.float32)
            value = value.reshape(PX, 16, WIDE)
            change = jnp.dot(rows, slope, preferred_element_type=jnp.float32)
            change = change.reshape(PX, 16, WIDE)
            level = jnp.zeros((16, WIDE), jnp.float32)
            along_x = level
            along_z = level
            for x in range(PX):
                at_x = xa == float(x - 1)
                level = level + jnp.where(at_x, value[x], 0.0)
                along_z = along_z + jnp.where(at_x, change[x], 0.0)
                side = jnp.where(xa == float(x - 2), 1.0, 0.0)
                side = side - jnp.where(xa == float(x), 1.0, 0.0)
                along_x = along_x + side * value[x]
            away = iota((16, WIDE), 0) + (y0.astype(jnp.float32) - float(Y0 - PAD)) - ya
            at_y = away == 0.0
            fx = jnp.where(at_y, along_x, 0.0)
            fy = jnp.where(away == 1.0, level, 0.0) - jnp.where(away == -1.0, level, 0.0)
            fz = jnp.where(at_y, along_z, 0.0)
            for d, one in enumerate((fx, fy, fz)):
                sums[d] = sums[d] + jnp.sum(one, axis=0, keepdims=True)
        slots = lax.broadcasted_iota(jnp.int32, (1, WIDE), 1) + k * WIDE
        factor = -0.5 * charge[:, cols]
        for d in range(3):
            forces[d, :, cols] = jnp.where(slots < count, sums[d] * factor, 0.0)
        return 0

    lax.fori_loop(0, (count + WIDE - 1) // WIDE, block, 0)
    for _, copy in slabs:
        copy.wait()


def swaps(block, other, axis):
    size = lax.axis_size(axis)
    first = [(i, i ^ 1) for i in range(size)]
    second = [(i, (i + 1 if i % 2 else i - 1) % size) for i in range(size)]
    return lax.ppermute(block, axis, first), lax.ppermute(other, axis, second)


VMEM = pl.BlockSpec(memory_space=pltpu.VMEM)
HBM = pl.BlockSpec(memory_space=pl.ANY)
LIMIT = 40 * 1024 * 1024


def call_compact(counts, charge, cells):
    shape = pltpu.VMEM((4, WIDTH), jnp.float32)
    return pl.pallas_call(
        compact,
        out_shape=(shape, shape),
        in_specs=[pl.BlockSpec(memory_space=pltpu.SMEM), VMEM, VMEM],
        out_specs=(VMEM,) * 2,
        scratch_shapes=[pltpu.VMEM((2, 4, WIDTH), jnp.float32)],
    )(counts, charge, cells)


def call_arrange(counts, charge, cells):
    return pl.pallas_call(
        arrange,
        out_shape=pltpu.VMEM((4, WIDTH), jnp.float32),
        in_specs=[pl.BlockSpec(memory_space=pltpu.SMEM), VMEM, VMEM],
        out_specs=VMEM,
        cost_estimate=pl.CostEstimate(flops=2 * 10**9, bytes_accessed=10**5, transcendentals=0),
    )(counts, charge, cells)


GRID = pltpu.VMEM((PX, PY, PZ), jnp.float32)
FOUND = pltpu.VMEM((8, A_DEV), jnp.float32)
ROWS_X = pltpu.VMEM((48, WIDE), jnp.float32)
LISTS = [
    pltpu.VMEM((8, MERGED), jnp.float32),
    pltpu.VMEM((8, A_DEV + SPAN), jnp.float32),
]
PARAMS = pltpu.CompilerParams(vmem_limit_bytes=LIMIT)


def cost(flops):
    return pl.CostEstimate(flops=flops, bytes_accessed=10**6, transcendentals=0)


def call_inner(lists):
    return pl.pallas_call(
        inner,
        out_shape=GRID,
        in_specs=[VMEM],
        out_specs=VMEM,
        scratch_shapes=[ROWS_X] + LISTS,
        compiler_params=PARAMS,
        cost_estimate=cost(2 * 10**9),
    )(lists)


def call_column(lists, cells, grid):
    return pl.pallas_call(
        column,
        out_shape=(GRID, jax.ShapeDtypeStruct((BX, BY, BZ), jnp.float32), FOUND),
        in_specs=[VMEM, VMEM, VMEM],
        out_specs=(VMEM, HBM, VMEM),
        input_output_aliases={2: 0},
        scratch_shapes=[ROWS_X, pltpu.VMEM((3, FX * FY, PZ), jnp.bfloat16)]
        + LISTS
        + [pltpu.SemaphoreType.DMA],
        compiler_params=PARAMS,
        cost_estimate=cost(6 * 10**9),
    )(lists, cells, grid)


def call_finish(near, far, own, cells, charge, grid, found, potential):
    return pl.pallas_call(
        finish,
        out_shape=(
            jax.ShapeDtypeStruct((BX, BY, BZ), jnp.float32),
            jax.ShapeDtypeStruct((3, 1, A_DEV), jnp.float32),
        ),
        in_specs=[VMEM] * 7 + [HBM],
        out_specs=(HBM, VMEM),
        input_output_aliases={7: 0},
        scratch_shapes=[
            pltpu.VMEM((2, PX, 16, PZ), jnp.float32),
            pltpu.VMEM((2, BX, 8, BZ), jnp.float32),
            ROWS_X,
        ]
        + LISTS
        + [pltpu.SemaphoreType.DMA((2,))],
        compiler_params=PARAMS,
    )(near, far, own, cells, charge, grid, found, potential)


def local(charges, cells, counts):
    charge = charges.reshape(1, A_DEV)
    cells = cells.reshape(3, 1, A_DEV)
    counts = counts.reshape(1)
    first, second = call_compact(counts, charge, cells)
    own = call_arrange(counts, charge, cells)[None]
    first, second = swaps(first[None], second[None], "gz")
    atoms = jnp.concatenate([first, own, second], axis=0)
    first, second = swaps(atoms, atoms, "gx")
    grid = call_inner(atoms)
    atoms = jnp.concatenate([first, atoms, second], axis=0)
    first, second = swaps(atoms, atoms, "gy")
    grid, potential, found = call_column(atoms, cells, grid)
    potential, forces = call_finish(first, second, own, cells, charge, grid, found, potential)
    return potential, forces.reshape(1, 1, 1, 3, A_DEV)


def solution(mesh):
    in_specs = (P("gx", "gy", "gz", None), P("gx", "gy", "gz", None, None), P("gx", "gy", "gz"))
    out_specs = (P("gx", "gy", "gz"), P("gx", "gy", "gz", None, None))
    return jax.shard_map(local, mesh=mesh, in_specs=in_specs, out_specs=out_specs, check_vma=False)
```

```python
import math

import jax
import jax.numpy as jnp
from jax import lax
from jax.experimental import pallas as pl
from jax.experimental.pallas import tpu as pltpu
from jax.sharding import PartitionSpec as P

BX = 32
BY = 32
BZ = 384
A_DEV = 1024
PAD = 4
REACH = 4
WIDTH = A_DEV + 128
BLOCK = 256
SMALL = 128
WIDE = 2 * BLOCK

X0 = 5
Y0 = 8
PX = 42
PY = 48
PZ = 512
CHUNK = 14
FX = 40
FY = 40
FCHUNK = 20

kernel_width = 2.0
EXPONENT = -math.log2(math.e) / (2.0 * kernel_width * kernel_width)
SCALE = 1.3903614627339054
UNIT = math.sqrt(-EXPONENT)
LOW_END = 2 * PAD + 5
HIGH_START = BZ + PAD - 9
HIGH_START_Y = BY + PAD - 9
MIDDLE = BZ // 2
SPAN = A_DEV + 256 + WIDE
FRONT = 128
MERGED = 9 * A_DEV + SPAN + FRONT
ROWS = FCHUNK * FY


def weight(first, second, scale=1.0):
    away = first - second
    square = away * away
    value = jnp.exp2(math.log2(scale) - square)
    return jnp.where(square < (REACH + 0.5) ** 2 * UNIT * UNIT, value, 0.0)


def iota(shape, dim):
    return lax.broadcasted_iota(jnp.int32, shape, dim).astype(jnp.float32)


def toward(axis):
    return 2 * (lax.axis_index(axis) % 2) - 1


def live_atoms(numbers, charges, cells):
    live = lax.broadcasted_iota(jnp.int32, (1, A_DEV), 1) < numbers[0]
    charge = jnp.where(live, charges[...], 0.0).astype(jnp.bfloat16).astype(jnp.float32)
    places = [jnp.where(live, cells[i], 0) for i in range(3)]
    rows = [charge] + [place.astype(jnp.float32) for place in places[:2]]
    rows.append((places[2] - MIDDLE).astype(jnp.float32))
    rows.append(jnp.zeros((4, A_DEV), jnp.float32))
    return live, places, jnp.concatenate(rows, axis=0).astype(jnp.bfloat16)


def running_sums(masks):
    rows = [jnp.where(mask, 1.0, 0.0) for mask in masks]
    rows.append(jnp.zeros((8 - len(masks), A_DEV), jnp.float32))
    near = jnp.concatenate(rows, axis=0)
    parts = A_DEV // 128
    chunks = jnp.concatenate([near[:, 128 * c : 128 * c + 128] for c in range(parts)], axis=0)
    upto = jnp.where(iota((128, 128), 0) <= iota((128, 128), 1), 1.0, 0.0)
    ahead = jnp.where(iota((A_DEV, 128), 0) < iota((A_DEV, 128), 1) * 128.0, 1.0, 0.0)
    within = jnp.dot(
        chunks.astype(jnp.bfloat16),
        upto.astype(jnp.bfloat16),
        preferred_element_type=jnp.float32,
    )
    before = jnp.dot(
        near.astype(jnp.bfloat16),
        ahead.astype(jnp.bfloat16),
        preferred_element_type=jnp.float32,
    )
    sums = [within[8 * c : 8 * c + 8] + before[:, c : c + 1] for c in range(parts)]
    return jnp.concatenate(sums, axis=1), near


def pick(rows, spot, start, size):
    want = iota((size, A_DEV), 0) + start.astype(jnp.float32)
    hot = jnp.where(want == spot, 1.0, 0.0).astype(jnp.bfloat16)
    return lax.dot_general(
        rows, hot, (((1,), (1,)), ((), ())), preferred_element_type=jnp.float32
    )


def compact(numbers, charges, cells, first, second, lists):
    live, places, rows = live_atoms(numbers, charges, cells)
    depth = places[2]
    sums, near = running_sums([live & (depth < LOW_END), live & (depth >= HIGH_START)])
    totals = sums[:, A_DEV - 1 : A_DEV]
    spot = jnp.where(near > 0.5, sums - 1.0, -1.0)
    steps = (jnp.max(totals).astype(jnp.int32) + SMALL - 1) // SMALL
    for side in range(2):
        lists[side, :, 0:A_DEV] = jnp.zeros((4, A_DEV), jnp.float32)
        lists[side, :, A_DEV:WIDTH] = jnp.broadcast_to(
            totals[side : side + 1], (4, WIDTH - A_DEV)
        )

    def window(k, _):
        cols = pl.ds(pl.multiple_of(k * SMALL, SMALL), SMALL)
        for side in range(2):
            moved = pick(rows, spot[side : side + 1], k * SMALL, SMALL)
            lists[side, 0:3, cols] = moved[0:3]
            lists[side, 3:4, cols] = moved[3:4] + float(MIDDLE)
        return 0

    window(jnp.int32(0), 0)
    lax.fori_loop(1, steps, window, 0)
    odd = lax.axis_index("gz") % 2
    first[...] = lists[odd]
    second[...] = lists[1 - odd]


def arrange(numbers, charges, cells, own):
    live, places, rows = live_atoms(numbers, charges, cells)
    high = live & (places[1] >= HIGH_START_Y)
    low = live & (places[1] < LOW_END)
    sums, near = running_sums([high, low, live])
    totals = sums[:, A_DEV - 1 : A_DEV]
    middle_at = totals[0:1] - 1.0
    low_at = totals[2:3] - totals[1:2] - 1.0
    spot = jnp.where(low, low_at + sums[1:2], middle_at + sums[2:3] - sums[0:1] - sums[1:2])
    spot = jnp.where(high, sums[0:1] - 1.0, spot)
    spot = jnp.where(live, spot, -1.0)
    own[:, 0:A_DEV] = jnp.zeros((4, A_DEV), jnp.float32)
    for row, total in enumerate((2, 0, 1, 2)):
        own[row : row + 1, A_DEV:WIDTH] = jnp.broadcast_to(
            totals[total : total + 1], (1, WIDTH - A_DEV)
        )

    def window(k, _):
        cols = pl.ds(pl.multiple_of(k * BLOCK, BLOCK), BLOCK)
        moved = pick(rows, spot, k * BLOCK, BLOCK)
        own[0:3, cols] = moved[0:3]
        own[3:4, cols] = moved[3:4] + float(MIDDLE)
        return 0

    lax.fori_loop(0, (numbers[0] + BLOCK - 1) // BLOCK, window, 0)


def append(ref, brick, start, number, offset, dx, dy, dz, merged, padded):
    row = lax.broadcasted_iota(jnp.int32, (4, 128), 0)
    moved = jnp.where(row == 1, jnp.float32(X0 - PAD + BX * dx), 0.0)
    moved = jnp.where(row == 2, jnp.float32(Y0 - PAD + BY * dy), moved)
    moved = jnp.where(row == 3, jnp.float32(BZ * dz - PAD), moved)
    unit = jnp.where(row == 0, 1.0, UNIT)
    for c in range(0, A_DEV, 128):
        padded[0:4, c : c + 128] = (ref[brick, :, c : c + 128] + moved) * unit
    skip = start % 128
    atoms = padded[:, pl.ds(pl.multiple_of(start - skip, 128), SPAN)]
    lanes = lax.broadcasted_iota(jnp.int32, (8, SPAN), 1)
    atoms = jnp.where((lanes >= skip) & (lanes < skip + number), atoms, 0.0)
    room = offset % 128
    back = jnp.where(room >= skip, 0, 128)
    atoms = pltpu.roll(atoms, room - skip + back, 1)
    base = pl.multiple_of(FRONT + offset - room - back, 128)
    merged[:, pl.ds(base, 256)] += atoms[:, 0:256]
    merged[:, pl.ds(base + 256, SPAN - 256)] = atoms[:, 256:SPAN]
    return offset + number


def spread(merged, start, size, x0, nx, y0, ny, grid, rows_x, first, row0):
    cols = pl.ds(pl.multiple_of(start + FRONT, 128), size)
    charge = merged[0:1, cols]
    xa = merged[1:2, cols]
    ya = merged[2:3, cols]
    za = merged[3:4, cols]
    gy = weight((iota((ny, size), 0) + jnp.float32(y0)) * UNIT, ya) * (charge * (1.0 / SCALE))
    zi = iota((PZ, size), 0)
    zi = jnp.where(zi < 448.0, zi, zi - float(PZ)) * UNIT
    right = weight(zi, za, SCALE).astype(jnp.bfloat16)
    rows_x[:, 0:size] = weight(iota((48, size), 0) * UNIT, xa)
    chunk = min(nx, CHUNK * PY // ny)
    for c in range(0, nx, chunk):
        at = x0 + c
        left = jnp.stack(
            [rows_x[pl.ds(at + i, 1), 0:size] * gy for i in range(chunk)], axis=0
        )
        left = left.reshape(chunk * ny, size).astype(jnp.bfloat16)
        part = lax.dot_general(
            left, right, (((1,), (1,)), ((), ())), preferred_element_type=jnp.float32
        )
        part = part.reshape(chunk, ny, PZ)
        if first:
            grid[pl.ds(at, chunk), pl.ds(row0, ny), :] = part
        else:
            grid[pl.ds(at, chunk), pl.ds(row0, ny), :] += part


def spread_all(merged, total, x0, nx, y0, ny, grid, rows_x, clear, row0):
    rest = total % WIDE
    wide = total // WIDE + (rest > BLOCK).astype(jnp.int32)
    if clear:
        wide = jnp.maximum(wide, 1)
        spread(merged, 0, WIDE, x0, nx, y0, ny, grid, rows_x, True, row0)

    def block(k, _):
        spread(merged, k * WIDE, WIDE, x0, nx, y0, ny, grid, rows_x, False, row0)
        return 0

    lax.fori_loop(1 if clear else 0, wide, block, 0)

    @pl.when(total > wide * WIDE)
    def _():
        spread(merged, wide * WIDE, BLOCK, x0, nx, y0, ny, grid, rows_x, False, row0)


def number_of(ref, brick, row):
    return ref[brick, row : row + 1, A_DEV:WIDTH][0, 0].astype(jnp.int32)


def gather(ref, bricks, side, merged, padded):
    merged[:, 0 : FRONT + 256] = jnp.zeros((8, FRONT + 256), jnp.float32)
    offset = jnp.int32(0)
    for brick, (dx, dy, dz) in bricks:
        number = number_of(ref, brick, 0)
        start = jnp.int32(0)
        if side is not None:
            low = number_of(ref, brick, 2)
            start = jnp.where(side > 0, number - low, 0)
            number = jnp.where(side > 0, low, number_of(ref, brick, 1))
        offset = append(ref, brick, start, number, offset, dx, dy, dz, merged, padded)
    return offset


def slots_of(axis):
    step = toward(axis)
    return (step, 0, -step)


def inner(lists, grid, rows_x, merged, padded):
    padded[...] = jnp.zeros_like(padded)
    zs = slots_of("gz")
    total = gather(lists, [(j, (0, 0, zs[j])) for j in (1, 0, 2)], None, merged, padded)
    spread_all(merged, total, 0, PX, 0, PY, grid, rows_x, True, 0)


def column(
    lists, place, before, grid, potential, found, rows_x, fields, merged, padded, sem
):
    padded[...] = jnp.zeros_like(padded)
    xs, zs = slots_of("gx"), slots_of("gz")
    for i in (0, 2):
        total = gather(
            lists, [(3 * i + j, (xs[i], 0, zs[j])) for j in range(3)], None, merged, padded
        )
        x0 = jnp.where(xs[i] > 0, 28, 0)
        spread_all(merged, total, x0, 14, 0, PY, grid, rows_x, False, 0)
    copy = pltpu.make_async_copy(
        grid.at[X0 : X0 + BX, 16:32, 0:BZ], potential.at[:, 8:24, :], sem
    )
    copy.start()
    found[...] = jnp.zeros_like(found)
    count = number_of(lists, 4, 0)

    def build(c):
        gx, gy, gz = [], [], []
        for x in range(c * FCHUNK, (c + 1) * FCHUNK):
            gx.append(grid[x + 2, 4:44, :] - grid[x, 4:44, :])
            gy.append(grid[x + 1, 5:45, :] - grid[x + 1, 3:43, :])
            mid = grid[x + 1, 4:44, :]
            gz.append(pltpu.roll(mid, PZ - 2, 1) - mid)
        for d, parts in enumerate((gx, gy, gz)):
            both = jnp.stack(parts, axis=0).reshape(ROWS, PZ).astype(jnp.bfloat16)
            fields[d, c * ROWS : (c + 1) * ROWS, :] = both

    def sample(start, fresh):
        cols = pl.ds(pl.multiple_of(start, WIDE), WIDE)
        xa, ya, za = atom_cells(place, cols)
        zi = depths(WIDE)
        depth = jnp.where(zi == za, 1.0, 0.0).astype(jnp.bfloat16)
        below = jnp.where(zi == za - 1.0, 1.0, 0.0).astype(jnp.bfloat16)
        sums = [jnp.zeros((FY, WIDE), jnp.float32)] * 3
        for c in range(FX // FCHUNK):
            if fresh:
                build(c)
            for d in range(3):
                part = jnp.dot(
                    fields[d, c * ROWS : (c + 1) * ROWS, :],
                    below if d == 2 else depth,
                    preferred_element_type=jnp.float32,
                ).reshape(FCHUNK, FY, WIDE)
                for i in range(FCHUNK):
                    hot_x = xa == float(c * FCHUNK + i)
                    sums[d] = sums[d] + jnp.where(hot_x, part[i], 0.0)
        hot_y = iota((FY, WIDE), 0) == ya
        for d in range(3):
            value = jnp.sum(jnp.where(hot_y, sums[d], 0.0), axis=0, keepdims=True)
            found[d : d + 1, cols] = value

    sample(0, True)

    def more(k, _):
        sample(k * WIDE, False)
        return 0

    lax.fori_loop(1, (count + WIDE - 1) // WIDE, more, 0)
    copy.wait()


def atom_cells(place, cols):
    xa = place[0, :, cols].astype(jnp.float32)
    ya = place[1, :, cols].astype(jnp.float32)
    return xa, ya, (place[2, :, cols] - PAD).astype(jnp.float32)


def depths(size):
    zi = iota((PZ, size), 0)
    return jnp.where(zi < 448.0, zi, zi - float(PZ))


def slab(turn, lists, grid, potential, part, stage, rows_x, merged, padded, sem):
    xs, zs = slots_of("gx"), slots_of("gz")
    dy = toward("gy") * turn
    total = gather(
        lists,
        [(3 * m + j, (xs[m], dy, zs[j])) for m in range(3) for j in range(3)],
        dy,
        merged,
        padded,
    )
    y0 = pl.multiple_of(jnp.where(dy > 0, 32, 0), 8)
    spread_all(merged, total, 0, PX, y0, 16, part, rows_x, True, 0)
    at = pl.multiple_of(jnp.where(dy > 0, 0, 8), 8)
    stage[...] = (
        part[X0 : X0 + BX, pl.ds(at, 8), 0:BZ] + grid[X0 : X0 + BX, pl.ds(y0 + at, 8), 0:BZ]
    )
    row = pl.multiple_of(jnp.where(dy > 0, 24, 0), 8)
    copy = pltpu.make_async_copy(stage, potential.at[:, pl.ds(row, 8), :], sem)
    copy.start()
    return y0, copy


def finish(
    near, far, own, place, charge, grid, found, potential_in, potential, forces,
    parts, stages, rows_x, merged, padded, sems,
):
    padded[...] = jnp.zeros_like(padded)
    slabs = [
        slab(
            1 - 2 * i, lists, grid, potential, parts.at[i], stages.at[i],
            rows_x, merged, padded, sems.at[i],
        )
        for i, lists in enumerate((near, far))
    ]
    count = number_of(own, 0, 0)
    forces[...] = jnp.zeros_like(forces)

    def block(k, _):
        cols = pl.ds(pl.multiple_of(k * WIDE, WIDE), WIDE)
        xa, ya, za = atom_cells(place, cols)
        zi = depths(WIDE)
        here = jnp.where(zi == za, 1.0, 0.0).astype(jnp.bfloat16)
        slope = jnp.where(zi == za + 1.0, 1.0, 0.0) - jnp.where(zi == za - 1.0, 1.0, 0.0)
        slope = slope.astype(jnp.bfloat16)
        sums = [found[d : d + 1, cols] for d in range(3)]
        for i, (y0, _) in enumerate(slabs):
            rows = parts[i].reshape(PX * 16, PZ).astype(jnp.bfloat16)
            value = jnp.dot(rows, here, preferred_element_type=jnp.float32)
            value = value.reshape(PX, 16, WIDE)
            change = jnp.dot(rows, slope, preferred_element_type=jnp.float32)
            change = change.reshape(PX, 16, WIDE)
            level = jnp.zeros((16, WIDE), jnp.float32)
            along_x = level
            along_z = level
            for x in range(PX):
                at_x = xa == float(x - 1)
                level = level + jnp.where(at_x, value[x], 0.0)
                along_z = along_z + jnp.where(at_x, change[x], 0.0)
                side = jnp.where(xa == float(x - 2), 1.0, 0.0)
                side = side - jnp.where(xa == float(x), 1.0, 0.0)
                along_x = along_x + side * value[x]
            away = iota((16, WIDE), 0) + (y0.astype(jnp.float32) - float(Y0 - PAD)) - ya
            at_y = away == 0.0
            fx = jnp.where(at_y, along_x, 0.0)
            fy = jnp.where(away == 1.0, level, 0.0) - jnp.where(away == -1.0, level, 0.0)
            fz = jnp.where(at_y, along_z, 0.0)
            for d, one in enumerate((fx, fy, fz)):
                sums[d] = sums[d] + jnp.sum(one, axis=0, keepdims=True)
        slots = lax.broadcasted_iota(jnp.int32, (1, WIDE), 1) + k * WIDE
        factor = -0.5 * charge[:, cols]
        for d in range(3):
            forces[d, :, cols] = jnp.where(slots < count, sums[d] * factor, 0.0)
        return 0

    lax.fori_loop(0, (count + WIDE - 1) // WIDE, block, 0)
    for _, copy in slabs:
        copy.wait()


def swaps(block, other, axis):
    size = lax.axis_size(axis)
    first = [(i, (i + 1 if i % 2 else i - 1) % size) for i in range(size)]
    second = [(i, i ^ 1) for i in range(size)]
    return lax.ppermute(block, axis, first), lax.ppermute(other, axis, second)


VMEM = pl.BlockSpec(memory_space=pltpu.VMEM)
HBM = pl.BlockSpec(memory_space=pl.ANY)
LIMIT = 40 * 1024 * 1024


def call_compact(counts, charge, cells):
    shape = pltpu.VMEM((4, WIDTH), jnp.float32)
    return pl.pallas_call(
        compact,
        out_shape=(shape, shape),
        in_specs=[pl.BlockSpec(memory_space=pltpu.SMEM), VMEM, VMEM],
        out_specs=(VMEM,) * 2,
        scratch_shapes=[pltpu.VMEM((2, 4, WIDTH), jnp.float32)],
    )(counts, charge, cells)


def call_arrange(counts, charge, cells):
    return pl.pallas_call(
        arrange,
        out_shape=pltpu.VMEM((4, WIDTH), jnp.float32),
        in_specs=[pl.BlockSpec(memory_space=pltpu.SMEM), VMEM, VMEM],
        out_specs=VMEM,
        cost_estimate=pl.CostEstimate(flops=2 * 10**9, bytes_accessed=10**5, transcendentals=0),
    )(counts, charge, cells)


GRID = pltpu.VMEM((PX, PY, PZ), jnp.float32)
FOUND = pltpu.VMEM((8, A_DEV), jnp.float32)
ROWS_X = pltpu.VMEM((48, WIDE), jnp.float32)
LISTS = [
    pltpu.VMEM((8, MERGED), jnp.float32),
    pltpu.VMEM((8, A_DEV + SPAN), jnp.float32),
]
PARAMS = pltpu.CompilerParams(vmem_limit_bytes=LIMIT)


def cost(flops):
    return pl.CostEstimate(flops=flops, bytes_accessed=10**6, transcendentals=0)


def call_inner(lists):
    return pl.pallas_call(
        inner,
        out_shape=GRID,
        in_specs=[VMEM],
        out_specs=VMEM,
        scratch_shapes=[ROWS_X] + LISTS,
        compiler_params=PARAMS,
        cost_estimate=cost(2 * 10**9),
    )(lists)


def call_column(lists, cells, grid):
    return pl.pallas_call(
        column,
        out_shape=(GRID, jax.ShapeDtypeStruct((BX, BY, BZ), jnp.float32), FOUND),
        in_specs=[VMEM, VMEM, VMEM],
        out_specs=(VMEM, HBM, VMEM),
        input_output_aliases={2: 0},
        scratch_shapes=[ROWS_X, pltpu.VMEM((3, FX * FY, PZ), jnp.bfloat16)]
        + LISTS
        + [pltpu.SemaphoreType.DMA],
        compiler_params=PARAMS,
        cost_estimate=cost(6 * 10**9),
    )(lists, cells, grid)


def call_finish(near, far, own, cells, charge, grid, found, potential):
    return pl.pallas_call(
        finish,
        out_shape=(
            jax.ShapeDtypeStruct((BX, BY, BZ), jnp.float32),
            jax.ShapeDtypeStruct((3, 1, A_DEV), jnp.float32),
        ),
        in_specs=[VMEM] * 7 + [HBM],
        out_specs=(HBM, VMEM),
        input_output_aliases={7: 0},
        scratch_shapes=[
            pltpu.VMEM((2, PX, 16, PZ), jnp.float32),
            pltpu.VMEM((2, BX, 8, BZ), jnp.float32),
            ROWS_X,
        ]
        + LISTS
        + [pltpu.SemaphoreType.DMA((2,))],
        compiler_params=PARAMS,
    )(near, far, own, cells, charge, grid, found, potential)


def local(charges, cells, counts):
    charge = charges.reshape(1, A_DEV)
    cells = cells.reshape(3, 1, A_DEV)
    counts = counts.reshape(1)
    first, second = call_compact(counts, charge, cells)
    own = call_arrange(counts, charge, cells)[None]
    first, second = swaps(first[None], second[None], "gz")
    atoms = jnp.concatenate([first, own, second], axis=0)
    first, second = swaps(atoms, atoms, "gx")
    grid = call_inner(atoms)
    atoms = jnp.concatenate([first, atoms, second], axis=0)
    first, second = swaps(atoms, atoms, "gy")
    grid, potential, found = call_column(atoms, cells, grid)
    potential, forces = call_finish(first, second, own, cells, charge, grid, found, potential)
    return potential, forces.reshape(1, 1, 1, 3, A_DEV)


def solution(mesh):
    in_specs = (P("gx", "gy", "gz", None), P("gx", "gy", "gz", None, None), P("gx", "gy", "gz"))
    out_specs = (P("gx", "gy", "gz"), P("gx", "gy", "gz", None, None))
    return jax.shard_map(local, mesh=mesh, in_specs=in_specs, out_specs=out_specs, check_vma=False)
```

```python
import math

import jax
import jax.numpy as jnp
from jax import lax
from jax.experimental import pallas as pl
from jax.experimental.pallas import tpu as pltpu
from jax.sharding import PartitionSpec as P

BX = 32
BY = 32
BZ = 384
A_DEV = 1024
PAD = 4
REACH = 4
WIDTH = A_DEV + 128
BLOCK = 256
SMALL = 128
WIDE = 2 * BLOCK

X0 = 5
Y0 = 8
PX = 42
PY = 48
PZ = 512
CHUNK = 14
FX = 40
FY = 40
FCHUNK = 20

kernel_width = 2.0
EXPONENT = -math.log2(math.e) / (2.0 * kernel_width * kernel_width)
SCALE = 1.3903614627339054
UNIT = math.sqrt(-EXPONENT)
LOW_END = 2 * PAD + 5
HIGH_START = BZ + PAD - 9
HIGH_START_X = BX + PAD - 9
HIGH_START_Y = BY + PAD - 9
MIDDLE = BZ // 2
SPAN = A_DEV + 256 + WIDE
FRONT = 128
MERGED = 9 * A_DEV + SPAN + FRONT
ROWS = FCHUNK * FY


def weight(first, second, scale=1.0):
    away = first - second
    square = away * away
    value = jnp.exp2(math.log2(scale) - square)
    return jnp.where(square < (REACH + 0.5) ** 2 * UNIT * UNIT, value, 0.0)


def iota(shape, dim):
    return lax.broadcasted_iota(jnp.int32, shape, dim).astype(jnp.float32)


def toward(axis):
    return 2 * (lax.axis_index(axis) % 2) - 1


def live_atoms(numbers, charges, cells):
    live = lax.broadcasted_iota(jnp.int32, (1, A_DEV), 1) < numbers[0]
    charge = jnp.where(live, charges[...], 0.0).astype(jnp.bfloat16).astype(jnp.float32)
    places = [jnp.where(live, cells[i], 0) for i in range(3)]
    rows = [charge] + [place.astype(jnp.float32) for place in places[:2]]
    rows.append((places[2] - MIDDLE).astype(jnp.float32))
    rows.append(jnp.zeros((4, A_DEV), jnp.float32))
    return live, places, jnp.concatenate(rows, axis=0).astype(jnp.bfloat16)


def running_sums(masks):
    height = (len(masks) + 7) // 8 * 8
    rows = [jnp.where(mask, 1.0, 0.0) for mask in masks]
    if height > len(masks):
        rows.append(jnp.zeros((height - len(masks), A_DEV), jnp.float32))
    near = jnp.concatenate(rows, axis=0)
    parts = A_DEV // 128
    chunks = jnp.concatenate([near[:, 128 * c : 128 * c + 128] for c in range(parts)], axis=0)
    upto = jnp.where(iota((128, 128), 0) <= iota((128, 128), 1), 1.0, 0.0)
    ahead = jnp.where(iota((A_DEV, 128), 0) < iota((A_DEV, 128), 1) * 128.0, 1.0, 0.0)
    within = jnp.dot(
        chunks.astype(jnp.bfloat16),
        upto.astype(jnp.bfloat16),
        preferred_element_type=jnp.float32,
    )
    before = jnp.dot(
        near.astype(jnp.bfloat16),
        ahead.astype(jnp.bfloat16),
        preferred_element_type=jnp.float32,
    )
    sums = [
        within[height * c : height * (c + 1)] + before[:, c : c + 1] for c in range(parts)
    ]
    return jnp.concatenate(sums, axis=1)


def pick(rows, spot, start, size):
    want = iota((size, A_DEV), 0) + start.astype(jnp.float32)
    hot = jnp.where(want == spot, 1.0, 0.0).astype(jnp.bfloat16)
    return lax.dot_general(
        rows, hot, (((1,), (1,)), ((), ())), preferred_element_type=jnp.float32
    )


def compact(numbers, charges, cells, first, second, lists):
    live, places, rows = live_atoms(numbers, charges, cells)
    depth = places[2]
    masks = [live & (depth < LOW_END), live & (depth >= HIGH_START)]
    sums = running_sums(masks)
    totals = sums[:, A_DEV - 1 : A_DEV]
    spot = [jnp.where(masks[i], sums[i : i + 1] - 1.0, -1.0) for i in range(2)]
    steps = (jnp.max(totals).astype(jnp.int32) + SMALL - 1) // SMALL
    for side in range(2):
        lists[side, :, 0:A_DEV] = jnp.zeros((4, A_DEV), jnp.float32)
        lists[side, :, A_DEV:WIDTH] = jnp.broadcast_to(
            totals[side : side + 1], (4, WIDTH - A_DEV)
        )

    def window(k, _):
        cols = pl.ds(pl.multiple_of(k * SMALL, SMALL), SMALL)
        for side in range(2):
            moved = pick(rows, spot[side], k * SMALL, SMALL)
            lists[side, 0:3, cols] = moved[0:3]
            lists[side, 3:4, cols] = moved[3:4] + float(MIDDLE)
        return 0

    window(jnp.int32(0), 0)
    lax.fori_loop(1, steps, window, 0)
    odd = lax.axis_index("gz") % 2
    first[...] = lists[odd]
    second[...] = lists[1 - odd]


def arrange(numbers, charges, cells, own, first, second, lists):
    live, places, rows = live_atoms(numbers, charges, cells)
    high = live & (places[1] >= HIGH_START_Y)
    low = live & (places[1] < LOW_END)
    sides = [live, live & (places[0] < LOW_END), live & (places[0] >= HIGH_START_X)]
    sums = running_sums([mask for side in sides for mask in (high & side, low & side, side)])
    totals = sums[:, A_DEV - 1 : A_DEV]
    spots = []
    for i, side in enumerate(sides):
        highs, lows, alls = (sums[3 * i + j : 3 * i + j + 1] for j in range(3))
        ends = [totals[3 * i + j : 3 * i + j + 1] for j in range(3)]
        spot = jnp.where(low, ends[2] - ends[1] + lows, ends[0] + alls - highs - lows)
        spot = jnp.where(high, highs, spot) - 1.0
        spots.append(jnp.where(side, spot, -1.0))
        out = own if i == 0 else lists.at[i - 1]
        out[:, 0:A_DEV] = jnp.zeros((4, A_DEV), jnp.float32)
        for row, end in enumerate((2, 0, 1, 2)):
            out[row : row + 1, A_DEV:WIDTH] = jnp.broadcast_to(ends[end], (1, WIDTH - A_DEV))

    def fill(out, spot, k):
        cols = pl.ds(pl.multiple_of(k * BLOCK, BLOCK), BLOCK)
        moved = pick(rows, spot, k * BLOCK, BLOCK)
        out[0:3, cols] = moved[0:3]
        out[3:4, cols] = moved[3:4] + float(MIDDLE)

    def window(k, _):
        fill(own, spots[0], k)
        return 0

    def side_window(k, _):
        fill(lists.at[0], spots[1], k)
        fill(lists.at[1], spots[2], k)
        return 0

    widest = jnp.maximum(jnp.max(totals[5:6]), jnp.max(totals[8:9])).astype(jnp.int32)
    side_window(jnp.int32(0), 0)
    lax.fori_loop(0, (numbers[0] + BLOCK - 1) // BLOCK, window, 0)
    lax.fori_loop(1, (widest + BLOCK - 1) // BLOCK, side_window, 0)
    odd = lax.axis_index("gx") % 2
    first[...] = lists[odd]
    second[...] = lists[1 - odd]


def append(ref, brick, start, number, offset, dx, dy, dz, merged, padded):
    row = lax.broadcasted_iota(jnp.int32, (4, 128), 0)
    moved = jnp.where(row == 1, jnp.float32(X0 - PAD + BX * dx), 0.0)
    moved = jnp.where(row == 2, jnp.float32(Y0 - PAD + BY * dy), moved)
    moved = jnp.where(row == 3, jnp.float32(BZ * dz - PAD), moved)
    unit = jnp.where(row == 0, 1.0, UNIT)
    for c in range(0, A_DEV, 128):
        padded[0:4, c : c + 128] = (ref[brick, :, c : c + 128] + moved) * unit
    skip = start % 128
    atoms = padded[:, pl.ds(pl.multiple_of(start - skip, 128), SPAN)]
    lanes = lax.broadcasted_iota(jnp.int32, (8, SPAN), 1)
    atoms = jnp.where((lanes >= skip) & (lanes < skip + number), atoms, 0.0)
    room = offset % 128
    back = jnp.where(room >= skip, 0, 128)
    atoms = pltpu.roll(atoms, room - skip + back, 1)
    base = pl.multiple_of(FRONT + offset - room - back, 128)
    merged[:, pl.ds(base, 256)] += atoms[:, 0:256]
    merged[:, pl.ds(base + 256, SPAN - 256)] = atoms[:, 256:SPAN]
    return offset + number


def spread(merged, start, size, x0, nx, y0, ny, grid, rows_x, first, row0):
    cols = pl.ds(pl.multiple_of(start + FRONT, 128), size)
    charge = merged[0:1, cols]
    xa = merged[1:2, cols]
    ya = merged[2:3, cols]
    za = merged[3:4, cols]
    gy = weight((iota((ny, size), 0) + jnp.float32(y0)) * UNIT, ya) * (charge * (1.0 / SCALE))
    zi = iota((PZ, size), 0)
    zi = jnp.where(zi < 448.0, zi, zi - float(PZ)) * UNIT
    right = weight(zi, za, SCALE).astype(jnp.bfloat16)
    rows_x[:, 0:size] = weight(iota((48, size), 0) * UNIT, xa)
    chunk = min(nx, CHUNK * PY // ny)
    for c in range(0, nx, chunk):
        at = x0 + c
        left = jnp.stack(
            [rows_x[pl.ds(at + i, 1), 0:size] * gy for i in range(chunk)], axis=0
        )
        left = left.reshape(chunk * ny, size).astype(jnp.bfloat16)
        part = lax.dot_general(
            left, right, (((1,), (1,)), ((), ())), preferred_element_type=jnp.float32
        )
        part = part.reshape(chunk, ny, PZ)
        if first:
            grid[pl.ds(at, chunk), pl.ds(row0, ny), :] = part
        else:
            grid[pl.ds(at, chunk), pl.ds(row0, ny), :] += part


def spread_all(merged, total, x0, nx, y0, ny, grid, rows_x, clear, row0):
    rest = total % WIDE
    wide = total // WIDE + (rest > BLOCK).astype(jnp.int32)
    if clear:
        wide = jnp.maximum(wide, 1)
        spread(merged, 0, WIDE, x0, nx, y0, ny, grid, rows_x, True, row0)

    def block(k, _):
        spread(merged, k * WIDE, WIDE, x0, nx, y0, ny, grid, rows_x, False, row0)
        return 0

    lax.fori_loop(1 if clear else 0, wide, block, 0)

    @pl.when(total > wide * WIDE)
    def _():
        spread(merged, wide * WIDE, BLOCK, x0, nx, y0, ny, grid, rows_x, False, row0)


def number_of(ref, brick, row):
    return ref[brick, row : row + 1, A_DEV:WIDTH][0, 0].astype(jnp.int32)


def gather(ref, bricks, side, merged, padded):
    merged[:, 0 : FRONT + 256] = jnp.zeros((8, FRONT + 256), jnp.float32)
    offset = jnp.int32(0)
    for brick, (dx, dy, dz) in bricks:
        number = number_of(ref, brick, 0)
        start = jnp.int32(0)
        if side is not None and type(dz) is int:
            low = number_of(ref, brick, 2)
            start = jnp.where(side > 0, number - low, 0)
            number = jnp.where(side > 0, low, number_of(ref, brick, 1))
        offset = append(ref, brick, start, number, offset, dx, dy, dz, merged, padded)
    return offset


def slots_of(axis):
    step = toward(axis)
    return (step, 0, -step)


def inner(lists, grid, rows_x, merged, padded):
    padded[...] = jnp.zeros_like(padded)
    zs = slots_of("gz")
    total = gather(lists, [(j, (0, 0, zs[j])) for j in (1, 0, 2)], None, merged, padded)
    spread_all(merged, total, 0, PX, 0, PY, grid, rows_x, True, 0)


def column(
    lists, place, before, grid, potential, found, rows_x, fields, merged, padded, sem
):
    padded[...] = jnp.zeros_like(padded)
    xs, zs = slots_of("gx"), slots_of("gz")
    for i in (0, 2):
        total = gather(
            lists, [(3 * i + j, (xs[i], 0, zs[j])) for j in range(3)], None, merged, padded
        )
        x0 = jnp.where(xs[i] > 0, 28, 0)
        spread_all(merged, total, x0, 14, 0, PY, grid, rows_x, False, 0)
    copy = pltpu.make_async_copy(
        grid.at[X0 : X0 + BX, 16:32, 0:BZ], potential.at[:, 8:24, :], sem
    )
    copy.start()
    found[...] = jnp.zeros_like(found)
    count = number_of(lists, 4, 0)

    def build(c):
        gx, gy, gz = [], [], []
        for x in range(c * FCHUNK, (c + 1) * FCHUNK):
            gx.append(grid[x + 2, 4:44, :] - grid[x, 4:44, :])
            gy.append(grid[x + 1, 5:45, :] - grid[x + 1, 3:43, :])
            mid = grid[x + 1, 4:44, :]
            gz.append(pltpu.roll(mid, PZ - 2, 1) - mid)
        for d, parts in enumerate((gx, gy, gz)):
            both = jnp.stack(parts, axis=0).reshape(ROWS, PZ).astype(jnp.bfloat16)
            fields[d, c * ROWS : (c + 1) * ROWS, :] = both

    def sample(start, fresh):
        cols = pl.ds(pl.multiple_of(start, WIDE), WIDE)
        xa, ya, za = atom_cells(place, cols)
        zi = depths(WIDE)
        depth = jnp.where(zi == za, 1.0, 0.0).astype(jnp.bfloat16)
        below = jnp.where(zi == za - 1.0, 1.0, 0.0).astype(jnp.bfloat16)
        sums = [jnp.zeros((FY, WIDE), jnp.float32)] * 3
        for c in range(FX // FCHUNK):
            if fresh:
                build(c)
            for d in range(3):
                part = jnp.dot(
                    fields[d, c * ROWS : (c + 1) * ROWS, :],
                    below if d == 2 else depth,
                    preferred_element_type=jnp.float32,
                ).reshape(FCHUNK, FY, WIDE)
                for i in range(FCHUNK):
                    hot_x = xa == float(c * FCHUNK + i)
                    sums[d] = sums[d] + jnp.where(hot_x, part[i], 0.0)
        hot_y = iota((FY, WIDE), 0) == ya
        for d in range(3):
            value = jnp.sum(jnp.where(hot_y, sums[d], 0.0), axis=0, keepdims=True)
            found[d : d + 1, cols] = value

    sample(0, True)

    def more(k, _):
        sample(k * WIDE, False)
        return 0

    lax.fori_loop(1, (count + WIDE - 1) // WIDE, more, 0)
    copy.wait()


def atom_cells(place, cols):
    xa = place[0, :, cols].astype(jnp.float32)
    ya = place[1, :, cols].astype(jnp.float32)
    return xa, ya, (place[2, :, cols] - PAD).astype(jnp.float32)


def depths(size):
    zi = iota((PZ, size), 0)
    return jnp.where(zi < 448.0, zi, zi - float(PZ))


def slab(turn, lists, grid, potential, part, stage, rows_x, merged, padded, sem):
    xs, zs = slots_of("gx"), slots_of("gz")
    dy = toward("gy") * turn
    total = gather(
        lists,
        [(3 * m + j, (xs[m], dy, zs[j])) for m in range(3) for j in range(3)],
        dy,
        merged,
        padded,
    )
    y0 = pl.multiple_of(jnp.where(dy > 0, 32, 0), 8)
    spread_all(merged, total, 0, PX, y0, 16, part, rows_x, True, 0)
    at = pl.multiple_of(jnp.where(dy > 0, 0, 8), 8)
    stage[...] = (
        part[X0 : X0 + BX, pl.ds(at, 8), 0:BZ] + grid[X0 : X0 + BX, pl.ds(y0 + at, 8), 0:BZ]
    )
    row = pl.multiple_of(jnp.where(dy > 0, 24, 0), 8)
    copy = pltpu.make_async_copy(stage, potential.at[:, pl.ds(row, 8), :], sem)
    copy.start()
    return y0, copy


def finish(
    near, far, own, place, charge, grid, found, potential_in, potential, forces,
    parts, stages, rows_x, merged, padded, sems,
):
    padded[...] = jnp.zeros_like(padded)
    slabs = [
        slab(
            1 - 2 * i, lists, grid, potential, parts.at[i], stages.at[i],
            rows_x, merged, padded, sems.at[i],
        )
        for i, lists in enumerate((near, far))
    ]
    count = number_of(own, 0, 0)
    forces[...] = jnp.zeros_like(forces)

    def block(k, _):
        cols = pl.ds(pl.multiple_of(k * WIDE, WIDE), WIDE)
        xa, ya, za = atom_cells(place, cols)
        zi = depths(WIDE)
        here = jnp.where(zi == za, 1.0, 0.0).astype(jnp.bfloat16)
        slope = jnp.where(zi == za + 1.0, 1.0, 0.0) - jnp.where(zi == za - 1.0, 1.0, 0.0)
        slope = slope.astype(jnp.bfloat16)
        sums = [found[d : d + 1, cols] for d in range(3)]
        for i, (y0, _) in enumerate(slabs):
            rows = parts[i].reshape(PX * 16, PZ).astype(jnp.bfloat16)
            value = jnp.dot(rows, here, preferred_element_type=jnp.float32)
            value = value.reshape(PX, 16, WIDE)
            change = jnp.dot(rows, slope, preferred_element_type=jnp.float32)
            change = change.reshape(PX, 16, WIDE)
            level = jnp.zeros((16, WIDE), jnp.float32)
            along_x = level
            along_z = level
            for x in range(PX):
                at_x = xa == float(x - 1)
                level = level + jnp.where(at_x, value[x], 0.0)
                along_z = along_z + jnp.where(at_x, change[x], 0.0)
                side = jnp.where(xa == float(x - 2), 1.0, 0.0)
                side = side - jnp.where(xa == float(x), 1.0, 0.0)
                along_x = along_x + side * value[x]
            away = iota((16, WIDE), 0) + (y0.astype(jnp.float32) - float(Y0 - PAD)) - ya
            at_y = away == 0.0
            fx = jnp.where(at_y, along_x, 0.0)
            fy = jnp.where(away == 1.0, level, 0.0) - jnp.where(away == -1.0, level, 0.0)
            fz = jnp.where(at_y, along_z, 0.0)
            for d, one in enumerate((fx, fy, fz)):
                sums[d] = sums[d] + jnp.sum(one, axis=0, keepdims=True)
        slots = lax.broadcasted_iota(jnp.int32, (1, WIDE), 1) + k * WIDE
        factor = -0.5 * charge[:, cols]
        for d in range(3):
            forces[d, :, cols] = jnp.where(slots < count, sums[d] * factor, 0.0)
        return 0

    lax.fori_loop(0, (count + WIDE - 1) // WIDE, block, 0)
    for _, copy in slabs:
        copy.wait()


def swaps(block, other, axis):
    size = lax.axis_size(axis)
    first = [(i, (i + 1 if i % 2 else i - 1) % size) for i in range(size)]
    second = [(i, i ^ 1) for i in range(size)]
    return lax.ppermute(block, axis, first), lax.ppermute(other, axis, second)


VMEM = pl.BlockSpec(memory_space=pltpu.VMEM)
HBM = pl.BlockSpec(memory_space=pl.ANY)
LIMIT = 40 * 1024 * 1024


def call_compact(counts, charge, cells):
    shape = pltpu.VMEM((4, WIDTH), jnp.float32)
    return pl.pallas_call(
        compact,
        out_shape=(shape, shape),
        in_specs=[pl.BlockSpec(memory_space=pltpu.SMEM), VMEM, VMEM],
        out_specs=(VMEM,) * 2,
        scratch_shapes=[pltpu.VMEM((2, 4, WIDTH), jnp.float32)],
    )(counts, charge, cells)


def call_arrange(counts, charge, cells):
    shape = pltpu.VMEM((4, WIDTH), jnp.float32)
    return pl.pallas_call(
        arrange,
        out_shape=(shape, shape, shape),
        in_specs=[pl.BlockSpec(memory_space=pltpu.SMEM), VMEM, VMEM],
        out_specs=(VMEM,) * 3,
        scratch_shapes=[pltpu.VMEM((2, 4, WIDTH), jnp.float32)],
        cost_estimate=pl.CostEstimate(flops=2 * 10**9, bytes_accessed=10**5, transcendentals=0),
    )(counts, charge, cells)


GRID = pltpu.VMEM((PX, PY, PZ), jnp.float32)
FOUND = pltpu.VMEM((8, A_DEV), jnp.float32)
ROWS_X = pltpu.VMEM((48, WIDE), jnp.float32)
LISTS = [
    pltpu.VMEM((8, MERGED), jnp.float32),
    pltpu.VMEM((8, A_DEV + SPAN), jnp.float32),
]
PARAMS = pltpu.CompilerParams(vmem_limit_bytes=LIMIT)


def cost(flops):
    return pl.CostEstimate(flops=flops, bytes_accessed=10**6, transcendentals=0)


def call_inner(lists):
    return pl.pallas_call(
        inner,
        out_shape=GRID,
        in_specs=[VMEM],
        out_specs=VMEM,
        scratch_shapes=[ROWS_X] + LISTS,
        compiler_params=PARAMS,
        cost_estimate=cost(2 * 10**9),
    )(lists)


def call_column(lists, cells, grid):
    return pl.pallas_call(
        column,
        out_shape=(GRID, jax.ShapeDtypeStruct((BX, BY, BZ), jnp.float32), FOUND),
        in_specs=[VMEM, VMEM, VMEM],
        out_specs=(VMEM, HBM, VMEM),
        input_output_aliases={2: 0},
        scratch_shapes=[ROWS_X, pltpu.VMEM((3, FX * FY, PZ), jnp.bfloat16)]
        + LISTS
        + [pltpu.SemaphoreType.DMA],
        compiler_params=PARAMS,
        cost_estimate=cost(6 * 10**9),
    )(lists, cells, grid)


def call_finish(near, far, own, cells, charge, grid, found, potential):
    return pl.pallas_call(
        finish,
        out_shape=(
            jax.ShapeDtypeStruct((BX, BY, BZ), jnp.float32),
            jax.ShapeDtypeStruct((3, 1, A_DEV), jnp.float32),
        ),
        in_specs=[VMEM] * 7 + [HBM],
        out_specs=(HBM, VMEM),
        input_output_aliases={7: 0},
        scratch_shapes=[
            pltpu.VMEM((2, PX, 16, PZ), jnp.float32),
            pltpu.VMEM((2, BX, 8, BZ), jnp.float32),
            ROWS_X,
        ]
        + LISTS
        + [pltpu.SemaphoreType.DMA((2,))],
        compiler_params=PARAMS,
    )(near, far, own, cells, charge, grid, found, potential)


def local(charges, cells, counts):
    charge = charges.reshape(1, A_DEV)
    cells = cells.reshape(3, 1, A_DEV)
    counts = counts.reshape(1)
    first, second = call_compact(counts, charge, cells)
    own, to_first, to_second = call_arrange(counts, charge, cells)
    own = own[None]
    first, second = swaps(first[None], second[None], "gz")
    atoms, to_first, to_second = (
        jnp.concatenate([first, middle, second], axis=0)
        for middle in (own, to_first[None], to_second[None])
    )
    first, second = swaps(to_first, to_second, "gx")
    grid = call_inner(atoms)
    atoms = jnp.concatenate([first, atoms, second], axis=0)
    first, second = swaps(atoms, atoms, "gy")
    grid, potential, found = call_column(atoms, cells, grid)
    potential, forces = call_finish(first, second, own, cells, charge, grid, found, potential)
    return potential, forces.reshape(1, 1, 1, 3, A_DEV)


def solution(mesh):
    in_specs = (P("gx", "gy", "gz", None), P("gx", "gy", "gz", None, None), P("gx", "gy", "gz"))
    out_specs = (P("gx", "gy", "gz"), P("gx", "gy", "gz", None, None))
    return jax.shard_map(local, mesh=mesh, in_specs=in_specs, out_specs=out_specs, check_vma=False)
```

```python
import math

import jax
import jax.numpy as jnp
from jax import lax
from jax.experimental import pallas as pl
from jax.experimental.pallas import tpu as pltpu
from jax.sharding import PartitionSpec as P

BX = 32
BY = 32
BZ = 384
A_DEV = 1024
PAD = 4
REACH = 4
WIDTH = A_DEV + 128
BLOCK = 256
SMALL = 128
WIDE = 2 * BLOCK

X0 = 5
Y0 = 8
PX = 42
PY = 48
PZ = 512
CHUNK = 14
FX = 40
FY = 40
FCHUNK = 20

kernel_width = 2.0
EXPONENT = -math.log2(math.e) / (2.0 * kernel_width * kernel_width)
SCALE = 1.3903614627339054
UNIT = math.sqrt(-EXPONENT)
LOW_END = 2 * PAD + 5
HIGH_START = BZ + PAD - 9
HIGH_START_X = BX + PAD - 9
HIGH_START_Y = BY + PAD - 9
MIDDLE = BZ // 2
SPAN = A_DEV + 256 + WIDE
FRONT = 128
MERGED = 9 * A_DEV + SPAN + FRONT
ROWS = FCHUNK * FY


def weight(first, second, scale=1.0):
    away = first - second
    square = away * away
    value = jnp.exp2(math.log2(scale) - square)
    return jnp.where(square < (REACH + 0.5) ** 2 * UNIT * UNIT, value, 0.0)


def iota(shape, dim):
    return lax.broadcasted_iota(jnp.int32, shape, dim).astype(jnp.float32)


def toward(axis):
    return 2 * (lax.axis_index(axis) % 2) - 1


def live_atoms(numbers, charges, cells):
    live = lax.broadcasted_iota(jnp.int32, (1, A_DEV), 1) < numbers[0]
    charge = jnp.where(live, charges[...], 0.0).astype(jnp.bfloat16).astype(jnp.float32)
    places = [jnp.where(live, cells[i], 0) for i in range(3)]
    rows = [charge] + [place.astype(jnp.float32) for place in places[:2]]
    rows.append((places[2] - MIDDLE).astype(jnp.float32))
    rows.append(jnp.zeros((4, A_DEV), jnp.float32))
    return live, places, jnp.concatenate(rows, axis=0).astype(jnp.bfloat16)


def running_sums(masks):
    height = (len(masks) + 7) // 8 * 8
    rows = [jnp.where(mask, 1.0, 0.0) for mask in masks]
    if height > len(masks):
        rows.append(jnp.zeros((height - len(masks), A_DEV), jnp.float32))
    near = jnp.concatenate(rows, axis=0)
    parts = A_DEV // 128
    chunks = jnp.concatenate([near[:, 128 * c : 128 * c + 128] for c in range(parts)], axis=0)
    upto = jnp.where(iota((128, 128), 0) <= iota((128, 128), 1), 1.0, 0.0)
    ahead = jnp.where(iota((A_DEV, 128), 0) < iota((A_DEV, 128), 1) * 128.0, 1.0, 0.0)
    within = jnp.dot(
        chunks.astype(jnp.bfloat16),
        upto.astype(jnp.bfloat16),
        preferred_element_type=jnp.float32,
    )
    before = jnp.dot(
        near.astype(jnp.bfloat16),
        ahead.astype(jnp.bfloat16),
        preferred_element_type=jnp.float32,
    )
    sums = [
        within[height * c : height * (c + 1)] + before[:, c : c + 1] for c in range(parts)
    ]
    return jnp.concatenate(sums, axis=1)


def pick(rows, spot, start, size):
    want = iota((size, A_DEV), 0) + start.astype(jnp.float32)
    hot = jnp.where(want == spot, 1.0, 0.0).astype(jnp.bfloat16)
    return lax.dot_general(
        rows, hot, (((1,), (1,)), ((), ())), preferred_element_type=jnp.float32
    )


def compact(numbers, charges, cells, first, second, lists):
    live, places, rows = live_atoms(numbers, charges, cells)
    depth = places[2]
    masks = [live & (depth < LOW_END), live & (depth >= HIGH_START)]
    sums = running_sums(masks)
    totals = sums[:, A_DEV - 1 : A_DEV]
    spot = [jnp.where(masks[i], sums[i : i + 1] - 1.0, -1.0) for i in range(2)]
    steps = (jnp.max(totals).astype(jnp.int32) + SMALL - 1) // SMALL
    for side in range(2):
        lists[side, :, 0:A_DEV] = jnp.zeros((4, A_DEV), jnp.float32)
        lists[side, :, A_DEV:WIDTH] = jnp.broadcast_to(
            totals[side : side + 1], (4, WIDTH - A_DEV)
        )

    def window(k, _):
        cols = pl.ds(pl.multiple_of(k * SMALL, SMALL), SMALL)
        for side in range(2):
            moved = pick(rows, spot[side], k * SMALL, SMALL)
            lists[side, 0:3, cols] = moved[0:3]
            lists[side, 3:4, cols] = moved[3:4] + float(MIDDLE)
        return 0

    window(jnp.int32(0), 0)
    lax.fori_loop(1, steps, window, 0)
    odd = lax.axis_index("gz") % 2
    first[...] = lists[odd]
    second[...] = lists[1 - odd]


def arrange(numbers, charges, cells, own, first, second, lists):
    live, places, rows = live_atoms(numbers, charges, cells)
    high = live & (places[1] >= HIGH_START_Y)
    low = live & (places[1] < LOW_END)
    sides = [live, live & (places[0] < LOW_END), live & (places[0] >= HIGH_START_X)]
    sums = running_sums([mask for side in sides for mask in (high & side, low & side, side)])
    totals = sums[:, A_DEV - 1 : A_DEV]
    spots = []
    for i, side in enumerate(sides):
        highs, lows, alls = (sums[3 * i + j : 3 * i + j + 1] for j in range(3))
        ends = [totals[3 * i + j : 3 * i + j + 1] for j in range(3)]
        spot = jnp.where(low, ends[2] - ends[1] + lows, ends[0] + alls - highs - lows)
        spot = jnp.where(high, highs, spot) - 1.0
        spots.append(jnp.where(side, spot, -1.0))
        out = own if i == 0 else lists.at[i - 1]
        out[:, 0:A_DEV] = jnp.zeros((4, A_DEV), jnp.float32)
        for row, end in enumerate((2, 0, 1, 2)):
            out[row : row + 1, A_DEV:WIDTH] = jnp.broadcast_to(ends[end], (1, WIDTH - A_DEV))

    def fill(out, spot, k):
        cols = pl.ds(pl.multiple_of(k * BLOCK, BLOCK), BLOCK)
        moved = pick(rows, spot, k * BLOCK, BLOCK)
        out[0:3, cols] = moved[0:3]
        out[3:4, cols] = moved[3:4] + float(MIDDLE)

    def window(k, _):
        fill(own, spots[0], k)
        return 0

    def side_window(k, _):
        fill(lists.at[0], spots[1], k)
        fill(lists.at[1], spots[2], k)
        return 0

    widest = jnp.maximum(jnp.max(totals[5:6]), jnp.max(totals[8:9])).astype(jnp.int32)
    side_window(jnp.int32(0), 0)
    lax.fori_loop(0, (numbers[0] + BLOCK - 1) // BLOCK, window, 0)
    lax.fori_loop(1, (widest + BLOCK - 1) // BLOCK, side_window, 0)
    odd = lax.axis_index("gx") % 2
    first[...] = lists[odd]
    second[...] = lists[1 - odd]


def append(ref, brick, start, number, offset, dx, dy, dz, merged, padded):
    row = lax.broadcasted_iota(jnp.int32, (4, 128), 0)
    moved = jnp.where(row == 1, jnp.float32(X0 - PAD + BX * dx), 0.0)
    moved = jnp.where(row == 2, jnp.float32(Y0 - PAD + BY * dy), moved)
    moved = jnp.where(row == 3, jnp.float32(BZ * dz - PAD), moved)
    unit = jnp.where(row == 0, 1.0, UNIT)
    for c in range(0, A_DEV, 128):
        padded[0:4, c : c + 128] = (ref[brick, :, c : c + 128] + moved) * unit
    skip = start % 128
    atoms = padded[:, pl.ds(pl.multiple_of(start - skip, 128), SPAN)]
    lanes = lax.broadcasted_iota(jnp.int32, (8, SPAN), 1)
    atoms = jnp.where((lanes >= skip) & (lanes < skip + number), atoms, 0.0)
    room = offset % 128
    back = jnp.where(room >= skip, 0, 128)
    atoms = pltpu.roll(atoms, room - skip + back, 1)
    base = pl.multiple_of(FRONT + offset - room - back, 128)
    merged[:, pl.ds(base, 256)] += atoms[:, 0:256]
    merged[:, pl.ds(base + 256, SPAN - 256)] = atoms[:, 256:SPAN]
    return offset + number


def spread(merged, start, size, x0, nx, y0, ny, grid, rows_x, first, row0):
    cols = pl.ds(pl.multiple_of(start + FRONT, 128), size)
    charge = merged[0:1, cols]
    xa = merged[1:2, cols]
    ya = merged[2:3, cols]
    za = merged[3:4, cols]
    gy = weight((iota((ny, size), 0) + jnp.float32(y0)) * UNIT, ya) * (charge * (1.0 / SCALE))
    zi = iota((PZ, size), 0)
    zi = jnp.where(zi < 448.0, zi, zi - float(PZ)) * UNIT
    right = weight(zi, za, SCALE).astype(jnp.bfloat16)
    rows_x[:, 0:size] = weight(iota((48, size), 0) * UNIT, xa)
    chunk = min(nx, CHUNK * PY // ny)
    for c in range(0, nx, chunk):
        at = x0 + c
        left = jnp.stack(
            [rows_x[pl.ds(at + i, 1), 0:size] * gy for i in range(chunk)], axis=0
        )
        left = left.reshape(chunk * ny, size).astype(jnp.bfloat16)
        part = lax.dot_general(
            left, right, (((1,), (1,)), ((), ())), preferred_element_type=jnp.float32
        )
        part = part.reshape(chunk, ny, PZ)
        if first:
            grid[pl.ds(at, chunk), pl.ds(row0, ny), :] = part
        else:
            grid[pl.ds(at, chunk), pl.ds(row0, ny), :] += part


def spread_all(merged, total, x0, nx, y0, ny, grid, rows_x, clear, row0):
    rest = total % WIDE
    wide = total // WIDE + (rest > BLOCK).astype(jnp.int32)

    def put(start, size, first):
        spread(merged, start, size, x0, nx, y0, ny, grid, rows_x, first, row0)

    def block(k, _):
        put(k * WIDE, WIDE, False)
        return 0

    if clear:

        @pl.when(wide > 0)
        def _():
            put(0, WIDE, True)

        @pl.when(wide == 0)
        def _():
            put(0, BLOCK, True)

    lax.fori_loop(1 if clear else 0, wide, block, 0)

    @pl.when(total > (jnp.maximum(wide * WIDE, BLOCK) if clear else wide * WIDE))
    def _():
        put(wide * WIDE, BLOCK, False)


def number_of(ref, brick, row):
    return ref[brick, row : row + 1, A_DEV:WIDTH][0, 0].astype(jnp.int32)


def gather(ref, bricks, side, merged, padded):
    merged[:, 0 : FRONT + 256] = jnp.zeros((8, FRONT + 256), jnp.float32)
    offset = jnp.int32(0)
    for brick, (dx, dy, dz) in bricks:
        number = number_of(ref, brick, 0)
        start = jnp.int32(0)
        if side is not None and type(dz) is int:
            low = number_of(ref, brick, 2)
            start = jnp.where(side > 0, number - low, 0)
            number = jnp.where(side > 0, low, number_of(ref, brick, 1))
        offset = append(ref, brick, start, number, offset, dx, dy, dz, merged, padded)
    return offset


def slots_of(axis):
    step = toward(axis)
    return (step, 0, -step)


def inner(lists, grid, rows_x, merged, padded):
    padded[...] = jnp.zeros_like(padded)
    zs = slots_of("gz")
    total = gather(lists, [(j, (0, 0, zs[j])) for j in (1, 0, 2)], None, merged, padded)
    spread_all(merged, total, 0, PX, 0, PY, grid, rows_x, True, 0)


def column(
    lists, place, before, grid, potential, found, rows_x, fields, merged, padded, sem
):
    padded[...] = jnp.zeros_like(padded)
    xs, zs = slots_of("gx"), slots_of("gz")
    for i in (0, 2):
        total = gather(
            lists, [(3 * i + j, (xs[i], 0, zs[j])) for j in range(3)], None, merged, padded
        )
        x0 = jnp.where(xs[i] > 0, 28, 0)
        spread_all(merged, total, x0, 14, 0, PY, grid, rows_x, False, 0)
    copy = pltpu.make_async_copy(
        grid.at[X0 : X0 + BX, 16:32, 0:BZ], potential.at[:, 8:24, :], sem
    )
    copy.start()
    found[...] = jnp.zeros_like(found)
    count = number_of(lists, 4, 0)

    def build(c):
        gx, gy, gz = [], [], []
        for x in range(c * FCHUNK, (c + 1) * FCHUNK):
            gx.append(grid[x + 2, 4:44, :] - grid[x, 4:44, :])
            gy.append(grid[x + 1, 5:45, :] - grid[x + 1, 3:43, :])
            mid = grid[x + 1, 4:44, :]
            gz.append(pltpu.roll(mid, PZ - 2, 1) - mid)
        for d, parts in enumerate((gx, gy, gz)):
            both = jnp.stack(parts, axis=0).reshape(ROWS, PZ).astype(jnp.bfloat16)
            fields[d, c * ROWS : (c + 1) * ROWS, :] = both

    def sample(start, fresh):
        cols = pl.ds(pl.multiple_of(start, WIDE), WIDE)
        xa, ya, za = atom_cells(place, cols)
        zi = depths(WIDE)
        depth = jnp.where(zi == za, 1.0, 0.0).astype(jnp.bfloat16)
        below = jnp.where(zi == za - 1.0, 1.0, 0.0).astype(jnp.bfloat16)
        sums = [jnp.zeros((FY, WIDE), jnp.float32)] * 3
        for c in range(FX // FCHUNK):
            if fresh:
                build(c)
            for d in range(3):
                part = jnp.dot(
                    fields[d, c * ROWS : (c + 1) * ROWS, :],
                    below if d == 2 else depth,
                    preferred_element_type=jnp.float32,
                ).reshape(FCHUNK, FY, WIDE)
                for i in range(FCHUNK):
                    hot_x = xa == float(c * FCHUNK + i)
                    sums[d] = sums[d] + jnp.where(hot_x, part[i], 0.0)
        hot_y = iota((FY, WIDE), 0) == ya
        for d in range(3):
            value = jnp.sum(jnp.where(hot_y, sums[d], 0.0), axis=0, keepdims=True)
            found[d : d + 1, cols] = value

    sample(0, True)

    def more(k, _):
        sample(k * WIDE, False)
        return 0

    lax.fori_loop(1, (count + WIDE - 1) // WIDE, more, 0)
    copy.wait()


def atom_cells(place, cols):
    xa = place[0, :, cols].astype(jnp.float32)
    ya = place[1, :, cols].astype(jnp.float32)
    return xa, ya, (place[2, :, cols] - PAD).astype(jnp.float32)


def depths(size):
    zi = iota((PZ, size), 0)
    return jnp.where(zi < 448.0, zi, zi - float(PZ))


def slab(turn, lists, grid, potential, part, stage, rows_x, merged, padded, sem):
    xs, zs = slots_of("gx"), slots_of("gz")
    dy = toward("gy") * turn
    total = gather(
        lists,
        [(3 * m + j, (xs[m], dy, zs[j])) for m in range(3) for j in range(3)],
        dy,
        merged,
        padded,
    )
    y0 = pl.multiple_of(jnp.where(dy > 0, 32, 0), 8)
    spread_all(merged, total, 0, PX, y0, 16, part, rows_x, True, 0)
    at = pl.multiple_of(jnp.where(dy > 0, 0, 8), 8)
    stage[...] = (
        part[X0 : X0 + BX, pl.ds(at, 8), 0:BZ] + grid[X0 : X0 + BX, pl.ds(y0 + at, 8), 0:BZ]
    )
    row = pl.multiple_of(jnp.where(dy > 0, 24, 0), 8)
    copy = pltpu.make_async_copy(stage, potential.at[:, pl.ds(row, 8), :], sem)
    copy.start()
    return y0, copy


def finish(
    near, far, own, place, charge, grid, found, potential_in, potential, forces,
    parts, stages, rows_x, merged, padded, sems,
):
    padded[...] = jnp.zeros_like(padded)
    slabs = [
        slab(
            1 - 2 * i, lists, grid, potential, parts.at[i], stages.at[i],
            rows_x, merged, padded, sems.at[i],
        )
        for i, lists in enumerate((near, far))
    ]
    count = number_of(own, 0, 0)
    forces[...] = jnp.zeros_like(forces)

    def block(k, _):
        cols = pl.ds(pl.multiple_of(k * WIDE, WIDE), WIDE)
        xa, ya, za = atom_cells(place, cols)
        zi = depths(WIDE)
        here = jnp.where(zi == za, 1.0, 0.0).astype(jnp.bfloat16)
        slope = jnp.where(zi == za + 1.0, 1.0, 0.0) - jnp.where(zi == za - 1.0, 1.0, 0.0)
        slope = slope.astype(jnp.bfloat16)
        sums = [found[d : d + 1, cols] for d in range(3)]
        for i, (y0, _) in enumerate(slabs):
            rows = parts[i].reshape(PX * 16, PZ).astype(jnp.bfloat16)
            value = jnp.dot(rows, here, preferred_element_type=jnp.float32)
            value = value.reshape(PX, 16, WIDE)
            change = jnp.dot(rows, slope, preferred_element_type=jnp.float32)
            change = change.reshape(PX, 16, WIDE)
            level = jnp.zeros((16, WIDE), jnp.float32)
            along_x = level
            along_z = level
            for x in range(PX):
                at_x = xa == float(x - 1)
                level = level + jnp.where(at_x, value[x], 0.0)
                along_z = along_z + jnp.where(at_x, change[x], 0.0)
                side = jnp.where(xa == float(x - 2), 1.0, 0.0)
                side = side - jnp.where(xa == float(x), 1.0, 0.0)
                along_x = along_x + side * value[x]
            away = iota((16, WIDE), 0) + (y0.astype(jnp.float32) - float(Y0 - PAD)) - ya
            at_y = away == 0.0
            fx = jnp.where(at_y, along_x, 0.0)
            fy = jnp.where(away == 1.0, level, 0.0) - jnp.where(away == -1.0, level, 0.0)
            fz = jnp.where(at_y, along_z, 0.0)
            for d, one in enumerate((fx, fy, fz)):
                sums[d] = sums[d] + jnp.sum(one, axis=0, keepdims=True)
        slots = lax.broadcasted_iota(jnp.int32, (1, WIDE), 1) + k * WIDE
        factor = -0.5 * charge[:, cols]
        for d in range(3):
            forces[d, :, cols] = jnp.where(slots < count, sums[d] * factor, 0.0)
        return 0

    lax.fori_loop(0, (count + WIDE - 1) // WIDE, block, 0)
    for _, copy in slabs:
        copy.wait()


def swaps(block, other, axis):
    size = lax.axis_size(axis)
    first = [(i, (i + 1 if i % 2 else i - 1) % size) for i in range(size)]
    second = [(i, i ^ 1) for i in range(size)]
    return lax.ppermute(block, axis, first), lax.ppermute(other, axis, second)


VMEM = pl.BlockSpec(memory_space=pltpu.VMEM)
HBM = pl.BlockSpec(memory_space=pl.ANY)
LIMIT = 40 * 1024 * 1024


def call_compact(counts, charge, cells):
    shape = pltpu.VMEM((4, WIDTH), jnp.float32)
    return pl.pallas_call(
        compact,
        out_shape=(shape, shape),
        in_specs=[pl.BlockSpec(memory_space=pltpu.SMEM), VMEM, VMEM],
        out_specs=(VMEM,) * 2,
        scratch_shapes=[pltpu.VMEM((2, 4, WIDTH), jnp.float32)],
    )(counts, charge, cells)


def call_arrange(counts, charge, cells):
    shape = pltpu.VMEM((4, WIDTH), jnp.float32)
    return pl.pallas_call(
        arrange,
        out_shape=(shape, shape, shape),
        in_specs=[pl.BlockSpec(memory_space=pltpu.SMEM), VMEM, VMEM],
        out_specs=(VMEM,) * 3,
        scratch_shapes=[pltpu.VMEM((2, 4, WIDTH), jnp.float32)],
        cost_estimate=pl.CostEstimate(flops=2 * 10**9, bytes_accessed=10**5, transcendentals=0),
    )(counts, charge, cells)


GRID = pltpu.VMEM((PX, PY, PZ), jnp.float32)
FOUND = pltpu.VMEM((8, A_DEV), jnp.float32)
ROWS_X = pltpu.VMEM((48, WIDE), jnp.float32)
LISTS = [
    pltpu.VMEM((8, MERGED), jnp.float32),
    pltpu.VMEM((8, A_DEV + SPAN), jnp.float32),
]
PARAMS = pltpu.CompilerParams(vmem_limit_bytes=LIMIT)


def cost(flops):
    return pl.CostEstimate(flops=flops, bytes_accessed=10**6, transcendentals=0)


def call_inner(lists):
    return pl.pallas_call(
        inner,
        out_shape=GRID,
        in_specs=[VMEM],
        out_specs=VMEM,
        scratch_shapes=[ROWS_X] + LISTS,
        compiler_params=PARAMS,
        cost_estimate=cost(2 * 10**9),
    )(lists)


def call_column(lists, cells, grid):
    return pl.pallas_call(
        column,
        out_shape=(GRID, jax.ShapeDtypeStruct((BX, BY, BZ), jnp.float32), FOUND),
        in_specs=[VMEM, VMEM, VMEM],
        out_specs=(VMEM, HBM, VMEM),
        input_output_aliases={2: 0},
        scratch_shapes=[ROWS_X, pltpu.VMEM((3, FX * FY, PZ), jnp.bfloat16)]
        + LISTS
        + [pltpu.SemaphoreType.DMA],
        compiler_params=PARAMS,
        cost_estimate=cost(6 * 10**9),
    )(lists, cells, grid)


def call_finish(near, far, own, cells, charge, grid, found, potential):
    return pl.pallas_call(
        finish,
        out_shape=(
            jax.ShapeDtypeStruct((BX, BY, BZ), jnp.float32),
            jax.ShapeDtypeStruct((3, 1, A_DEV), jnp.float32),
        ),
        in_specs=[VMEM] * 7 + [HBM],
        out_specs=(HBM, VMEM),
        input_output_aliases={7: 0},
        scratch_shapes=[
            pltpu.VMEM((2, PX, 16, PZ), jnp.float32),
            pltpu.VMEM((2, BX, 8, BZ), jnp.float32),
            ROWS_X,
        ]
        + LISTS
        + [pltpu.SemaphoreType.DMA((2,))],
        compiler_params=PARAMS,
    )(near, far, own, cells, charge, grid, found, potential)


def local(charges, cells, counts):
    charge = charges.reshape(1, A_DEV)
    cells = cells.reshape(3, 1, A_DEV)
    counts = counts.reshape(1)
    first, second = call_compact(counts, charge, cells)
    own, to_first, to_second = call_arrange(counts, charge, cells)
    own = own[None]
    first, second = swaps(first[None], second[None], "gz")
    atoms, to_first, to_second = (
        jnp.concatenate([first, middle, second], axis=0)
        for middle in (own, to_first[None], to_second[None])
    )
    first, second = swaps(to_first, to_second, "gx")
    grid = call_inner(atoms)
    atoms = jnp.concatenate([first, atoms, second], axis=0)
    first, second = swaps(atoms, atoms, "gy")
    grid, potential, found = call_column(atoms, cells, grid)
    potential, forces = call_finish(first, second, own, cells, charge, grid, found, potential)
    return potential, forces.reshape(1, 1, 1, 3, A_DEV)


def solution(mesh):
    in_specs = (P("gx", "gy", "gz", None), P("gx", "gy", "gz", None, None), P("gx", "gy", "gz"))
    out_specs = (P("gx", "gy", "gz"), P("gx", "gy", "gz", None, None))
    return jax.shard_map(local, mesh=mesh, in_specs=in_specs, out_specs=out_specs, check_vma=False)
```

```python
import math

import jax
import jax.numpy as jnp
from jax import lax
from jax.experimental import pallas as pl
from jax.experimental.pallas import tpu as pltpu
from jax.sharding import PartitionSpec as P

BX = 32
BY = 32
BZ = 384
A_DEV = 1024
PAD = 4
REACH = 4
WIDTH = A_DEV + 128
BLOCK = 256
SMALL = 128
WIDE = 2 * BLOCK

X0 = 5
Y0 = 8
PX = 42
PY = 48
PZ = 512
CHUNK = 42
FX = 40
FY = 40
FCHUNK = 10

kernel_width = 2.0
EXPONENT = -math.log2(math.e) / (2.0 * kernel_width * kernel_width)
SCALE = 1.3903614627339054
UNIT = math.sqrt(-EXPONENT)
LOW_END = 2 * PAD + 5
HIGH_START = BZ + PAD - 9
HIGH_START_X = BX + PAD - 9
HIGH_START_Y = BY + PAD - 9
MIDDLE = BZ // 2
SPAN = A_DEV + 256 + WIDE
FRONT = 128
MERGED = 9 * A_DEV + SPAN + FRONT
ROWS = FCHUNK * FY


def weight(first, second, scale=1.0):
    away = first - second
    square = away * away
    value = jnp.exp2(math.log2(scale) - square)
    return jnp.where(square < (REACH + 0.5) ** 2 * UNIT * UNIT, value, 0.0)


def iota(shape, dim):
    return lax.broadcasted_iota(jnp.int32, shape, dim).astype(jnp.float32)


def toward(axis):
    return 2 * (lax.axis_index(axis) % 2) - 1


def live_atoms(numbers, charges, cells):
    live = lax.broadcasted_iota(jnp.int32, (1, A_DEV), 1) < numbers[0]
    charge = jnp.where(live, charges[...], 0.0).astype(jnp.bfloat16).astype(jnp.float32)
    places = [jnp.where(live, cells[i], 0) for i in range(3)]
    rows = [charge] + [place.astype(jnp.float32) for place in places[:2]]
    rows.append((places[2] - MIDDLE).astype(jnp.float32))
    rows.append(jnp.zeros((4, A_DEV), jnp.float32))
    return live, places, jnp.concatenate(rows, axis=0).astype(jnp.bfloat16)


def running_sums(masks):
    height = (len(masks) + 7) // 8 * 8
    rows = [jnp.where(mask, 1.0, 0.0) for mask in masks]
    if height > len(masks):
        rows.append(jnp.zeros((height - len(masks), A_DEV), jnp.float32))
    near = jnp.concatenate(rows, axis=0)
    parts = A_DEV // 128
    chunks = jnp.concatenate([near[:, 128 * c : 128 * c + 128] for c in range(parts)], axis=0)
    upto = jnp.where(iota((128, 128), 0) <= iota((128, 128), 1), 1.0, 0.0)
    ahead = jnp.where(iota((A_DEV, 128), 0) < iota((A_DEV, 128), 1) * 128.0, 1.0, 0.0)
    within = jnp.dot(
        chunks.astype(jnp.bfloat16),
        upto.astype(jnp.bfloat16),
        preferred_element_type=jnp.float32,
    )
    before = jnp.dot(
        near.astype(jnp.bfloat16),
        ahead.astype(jnp.bfloat16),
        preferred_element_type=jnp.float32,
    )
    sums = [
        within[height * c : height * (c + 1)] + before[:, c : c + 1] for c in range(parts)
    ]
    return jnp.concatenate(sums, axis=1)


def pick(rows, spot, start, size):
    want = iota((size, A_DEV), 0) + start.astype(jnp.float32)
    hot = jnp.where(want == spot, 1.0, 0.0).astype(jnp.bfloat16)
    return lax.dot_general(
        rows, hot, (((1,), (1,)), ((), ())), preferred_element_type=jnp.float32
    )


def compact(numbers, charges, cells, first, second, lists):
    live, places, rows = live_atoms(numbers, charges, cells)
    depth = places[2]
    masks = [live & (depth < LOW_END), live & (depth >= HIGH_START)]
    sums = running_sums(masks)
    totals = sums[:, A_DEV - 1 : A_DEV]
    spot = [jnp.where(masks[i], sums[i : i + 1] - 1.0, -1.0) for i in range(2)]
    steps = (jnp.max(totals).astype(jnp.int32) + SMALL - 1) // SMALL
    for side in range(2):
        lists[side, :, 0:A_DEV] = jnp.zeros((4, A_DEV), jnp.float32)
        lists[side, :, A_DEV:WIDTH] = jnp.broadcast_to(
            totals[side : side + 1], (4, WIDTH - A_DEV)
        )

    def window(k, _):
        cols = pl.ds(pl.multiple_of(k * SMALL, SMALL), SMALL)
        for side in range(2):
            moved = pick(rows, spot[side], k * SMALL, SMALL)
            lists[side, 0:3, cols] = moved[0:3]
            lists[side, 3:4, cols] = moved[3:4] + float(MIDDLE)
        return 0

    window(jnp.int32(0), 0)
    lax.fori_loop(1, steps, window, 0)
    odd = lax.axis_index("gz") % 2
    first[...] = lists[odd]
    second[...] = lists[1 - odd]


def arrange(numbers, charges, cells, own, first, second, lists):
    live, places, rows = live_atoms(numbers, charges, cells)
    high = live & (places[1] >= HIGH_START_Y)
    low = live & (places[1] < LOW_END)
    sides = [live, live & (places[0] < LOW_END), live & (places[0] >= HIGH_START_X)]
    sums = running_sums([mask for side in sides for mask in (high & side, low & side, side)])
    totals = sums[:, A_DEV - 1 : A_DEV]
    spots = []
    for i, side in enumerate(sides):
        highs, lows, alls = (sums[3 * i + j : 3 * i + j + 1] for j in range(3))
        ends = [totals[3 * i + j : 3 * i + j + 1] for j in range(3)]
        spot = jnp.where(low, ends[2] - ends[1] + lows, ends[0] + alls - highs - lows)
        spot = jnp.where(high, highs, spot) - 1.0
        spots.append(jnp.where(side, spot, -1.0))
        out = own if i == 0 else lists.at[i - 1]
        out[:, 0:A_DEV] = jnp.zeros((4, A_DEV), jnp.float32)
        for row, end in enumerate((2, 0, 1, 2)):
            out[row : row + 1, A_DEV:WIDTH] = jnp.broadcast_to(ends[end], (1, WIDTH - A_DEV))

    def fill(out, spot, k):
        cols = pl.ds(pl.multiple_of(k * BLOCK, BLOCK), BLOCK)
        moved = pick(rows, spot, k * BLOCK, BLOCK)
        out[0:3, cols] = moved[0:3]
        out[3:4, cols] = moved[3:4] + float(MIDDLE)

    def window(k, _):
        fill(own, spots[0], k)
        return 0

    def side_window(k, _):
        fill(lists.at[0], spots[1], k)
        fill(lists.at[1], spots[2], k)
        return 0

    widest = jnp.maximum(jnp.max(totals[5:6]), jnp.max(totals[8:9])).astype(jnp.int32)
    side_window(jnp.int32(0), 0)
    lax.fori_loop(0, (numbers[0] + BLOCK - 1) // BLOCK, window, 0)
    lax.fori_loop(1, (widest + BLOCK - 1) // BLOCK, side_window, 0)
    odd = lax.axis_index("gx") % 2
    first[...] = lists[odd]
    second[...] = lists[1 - odd]


def append(ref, brick, start, number, offset, dx, dy, dz, merged, padded):
    row = lax.broadcasted_iota(jnp.int32, (4, 128), 0)
    moved = jnp.where(row == 1, jnp.float32(X0 - PAD + BX * dx), 0.0)
    moved = jnp.where(row == 2, jnp.float32(Y0 - PAD + BY * dy), moved)
    moved = jnp.where(row == 3, jnp.float32(BZ * dz - PAD), moved)
    unit = jnp.where(row == 0, 1.0, UNIT)
    for c in range(0, A_DEV, 128):
        padded[0:4, c : c + 128] = (ref[brick, :, c : c + 128] + moved) * unit
    skip = start % 128
    atoms = padded[:, pl.ds(pl.multiple_of(start - skip, 128), SPAN)]
    lanes = lax.broadcasted_iota(jnp.int32, (8, SPAN), 1)
    atoms = jnp.where((lanes >= skip) & (lanes < skip + number), atoms, 0.0)
    room = offset % 128
    back = jnp.where(room >= skip, 0, 128)
    atoms = pltpu.roll(atoms, room - skip + back, 1)
    base = pl.multiple_of(FRONT + offset - room - back, 128)
    merged[:, pl.ds(base, 256)] += atoms[:, 0:256]
    merged[:, pl.ds(base + 256, SPAN - 256)] = atoms[:, 256:SPAN]
    return offset + number


def spread(merged, start, size, x0, nx, y0, ny, grid, rows_x, first, row0):
    cols = pl.ds(pl.multiple_of(start + FRONT, 128), size)
    charge = merged[0:1, cols]
    xa = merged[1:2, cols]
    ya = merged[2:3, cols]
    za = merged[3:4, cols]
    gy = weight((iota((ny, size), 0) + jnp.float32(y0)) * UNIT, ya) * (charge * (1.0 / SCALE))
    zi = iota((PZ, size), 0)
    zi = jnp.where(zi < 448.0, zi, zi - float(PZ)) * UNIT
    right = weight(zi, za, SCALE).astype(jnp.bfloat16)
    rows_x[:, 0:size] = weight(iota((48, size), 0) * UNIT, xa)
    chunk = min(nx, CHUNK * PY // ny)
    for c in range(0, nx, chunk):
        at = x0 + c
        left = jnp.stack(
            [rows_x[pl.ds(at + i, 1), 0:size] * gy for i in range(chunk)], axis=0
        )
        left = left.reshape(chunk * ny, size).astype(jnp.bfloat16)
        part = lax.dot_general(
            left, right, (((1,), (1,)), ((), ())), preferred_element_type=jnp.float32
        )
        part = part.reshape(chunk, ny, PZ)
        if first:
            grid[pl.ds(at, chunk), pl.ds(row0, ny), :] = part
        else:
            grid[pl.ds(at, chunk), pl.ds(row0, ny), :] += part


def spread_all(merged, total, x0, nx, y0, ny, grid, rows_x, clear, row0):
    rest = total % WIDE
    wide = total // WIDE + (rest > BLOCK).astype(jnp.int32)

    def put(start, size, first):
        spread(merged, start, size, x0, nx, y0, ny, grid, rows_x, first, row0)

    def block(k, _):
        put(k * WIDE, WIDE, False)
        return 0

    if clear:

        @pl.when(wide > 0)
        def _():
            put(0, WIDE, True)

        @pl.when(wide == 0)
        def _():
            put(0, BLOCK, True)

    lax.fori_loop(1 if clear else 0, wide, block, 0)

    @pl.when(total > (jnp.maximum(wide * WIDE, BLOCK) if clear else wide * WIDE))
    def _():
        put(wide * WIDE, BLOCK, False)


def number_of(ref, brick, row):
    return ref[brick, row : row + 1, A_DEV:WIDTH][0, 0].astype(jnp.int32)


def gather(ref, bricks, side, merged, padded):
    merged[:, 0 : FRONT + 256] = jnp.zeros((8, FRONT + 256), jnp.float32)
    offset = jnp.int32(0)
    for brick, (dx, dy, dz) in bricks:
        number = number_of(ref, brick, 0)
        start = jnp.int32(0)
        if side is not None and type(dz) is int:
            low = number_of(ref, brick, 2)
            start = jnp.where(side > 0, number - low, 0)
            number = jnp.where(side > 0, low, number_of(ref, brick, 1))
        offset = append(ref, brick, start, number, offset, dx, dy, dz, merged, padded)
    return offset


def slots_of(axis):
    step = toward(axis)
    return (step, 0, -step)


def inner(lists, grid, rows_x, merged, padded):
    padded[...] = jnp.zeros_like(padded)
    zs = slots_of("gz")
    total = gather(lists, [(j, (0, 0, zs[j])) for j in (1, 0, 2)], None, merged, padded)
    spread_all(merged, total, 0, PX, 0, PY, grid, rows_x, True, 0)


def column(
    lists, place, before, grid, potential, found, rows_x, fields, merged, padded, sem
):
    padded[...] = jnp.zeros_like(padded)
    xs, zs = slots_of("gx"), slots_of("gz")
    for i in (0, 2):
        total = gather(
            lists, [(3 * i + j, (xs[i], 0, zs[j])) for j in range(3)], None, merged, padded
        )
        x0 = jnp.where(xs[i] > 0, 28, 0)
        spread_all(merged, total, x0, 14, 0, PY, grid, rows_x, False, 0)
    copy = pltpu.make_async_copy(
        grid.at[X0 : X0 + BX, 16:32, 0:BZ], potential.at[:, 8:24, :], sem
    )
    copy.start()
    found[...] = jnp.zeros_like(found)
    count = number_of(lists, 4, 0)

    def build(c):
        gx, gy, gz = [], [], []
        for x in range(c * FCHUNK, (c + 1) * FCHUNK):
            gx.append(grid[x + 2, 4:44, :] - grid[x, 4:44, :])
            gy.append(grid[x + 1, 5:45, :] - grid[x + 1, 3:43, :])
            mid = grid[x + 1, 4:44, :]
            gz.append(pltpu.roll(mid, PZ - 2, 1) - mid)
        for d, parts in enumerate((gx, gy, gz)):
            both = jnp.stack(parts, axis=0).reshape(ROWS, PZ).astype(jnp.bfloat16)
            fields[d, c * ROWS : (c + 1) * ROWS, :] = both

    def sample(start, fresh):
        cols = pl.ds(pl.multiple_of(start, WIDE), WIDE)
        xa, ya, za = atom_cells(place, cols)
        zi = depths(WIDE)
        depth = jnp.where(zi == za, 1.0, 0.0).astype(jnp.bfloat16)
        below = jnp.where(zi == za - 1.0, 1.0, 0.0).astype(jnp.bfloat16)
        sums = [jnp.zeros((FY, WIDE), jnp.float32)] * 3
        for c in range(FX // FCHUNK):
            if fresh:
                build(c)
            for d in range(3):
                part = jnp.dot(
                    fields[d, c * ROWS : (c + 1) * ROWS, :],
                    below if d == 2 else depth,
                    preferred_element_type=jnp.float32,
                ).reshape(FCHUNK, FY, WIDE)
                for i in range(FCHUNK):
                    hot_x = xa == float(c * FCHUNK + i)
                    sums[d] = sums[d] + jnp.where(hot_x, part[i], 0.0)
        hot_y = iota((FY, WIDE), 0) == ya
        for d in range(3):
            value = jnp.sum(jnp.where(hot_y, sums[d], 0.0), axis=0, keepdims=True)
            found[d : d + 1, cols] = value

    sample(0, True)

    def more(k, _):
        sample(k * WIDE, False)
        return 0

    lax.fori_loop(1, (count + WIDE - 1) // WIDE, more, 0)
    copy.wait()


def atom_cells(place, cols):
    xa = place[0, :, cols].astype(jnp.float32)
    ya = place[1, :, cols].astype(jnp.float32)
    return xa, ya, (place[2, :, cols] - PAD).astype(jnp.float32)


def depths(size):
    zi = iota((PZ, size), 0)
    return jnp.where(zi < 448.0, zi, zi - float(PZ))


def slab(turn, lists, grid, potential, part, stage, rows_x, merged, padded, sem):
    xs, zs = slots_of("gx"), slots_of("gz")
    dy = toward("gy") * turn
    total = gather(
        lists,
        [(3 * m + j, (xs[m], dy, zs[j])) for m in range(3) for j in range(3)],
        dy,
        merged,
        padded,
    )
    y0 = pl.multiple_of(jnp.where(dy > 0, 32, 0), 8)
    spread_all(merged, total, 0, PX, y0, 16, part, rows_x, True, 0)
    at = pl.multiple_of(jnp.where(dy > 0, 0, 8), 8)
    stage[...] = (
        part[X0 : X0 + BX, pl.ds(at, 8), 0:BZ] + grid[X0 : X0 + BX, pl.ds(y0 + at, 8), 0:BZ]
    )
    row = pl.multiple_of(jnp.where(dy > 0, 24, 0), 8)
    copy = pltpu.make_async_copy(stage, potential.at[:, pl.ds(row, 8), :], sem)
    copy.start()
    return y0, copy


def finish(
    near, far, own, place, charge, grid, found, potential_in, potential, forces,
    parts, stages, rows_x, merged, padded, sems,
):
    padded[...] = jnp.zeros_like(padded)
    slabs = [
        slab(
            1 - 2 * i, lists, grid, potential, parts.at[i], stages.at[i],
            rows_x, merged, padded, sems.at[i],
        )
        for i, lists in enumerate((near, far))
    ]
    count = number_of(own, 0, 0)
    forces[...] = jnp.zeros_like(forces)

    def block(k, _):
        cols = pl.ds(pl.multiple_of(k * WIDE, WIDE), WIDE)
        xa, ya, za = atom_cells(place, cols)
        zi = depths(WIDE)
        here = jnp.where(zi == za, 1.0, 0.0).astype(jnp.bfloat16)
        slope = jnp.where(zi == za + 1.0, 1.0, 0.0) - jnp.where(zi == za - 1.0, 1.0, 0.0)
        slope = slope.astype(jnp.bfloat16)
        sums = [found[d : d + 1, cols] for d in range(3)]
        for i, (y0, _) in enumerate(slabs):
            rows = parts[i].reshape(PX * 16, PZ).astype(jnp.bfloat16)
            value = jnp.dot(rows, here, preferred_element_type=jnp.float32)
            value = value.reshape(PX, 16, WIDE)
            change = jnp.dot(rows, slope, preferred_element_type=jnp.float32)
            change = change.reshape(PX, 16, WIDE)
            level = jnp.zeros((16, WIDE), jnp.float32)
            along_x = level
            along_z = level
            for x in range(PX):
                at_x = xa == float(x - 1)
                level = level + jnp.where(at_x, value[x], 0.0)
                along_z = along_z + jnp.where(at_x, change[x], 0.0)
                side = jnp.where(xa == float(x - 2), 1.0, 0.0)
                side = side - jnp.where(xa == float(x), 1.0, 0.0)
                along_x = along_x + side * value[x]
            away = iota((16, WIDE), 0) + (y0.astype(jnp.float32) - float(Y0 - PAD)) - ya
            at_y = away == 0.0
            fx = jnp.where(at_y, along_x, 0.0)
            fy = jnp.where(away == 1.0, level, 0.0) - jnp.where(away == -1.0, level, 0.0)
            fz = jnp.where(at_y, along_z, 0.0)
            for d, one in enumerate((fx, fy, fz)):
                sums[d] = sums[d] + jnp.sum(one, axis=0, keepdims=True)
        slots = lax.broadcasted_iota(jnp.int32, (1, WIDE), 1) + k * WIDE
        factor = -0.5 * charge[:, cols]
        for d in range(3):
            forces[d, :, cols] = jnp.where(slots < count, sums[d] * factor, 0.0)
        return 0

    lax.fori_loop(0, (count + WIDE - 1) // WIDE, block, 0)
    for _, copy in slabs:
        copy.wait()


def swaps(block, other, axis):
    size = lax.axis_size(axis)
    first = [(i, (i + 1 if i % 2 else i - 1) % size) for i in range(size)]
    second = [(i, i ^ 1) for i in range(size)]
    return lax.ppermute(block, axis, first), lax.ppermute(other, axis, second)


VMEM = pl.BlockSpec(memory_space=pltpu.VMEM)
HBM = pl.BlockSpec(memory_space=pl.ANY)
LIMIT = 40 * 1024 * 1024


def call_compact(counts, charge, cells):
    shape = pltpu.VMEM((4, WIDTH), jnp.float32)
    return pl.pallas_call(
        compact,
        out_shape=(shape, shape),
        in_specs=[pl.BlockSpec(memory_space=pltpu.SMEM), VMEM, VMEM],
        out_specs=(VMEM,) * 2,
        scratch_shapes=[pltpu.VMEM((2, 4, WIDTH), jnp.float32)],
    )(counts, charge, cells)


def call_arrange(counts, charge, cells):
    shape = pltpu.VMEM((4, WIDTH), jnp.float32)
    return pl.pallas_call(
        arrange,
        out_shape=(shape, shape, shape),
        in_specs=[pl.BlockSpec(memory_space=pltpu.SMEM), VMEM, VMEM],
        out_specs=(VMEM,) * 3,
        scratch_shapes=[pltpu.VMEM((2, 4, WIDTH), jnp.float32)],
        cost_estimate=pl.CostEstimate(flops=2 * 10**9, bytes_accessed=10**5, transcendentals=0),
    )(counts, charge, cells)


GRID = pltpu.VMEM((PX, PY, PZ), jnp.float32)
FOUND = pltpu.VMEM((8, A_DEV), jnp.float32)
ROWS_X = pltpu.VMEM((48, WIDE), jnp.float32)
LISTS = [
    pltpu.VMEM((8, MERGED), jnp.float32),
    pltpu.VMEM((8, A_DEV + SPAN), jnp.float32),
]
PARAMS = pltpu.CompilerParams(vmem_limit_bytes=LIMIT)


def cost(flops):
    return pl.CostEstimate(flops=flops, bytes_accessed=10**6, transcendentals=0)


def call_inner(lists):
    return pl.pallas_call(
        inner,
        out_shape=GRID,
        in_specs=[VMEM],
        out_specs=VMEM,
        scratch_shapes=[ROWS_X] + LISTS,
        compiler_params=PARAMS,
        cost_estimate=cost(2 * 10**9),
    )(lists)


def call_column(lists, cells, grid):
    return pl.pallas_call(
        column,
        out_shape=(GRID, jax.ShapeDtypeStruct((BX, BY, BZ), jnp.float32), FOUND),
        in_specs=[VMEM, VMEM, VMEM],
        out_specs=(VMEM, HBM, VMEM),
        input_output_aliases={2: 0},
        scratch_shapes=[ROWS_X, pltpu.VMEM((3, FX * FY, PZ), jnp.bfloat16)]
        + LISTS
        + [pltpu.SemaphoreType.DMA],
        compiler_params=PARAMS,
        cost_estimate=cost(6 * 10**9),
    )(lists, cells, grid)


def call_finish(near, far, own, cells, charge, grid, found, potential):
    return pl.pallas_call(
        finish,
        out_shape=(
            jax.ShapeDtypeStruct((BX, BY, BZ), jnp.float32),
            jax.ShapeDtypeStruct((3, 1, A_DEV), jnp.float32),
        ),
        in_specs=[VMEM] * 7 + [HBM],
        out_specs=(HBM, VMEM),
        input_output_aliases={7: 0},
        scratch_shapes=[
            pltpu.VMEM((2, PX, 16, PZ), jnp.float32),
            pltpu.VMEM((2, BX, 8, BZ), jnp.float32),
            ROWS_X,
        ]
        + LISTS
        + [pltpu.SemaphoreType.DMA((2,))],
        compiler_params=PARAMS,
    )(near, far, own, cells, charge, grid, found, potential)


def local(charges, cells, counts):
    charge = charges.reshape(1, A_DEV)
    cells = cells.reshape(3, 1, A_DEV)
    counts = counts.reshape(1)
    first, second = call_compact(counts, charge, cells)
    own, to_first, to_second = call_arrange(counts, charge, cells)
    own = own[None]
    first, second = swaps(first[None], second[None], "gz")
    atoms, to_first, to_second = (
        jnp.concatenate([first, middle, second], axis=0)
        for middle in (own, to_first[None], to_second[None])
    )
    first, second = swaps(to_first, to_second, "gx")
    grid = call_inner(atoms)
    atoms = jnp.concatenate([first, atoms, second], axis=0)
    first, second = swaps(atoms, atoms, "gy")
    grid, potential, found = call_column(atoms, cells, grid)
    potential, forces = call_finish(first, second, own, cells, charge, grid, found, potential)
    return potential, forces.reshape(1, 1, 1, 3, A_DEV)


def solution(mesh):
    in_specs = (P("gx", "gy", "gz", None), P("gx", "gy", "gz", None, None), P("gx", "gy", "gz"))
    out_specs = (P("gx", "gy", "gz"), P("gx", "gy", "gz", None, None))
    return jax.shard_map(local, mesh=mesh, in_specs=in_specs, out_specs=out_specs, check_vma=False)
```
